256 devices in a mesh: gx: 4 (over y), gy: 8 (over z), gz: 8 (over x, core).
Axes of the slice: x: 4, y: 4, z: 8, core: 2. Of those that a mesh axis runs over, the one named last changes fastest.
Arguments:
- right_side: float32 [16, 32, 64, 1024], P(None, 'gx', 'gy', 'gz'), may hold values from -21 to 21, as said below
- absorption: float32 [32, 64, 1024], P('gx', 'gy', 'gz'), may hold values from 0.25 to 4
- velocity: float32 [3, 32, 64, 1024], P(None, 'gx', 'gy', 'gz'), may hold values from -1 to 1
Outputs:
- solution_field: float32 [16, 32, 64, 1024], P(None, 'gx', 'gy', 'gz')
- residual: float32 [16, 32, 64, 1024], P(None, 'gx', 'gy', 'gz')
The draws below stay inside these ranges and needn't reach their ends.
Inputs may be any that keep to these rules, and one draw needn't show every extreme that they name: `right_side`: Right-hand sides of order one, scaled from cell to cell.
All inputs are finite; a program needn't handle non-finite values.
Results may differ from the reference program's by a relative error of at most 0.0003.
Values sent between devices are 32-bit elements; how exact they have to be, the bound alone decides.
No kernel may reach another device: no remote copies, remote signals or barrier semaphores. Data moves between devices by JAX's collectives and lax.ppermute only.
A program may use at most 128 MiB of HBM per device.

```python
import math
import jax
import jax.numpy as jnp
from jax import lax

RHS = 16
STEPS = 4
NX = 32
NY = 64
NZ = 1024


def draw_right_side(key, part):
    key = jax.random.fold_in(key, 5)
    first, second = jax.random.split(key)
    fx = jnp.arange(NX, dtype=jnp.float32).reshape(1, NX, 1, 1) / max(NX - 1, 1)
    fy = jnp.arange(NY, dtype=jnp.float32).reshape(1, 1, NY, 1) / max(NY - 1, 1)
    fz = jnp.arange(NZ, dtype=jnp.float32).reshape(1, 1, 1, NZ) / max(NZ - 1, 1)
    rising = jnp.exp(math.log(3.0) * (fx + fy + fz) / 3.0) / math.sqrt(3.0)
    rough = jnp.exp(jax.random.uniform(second, (1, NX, NY, NZ), jnp.float32, math.log(0.3), math.log(3.0)))
    base = jnp.clip(jax.random.normal(first, (RHS, NX, NY, NZ), jnp.float32), -4.0, 4.0)
    return (base * rough * rising).astype(jnp.float32)


def shard_levels(rng, shape, pieces, smallest, largest):
    loudness, own = 1.0, jax.random.fold_in(rng, 6)
    for axis_at, blocks in pieces:
        draws = jnp.exp(jax.random.uniform(jax.random.fold_in(own, axis_at), (blocks,), jnp.float32, smallest / len(pieces), largest / len(pieces)))
        loudness = loudness * jnp.repeat(draws, shape[axis_at] // blocks).reshape([-1 if axis == axis_at else 1 for axis in range(len(shape))])
    return loudness


def setup_inputs(seed: int = 0) -> dict:
    seeds = jax.random.split(jax.random.key(seed), 4)
    right_side = draw_right_side(jax.random.fold_in(seeds[3], 71), 0)
    absorption = jnp.clip(jnp.exp(math.log(4.0) - 2.7725887 * jax.random.uniform(seeds[1], (NX, NY, NZ), jnp.float32) ** shard_levels(seeds[1], (NX, NY, NZ), ((0, 4), (1, 8), (2, 8)), -0.2, 0.2)), 0.25, 4.0)
    velocity = jnp.clip(jax.random.uniform(seeds[2], (3, NX, NY, NZ), jnp.float32, -1.0, 1.0) * shard_levels(seeds[2], (3, NX, NY, NZ), ((1, 4), (2, 8), (3, 8)), -0.4, 0.0), -1.0, 1.0)
    return {"right_side": right_side, "absorption": absorption, "velocity": velocity}


def apply_shifted(field, coeff):
    padded = jnp.pad(field, ((0, 0), (1, 1), (1, 1), (1, 1)))
    center = padded[:, 1:-1, 1:-1, 1:-1]
    xplus = padded[:, 2:, 1:-1, 1:-1]
    xminus = padded[:, :-2, 1:-1, 1:-1]
    yplus = padded[:, 1:-1, 2:, 1:-1]
    yminus = padded[:, 1:-1, :-2, 1:-1]
    zplus = padded[:, 1:-1, 1:-1, 2:]
    zminus = padded[:, 1:-1, 1:-1, :-2]
    result = (6.0 + coeff[0]) * center - (xplus + xminus + yplus + yminus + zplus + zminus)
    result = result + 0.5 * (coeff[1] * (xplus - xminus) + coeff[2] * (yplus - yminus) + coeff[3] * (zplus - zminus))
    return (result - 7.0 * center) / 6.0

def cholesky_solve(normal, target):
    lower = jnp.linalg.cholesky(normal)
    middle = lax.linalg.triangular_solve(lower, target, left_side=True, lower=True)
    return lax.linalg.triangular_solve(lower, middle, left_side=True, lower=True, transpose_a=True)

def small_solve(gram, count, steps):
    cols = count * (steps + 1)
    change = 7.0 * jnp.eye(cols, count * steps, dtype=gram.dtype) + 6.0 * jnp.eye(cols, count * steps, k=-count, dtype=gram.dtype)
    high = lax.Precision.HIGHEST
    gram_change = jnp.dot(gram, change, precision=high)
    normal = jnp.dot(change.T, gram_change, precision=high)
    target = jnp.dot(change.T, gram[:, :count], precision=high)
    coef = cholesky_solve(normal, target)
    return (coef, jnp.dot(change, coef, precision=high))

def reference(right_side, absorption, velocity):
    coeff = jnp.concatenate([absorption[None], velocity], axis=0)
    blocks = [right_side]
    current = right_side
    for step in range(STEPS):
        current = apply_shifted(current, coeff)
        blocks.append(current)
    count = right_side.shape[0]
    basis = jnp.stack(blocks).reshape(count * (STEPS + 1), -1)
    high = lax.Precision.HIGHEST
    gram = jnp.dot(basis, basis.T, precision=high)
    coef, mixed = small_solve(gram, count, STEPS)
    solution_field = jnp.dot(coef.T, basis[:count * STEPS], precision=high)
    residual = basis[:count] - jnp.dot(mixed.T, basis, precision=high)
    return (solution_field.reshape(right_side.shape), residual.reshape(right_side.shape))
```

```python
import jax
import jax.numpy as jnp
from jax import lax
from jax.experimental import pallas as pl
from jax.experimental.pallas import tpu as pltpu
from jax.sharding import Mesh, PartitionSpec as P

RHS = 16
STEPS = 4
COLS = RHS * (STEPS + 1)
KEEP = RHS * STEPS
FIELDS = RHS + 1
ALL = FIELDS + 5
LIMIT = 48 * 1024 * 1024
F32 = jnp.float32
BF16 = jnp.bfloat16


def lanes():
    return lax.broadcasted_iota(jnp.int32, (8, 128), 1)


def rolled(x, amount):
    amount = amount % x.shape[-1]
    return x if amount == 0 else pltpu.roll(x, amount, x.ndim - 1)


def wide(pieces):
    return jnp.concatenate(pieces, axis=0)


def pack_z(rs, ab, ve, out):
    group = lanes() // 8
    for x in range(8):
        acc = rolled(rs[x * 8 : x * 8 + 8, :], 4)
        for r in range(1, RHS):
            acc = jnp.where(group == r, rolled(rs[r * 64 + x * 8 : r * 64 + x * 8 + 8, :], 8 * r + 4), acc)
        out[x * 8 : x * 8 + 8, :] = acc
        acc = rolled(ab[x * 8 : x * 8 + 8, :], 4)
        for f in range(3):
            acc = jnp.where(
                group == f + 1, rolled(ve[f * 64 + x * 8 : f * 64 + x * 8 + 8, :], 8 * (f + 1) + 4), acc
            )
        out[64 + x * 8 : 64 + x * 8 + 8, :] = acc


def pack_xy(flags, rs, ab, ve, zprev, znext, slab, xlow, xhigh, ylow, yhigh):
    low = lanes() % 8 < 4
    zm, zp = flags[4], flags[5]
    for x in range(8):
        at = slice(x * 8, x * 8 + 8)
        slab[at, :] = jnp.where(low, zprev[at, :] * zm, znext[at, :] * zp)
        at = slice(64 + x * 8, 64 + x * 8 + 8)
        slab[at, :] = jnp.where(low, zprev[at, :], znext[at, :])

    def put(f, src, base):
        for x in range(8):
            tile = src[pl.ds(base + x * 8, 8), :]
            if x < 4:
                xlow[pl.ds(f * 32 + x * 8, 8), :] = tile
            else:
                xhigh[pl.ds(f * 32 + (x - 4) * 8, 8), :] = tile
            ylow[pl.ds(f * 32 + x * 4, 4), :] = tile[:4]
            yhigh[pl.ds(f * 32 + x * 4, 4), :] = tile[4:]

    for r in range(RHS):
        put(r, rs, r * 64)
    put(RHS, slab, 0)
    put(RHS + 1, ab, 0)
    for f in range(3):
        put(RHS + 2 + f, ve, f * 64)
    put(RHS + 5, slab, 64)


EDGES = ((-1, 3, 0), (8, 3, 3), (-2, 2, 6), (9, 2, 8), (-3, 1, 10), (10, 1, 11))


def pack_edges(xprev, xnext, ylow, yhigh):
    def body(f, carry):
        for x, rows, at in EDGES:
            src = xprev if x < 0 else xnext
            start = f * 32 + (x + 4 if x < 0 else x - 8) * 8
            tile = src[pl.ds(start, 8), :]
            ylow[pl.ds(f * 12 + at, rows), :] = tile[:rows]
            yhigh[pl.ds(f * 12 + at, rows), :] = tile[8 - rows :]
        return carry

    lax.fori_loop(0, ALL, body, 0)


def steps_gram(
    flags, rs, ab, ve, slab, xprev, xnext, yprev, ynext, eprev, enext, basis, packed, ea, eb, ec, main, side
):
    lane = lanes()
    lane8 = lane % 8
    group = lane // 8
    row = lax.broadcasted_iota(jnp.int32, (8, 128), 0)
    xm, xp, ym, yp, zm, zp = [flags[i] for i in range(6)]

    def fill(f, dst, base, src, at):
        one = jnp.float32(1)
        for x in range(8):
            dst[pl.ds(base + (x + 4) * 16 + 4, 8), :] = src[pl.ds(at + x * 8, 8), :]
            dst[pl.ds(base + (x + 4) * 16, 4), :] = yprev[pl.ds(f * 32 + x * 4, 4), :] * ym
            dst[pl.ds(base + (x + 4) * 16 + 12, 4), :] = ynext[pl.ds(f * 32 + x * 4, 4), :] * yp
        for x in range(4):
            dst[pl.ds(base + x * 16 + 4, 8), :] = xprev[pl.ds(f * 32 + x * 8, 8), :] * xm
            dst[pl.ds(base + (x + 12) * 16 + 4, 8), :] = xnext[pl.ds(f * 32 + x * 8, 8), :] * xp
        for x, rows, off in EDGES:
            m = xm if x < 0 else xp
            dst[pl.ds(base + (x + 4) * 16 + 4 - rows, rows), :] = eprev[pl.ds(f * 12 + off, rows), :] * (m * ym)
            dst[pl.ds(base + (x + 4) * 16 + 12, rows), :] = enext[pl.ds(f * 12 + off, rows), :] * (m * yp)

    def fill_rhs(r, carry):
        fill(r, ea, r * 256, rs, r * 64)
        for x in range(8):
            basis[pl.ds(x * 8 * COLS + r, 8, stride=COLS), :] = rs[pl.ds(r * 64 + x * 8, 8), :]
        return carry

    lax.fori_loop(0, RHS, fill_rhs, 0)
    fill(RHS, ea, RHS * 256, slab, 0)
    fill(RHS + 1, ec, 0, ab, 0)
    for i in range(3):
        fill(RHS + 2 + i, ec, (i + 1) * 256, ve, i * 64)
    fill(RHS + 5, ec, 4 * 256, slab, 64)

    def weights(dst, at, a, vs, ok):
        sixth = ok * F32(1 / 6)
        dst[pl.ds(at, 8), :] = (a - 1.0) * sixth
        for i in range(3):
            dst[pl.ds((2 * i + 1) * 256 + at, 8), :] = (0.5 * vs[i] - 1.0) * sixth
            dst[pl.ds((2 * i + 2) * 256 + at, 8), :] = (-0.5 * vs[i] - 1.0) * sixth

    def make(x, carry):
        okx = jnp.where(x < 4, xm, jnp.where(x >= 12, xp, F32(1)))
        for row0 in (1, 7):
            at = x * 16 + row0
            ok = okx * jnp.where(row + row0 < 4, ym, jnp.where(row + row0 >= 12, yp, F32(1)))
            vs = [ec[pl.ds((i + 1) * 256 + at, 8), :] for i in range(3)]
            weights(main, at, ec[pl.ds(at, 8), :], vs, ok)
            narrow = ec[pl.ds(4 * 256 + at, 8), :]
            spread = []
            for i in range(4):
                part = jnp.where(lane < 8, rolled(narrow, -8 * i), 0.0)
                for by in (8, 16, 32, 64):
                    part = part + rolled(part, by)
                spread.append(part)
            okz = jnp.where(lane8 < 4, zm, zp)
            weights(side, at, spread[0], spread[1:], ok * okz)
        return carry

    lax.fori_loop(1, 15, make, 0)

    for s in range(1, STEPS + 1):
        src, dst = (ea, eb) if s % 2 else (eb, ea)
        last = s == STEPS

        def plane(x, carry, s=s, src=src, dst=dst, last=last):
            for row0 in (4,) if last else (s, 8 - s):
                at = x * 16 + row0
                cm = [main[pl.ds(i * 256 + at, 8), :] for i in range(7)]
                edge = src[pl.ds(RHS * 256 + at, 8), :]

                def apply(c, base, v, zplus, zminus):
                    out = c[0] * v
                    out = out + c[1] * src[pl.ds(base + at + 16, 8), :]
                    out = out + c[2] * src[pl.ds(base + at - 16, 8), :]
                    out = out + c[3] * src[pl.ds(base + at + 1, 8), :]
                    out = out + c[4] * src[pl.ds(base + at - 1, 8), :]
                    out = out + c[5] * zplus
                    return out + c[6] * zminus

                ends = edge
                for r in range(RHS):
                    v = src[pl.ds(r * 256 + at, 8), :]
                    turn = rolled(edge, -(8 * r + 4))
                    zplus = rolled(jnp.where(lane == 0, turn, v), -1)
                    zminus = rolled(jnp.where(lane == 127, turn, v), 1)
                    out = apply(cm, r * 256, v, zplus, zminus)
                    if last:
                        first = (x - 4) * 8 * COLS + s * RHS + r
                        basis[pl.ds(first, 8, stride=COLS), :] = out
                    else:
                        dst[pl.ds(r * 256 + at, 8), :] = out
                        ends = jnp.where(group == r, rolled(v, 8 * r + 4), ends)
                if not last:
                    cs = [side[pl.ds(i * 256 + at, 8), :] for i in range(7)]
                    zplus = rolled(jnp.where(lane8 == 4, ends, edge), -1)
                    zminus = rolled(jnp.where(lane8 == 3, ends, edge), 1)
                    dst[pl.ds(RHS * 256 + at, 8), :] = apply(cs, RHS * 256, edge, zplus, zminus)
            return carry

        lax.fori_loop(s, 16 - s, plane, 0)
        if not last:

            def keep(r, carry, s=s, dst=dst):
                for x in range(8):
                    value = dst[pl.ds(r * 256 + (x + 4) * 16 + 4, 8), :]
                    basis[pl.ds(x * 8 * COLS + s * RHS + r, 8, stride=COLS), :] = value
                return carry

            lax.fori_loop(0, RHS, keep, 0)

    zeros = jnp.zeros((128 - COLS, 256), BF16)

    def product(i, acc):
        base = pl.multiple_of(i * 2 * COLS, 2 * COLS)
        value = jnp.concatenate([basis[pl.ds(base, COLS), :], basis[pl.ds(base + COLS, COLS), :]], axis=1)
        high = value.astype(BF16)
        low = (value - high.astype(F32)).astype(BF16)
        return acc + lax.dot_general(
            wide([high, low]),
            wide([high, zeros, low, zeros]),
            (((1,), (1,)), ((), ())),
            preferred_element_type=F32,
        )

    acc = lax.fori_loop(0, 32, product, jnp.zeros((2 * COLS, 256), F32))
    gram = (acc[:COLS, :128] + acc[COLS:, 128:]) + (acc[:COLS, 128:] + acc[COLS:, :128])
    part = [gram[i * RHS : (i + 1) * RHS] for i in range(STEPS + 1)]
    lane = lax.broadcasted_iota(jnp.int32, (RHS, 128), 1)
    packed[:RHS, :] = jnp.where(
        lane < 80, part[0], jnp.where(lane < 112, rolled(part[3], 32), rolled(part[4], 48))
    )
    packed[RHS:, :] = jnp.where(
        lane < 64, rolled(part[1], -16), jnp.where(lane < 112, rolled(part[2], 32), 0.0)
    )


def solve_combine(parts, basis, solution_field, residual):
    total = parts[0]
    for i in range(1, parts.shape[0]):
        total = total + parts[i]
    first, second = total[:RHS], total[RHS:]
    lane = lax.broadcasted_iota(jnp.int32, (RHS, 128), 1)

    def span(value, start):
        return jnp.where((lane >= start) & (lane < COLS), value, 0.0)

    upper = [
        span(first, 0),
        span(rolled(second, 16), 16),
        span(rolled(second, -32), 32),
        span(rolled(first, -32), 48),
        span(rolled(first, -48), 64),
    ]
    flipped = jnp.transpose(wide(upper + [jnp.zeros((128 - COLS, 128), F32)]))
    gram = wide(
        [
            jnp.where(lane < i * RHS, flipped[i * RHS : (i + 1) * RHS], upper[i])
            for i in range(STEPS + 1)
        ]
    )
    half = 7.0 * gram + 6.0 * rolled(gram, -RHS)
    half = jnp.where(lax.broadcasted_iota(jnp.int32, (COLS, 128), 1) < KEEP, half, 0.0)
    normal = 7.0 * half[:KEEP] + 6.0 * half[RHS:]
    m = [normal[i * 8 : i * 8 + 8] for i in range(8)] + [half[:8], half[8:RHS]]
    lane = lanes()
    for k in range(KEEP):
        i0, s = divmod(k, 8)
        pivot_row = m[i0][s : s + 1, :]
        inverse = 1.0 / pivot_row[:, k : k + 1]
        scaled = pivot_row * inverse
        for i in range(i0 if s < 7 else i0 + 1, 10):
            column = jnp.broadcast_to(m[i][:, k : k + 1], (8, 128))
            m[i] = jnp.where(lane == k, column * inverse, m[i] - column * scaled)
    coef = wide(m[8:])
    mixed = 7.0 * coef + 6.0 * rolled(coef, RHS)
    both = wide([coef, mixed])
    high = both.astype(BF16).astype(F32)
    low = both - high
    lane = lax.broadcasted_iota(jnp.int32, (2 * RHS, 128), 1)
    left = jnp.where(lane < 80, high, rolled(high, 80))
    right = jnp.where(lane < 32, rolled(high, -48), jnp.where(lane < 112, rolled(low, 32), 0.0))
    factors = jnp.concatenate([left, right], axis=1).astype(BF16)
    zeros = jnp.zeros((16, 256), BF16)

    def combine(i, carry):
        base = pl.multiple_of(i * 2 * COLS, 2 * COLS)
        value = jnp.concatenate([basis[pl.ds(base, COLS), :], basis[pl.ds(base + COLS, COLS), :]], axis=1)
        high = value.astype(BF16)
        low = (value - high.astype(F32)).astype(BF16)
        out = jnp.dot(factors, wide([high, low, high, zeros]), preferred_element_type=F32)
        rest = value[:RHS] - out[RHS:]
        for c in range(2):
            at = pl.ds(2 * i + c, RHS, stride=64)
            solution_field[at, :] = out[:RHS, c * 128 : (c + 1) * 128]
            residual[at, :] = rest[:, c * 128 : (c + 1) * 128]
        return carry

    lax.fori_loop(0, 32, combine, 0)


def call(kernel, ins, outs, scratch=(), smem=False):
    vmem = pl.BlockSpec(memory_space=pltpu.VMEM)
    specs = [vmem] * len(ins)
    if smem:
        specs[0] = pl.BlockSpec(memory_space=pltpu.SMEM)
    return pl.pallas_call(
        kernel,
        out_shape=[jax.ShapeDtypeStruct(s, F32) for s in outs],
        in_specs=specs,
        out_specs=[vmem] * len(outs),
        scratch_shapes=[pltpu.VMEM(s, F32) for s in scratch],
        compiler_params=pltpu.CompilerParams(vmem_limit_bytes=LIMIT),
    )(*ins)


def shift(value, axis, by):
    count = lax.axis_size(axis)
    return lax.ppermute(value, axis, [(i, (i + by) % count) for i in range(count)])


def gathered(value, axis):
    count = lax.axis_size(axis)
    return lax.all_to_all(jnp.broadcast_to(value[None], (count,) + value.shape), axis, 0, 0)


def shards(right_side, absorption, velocity):
    axes = ("gx", "gy", ("zx", "core"))
    ends = []
    for axis in axes:
        at = lax.axis_index(axis)
        ends += [at > 0, at < lax.axis_size(axis) - 1]
    flags = jnp.stack(ends).astype(F32)
    rs = right_side.reshape(1024, 128)
    ab = absorption.reshape(64, 128)
    ve = velocity.reshape(192, 128)

    (ends_z,) = call(pack_z, [rs, ab, ve], [(128, 128)])
    zprev = shift(ends_z, axes[2], 1)
    znext = shift(ends_z, axes[2], -1)
    face = (ALL * 32, 128)
    slab, xlow, xhigh, ylow, yhigh = call(
        pack_xy, [flags, rs, ab, ve, zprev, znext], [(128, 128), face, face, face, face], smem=True
    )
    xprev = shift(xhigh, "gx", 1)
    xnext = shift(xlow, "gx", -1)
    yprev = shift(yhigh, "gy", 1)
    ynext = shift(ylow, "gy", -1)
    edge = (ALL * 12, 128)
    elow, ehigh = call(pack_edges, [xprev, xnext], [edge, edge])
    eprev = shift(ehigh, "gy", 1)
    enext = shift(elow, "gy", -1)
    basis, packed = call(
        steps_gram,
        [flags, rs, ab, ve, slab, xprev, xnext, yprev, ynext, eprev, enext],
        [(64 * COLS, 128), (2 * RHS, 128)],
        [(FIELDS * 256, 128), (FIELDS * 256, 128), (5 * 256, 128), (7 * 256, 128), (7 * 256, 128)],
        smem=True,
    )
    packed = packed + shift(packed, "core", 1)
    packed = gathered(packed, ("gx", "zx")).sum(0)
    parts = gathered(packed, "gy")
    solution_field, residual = call(solve_combine, [parts, basis], [(1024, 128), (1024, 128)])
    return solution_field.reshape(right_side.shape), residual.reshape(right_side.shape)


def solution(mesh):
    nx, ny, nz = mesh.devices.shape
    split = Mesh(mesh.devices.reshape(nx, ny, nz // 2, 2), ("gx", "gy", "zx", "core"))
    z = ("zx", "core")
    return jax.shard_map(
        shards,
        mesh=split,
        in_specs=(P(None, "gx", "gy", z), P("gx", "gy", z), P(None, "gx", "gy", z)),
        out_specs=(P(None, "gx", "gy", z), P(None, "gx", "gy", z)),
        check_vma=False,
    )
```

```python
import jax
import jax.numpy as jnp
from jax import lax
from jax.experimental import pallas as pl
from jax.experimental.pallas import tpu as pltpu
from jax.sharding import Mesh, PartitionSpec as P

RHS = 16
STEPS = 4
COLS = RHS * (STEPS + 1)
KEEP = RHS * STEPS
FIELDS = RHS + 1
ALL = FIELDS + 5
ENDS = 8
MAKES = 2
TURNS = 1
SOME = (0, 7, 6, 5, 4)
KEEPS = 4
GROUP = 4
GRAMS = 8
PAIRS = 16
BLOCK = 4
LOW = RHS * 256
HIGH = LOW + 256
LIMIT = 48 * 1024 * 1024
F32 = jnp.float32
BF16 = jnp.bfloat16


def lanes():
    return lax.broadcasted_iota(jnp.int32, (8, 128), 1)


def rolled(x, amount):
    amount = amount % x.shape[-1]
    return x if amount == 0 else pltpu.roll(x, amount, x.ndim - 1)


def wide(pieces):
    return jnp.concatenate(pieces, axis=0)


def pack_z(rs_in, ab_in, ve_in, rs, ab, ve, out, sems):
    pairs = ((rs_in, rs), (ab_in, ab), (ve_in, ve))
    copies = [pltpu.make_async_copy(a, b, sems.at[i]) for i, (a, b) in enumerate(pairs)]
    for copy in copies:
        copy.start()
    for copy in copies:
        copy.wait()
    group = lanes() // 8
    for x in range(8):
        acc = rolled(rs[x * 8 : x * 8 + 8, :], 4)
        for r in range(1, RHS):
            acc = jnp.where(group == r, rolled(rs[r * 64 + x * 8 : r * 64 + x * 8 + 8, :], 8 * r + 4), acc)
        out[x * 8 : x * 8 + 8, :] = acc
        acc = rolled(ab[x * 8 : x * 8 + 8, :], 4)
        for f in range(3):
            acc = jnp.where(
                group == f + 1, rolled(ve[f * 64 + x * 8 : f * 64 + x * 8 + 8, :], 8 * (f + 1) + 4), acc
            )
        out[64 + x * 8 : 64 + x * 8 + 8, :] = acc


def pack_xy(flags, rs, ab, ve, zprev, znext, slab, xlow, xhigh, ylow, yhigh):
    low = lanes() % 8 < 4
    zm, zp = flags[4], flags[5]
    for x in range(8):
        at = slice(x * 8, x * 8 + 8)
        slab[at, :] = jnp.where(low, zprev[at, :] * zm, znext[at, :] * zp)
        at = slice(64 + x * 8, 64 + x * 8 + 8)
        slab[at, :] = jnp.where(low, zprev[at, :], znext[at, :])

    def put(f, src, base):
        for x in range(8):
            tile = src[pl.ds(base + x * 8, 8), :]
            if x < 4:
                xlow[pl.ds(f * 32 + x * 8, 8), :] = tile
            else:
                xhigh[pl.ds(f * 32 + (x - 4) * 8, 8), :] = tile
            ylow[pl.ds(f * 32 + x * 4, 4), :] = tile[:4]
            yhigh[pl.ds(f * 32 + x * 4, 4), :] = tile[4:]

    for r in range(RHS):
        put(r, rs, r * 64)
    put(RHS, slab, 0)
    put(RHS + 1, ab, 0)
    for f in range(3):
        put(RHS + 2 + f, ve, f * 64)
    put(RHS + 5, slab, 64)


EDGES = ((-1, 3, 0), (8, 3, 3), (-2, 2, 6), (9, 2, 8), (-3, 1, 10), (10, 1, 11))


def pack_edges(xprev, xnext, ylow, yhigh):
    def body(f, carry):
        for x, rows, at in EDGES:
            src = xprev if x < 0 else xnext
            start = f * 32 + (x + 4 if x < 0 else x - 8) * 8
            tile = src[pl.ds(start, 8), :]
            ylow[pl.ds(f * 12 + at, rows), :] = tile[:rows]
            yhigh[pl.ds(f * 12 + at, rows), :] = tile[8 - rows :]
        return carry

    lax.fori_loop(0, ALL, body, 0)


def steps_gram(
    flags, rs, ab, ve, slab, xprev, xnext, yprev, ynext, eprev, enext, basis, packed, ea, eb, es, ec, main, side, turn
):
    lane = lanes()
    lane8 = lane % 8
    group = lane // 8
    row = lax.broadcasted_iota(jnp.int32, (8, 128), 0)
    xm, xp, ym, yp, zm, zp = [flags[i] for i in range(6)]

    def fill(f, dst, base, src, at):
        one = jnp.float32(1)
        for x in range(8):
            dst[pl.ds(base + (x + 4) * 16 + 4, 8), :] = src[pl.ds(at + x * 8, 8), :]
            dst[pl.ds(base + (x + 4) * 16, 4), :] = yprev[pl.ds(f * 32 + x * 4, 4), :] * ym
            dst[pl.ds(base + (x + 4) * 16 + 12, 4), :] = ynext[pl.ds(f * 32 + x * 4, 4), :] * yp
        for x in range(4):
            dst[pl.ds(base + x * 16 + 4, 8), :] = xprev[pl.ds(f * 32 + x * 8, 8), :] * xm
            dst[pl.ds(base + (x + 12) * 16 + 4, 8), :] = xnext[pl.ds(f * 32 + x * 8, 8), :] * xp
        for x, rows, off in EDGES:
            m = xm if x < 0 else xp
            dst[pl.ds(base + (x + 4) * 16 + 4 - rows, rows), :] = eprev[pl.ds(f * 12 + off, rows), :] * (m * ym)
            dst[pl.ds(base + (x + 4) * 16 + 12, rows), :] = enext[pl.ds(f * 12 + off, rows), :] * (m * yp)

    def fill_rhs(r, carry):
        fill(r, ea, r * 256, rs, r * 64)
        for x in range(8):
            basis[pl.ds(x * 8 * COLS + r, 8, stride=COLS), :] = rs[pl.ds(r * 64 + x * 8, 8), :]
        return carry

    lax.fori_loop(0, RHS, fill_rhs, 0)
    fill(RHS, es, 0, slab, 0)
    fill(RHS + 1, ec, 0, ab, 0)
    for i in range(3):
        fill(RHS + 2 + i, ec, (i + 1) * 256, ve, i * 64)
    fill(RHS + 5, ec, 4 * 256, slab, 64)

    def ends(i, carry):
        tiles = [(i * ENDS + u) * 16 + row0 for u in range(ENDS) for row0 in (0, 8)]
        done = []
        for at in tiles:
            outer = es[pl.ds(at, 8), :]
            inner = rolled(ea[pl.ds(at, 8), :], 4)
            for r in range(1, RHS):
                inner = jnp.where(group == r, rolled(ea[pl.ds(r * 256 + at, 8), :], 8 * r + 4), inner)
            done.append((jnp.where(lane8 < 4, outer, inner), jnp.where(lane8 < 4, inner, outer)))
        for at, (low, high) in zip(tiles, done):
            ea[pl.ds(LOW + at, 8), :] = low
            ea[pl.ds(HIGH + at, 8), :] = high
        return carry

    lax.fori_loop(0, 16 // ENDS, ends, 0)

    def weights(a, vs, ok):
        sixth = ok * F32(1 / 6)
        out = [(a - 1.0) * sixth]
        for v in vs:
            out += [(0.5 * v - 1.0) * sixth, (-0.5 * v - 1.0) * sixth]
        return out

    def make(i, carry):
        done = []
        for x, row0 in [(1 + i * MAKES + u, row0) for u in range(MAKES) for row0 in (1, 7)]:
            okx = jnp.where(x < 4, xm, jnp.where(x >= 12, xp, F32(1)))
            at = x * 16 + row0
            ok = okx * jnp.where(row + row0 < 4, ym, jnp.where(row + row0 >= 12, yp, F32(1)))
            cs = [ec[pl.ds(i * 256 + at, 8), :] for i in range(4)]
            done.append((main, at, weights(cs[0], cs[1:], ok)))
            outer = ec[pl.ds(4 * 256 + at, 8), :]
            inner = rolled(cs[0], 4)
            for i in range(1, 4):
                inner = jnp.where(group == i, rolled(cs[i], 8 * i + 4), inner)
            for k, (pick, okz) in enumerate(((lane8 < 4, zm), (lane8 >= 4, zp))):
                narrow = jnp.where(pick, outer, inner)
                cs = [jnp.take_along_axis(narrow, lane8 + 8 * i, axis=1) for i in range(4)]
                done.append((side, k * 7 * 256 + at, weights(cs[0], cs[1:], ok * jnp.where(pick, okz, F32(1)))))
        for dst, at, values in done:
            for i in range(7):
                dst[pl.ds(i * 256 + at, 8), :] = values[i]
        return carry

    lax.fori_loop(0, 14 // MAKES, make, 0)

    for s in range(1, STEPS + 1):
        src, dst = (ea, eb) if s % 2 else (eb, ea)
        last = s == STEPS
        row0s = (4,) if last else (s, 8 - s)

        planes = 16 - 2 * s

        def beyond(i, carry, s=s, src=src, row0s=row0s, planes=planes):
            some = planes // TURNS
            tiles = [(s + i * some + u) * 16 + row0 for u in range(some) for row0 in row0s]
            both = [
                jnp.where(lane8 == 4, src[pl.ds(HIGH + at, 8), :], src[pl.ds(LOW + at, 8), :]) for at in tiles
            ]
            for at, value in zip(tiles, both):
                for r in range(RHS):
                    turn[pl.ds(r * 256 + at, 8), :] = rolled(value, -(8 * r + 4))
            return carry

        lax.fori_loop(0, TURNS, beyond, 0)

        def plane(i, carry, s=s, src=src, dst=dst, last=last, row0s=row0s):
            for x, row0 in [(s + i * SOME[s] + u, row0) for u in range(SOME[s]) for row0 in row0s]:
                at = x * 16 + row0

                def apply(c, base, v, zplus, zminus):
                    out = c[0] * v
                    out = out + c[1] * src[pl.ds(base + at + 16, 8), :]
                    out = out + c[2] * src[pl.ds(base + at - 16, 8), :]
                    out = out + c[3] * src[pl.ds(base + at + 1, 8), :]
                    out = out + c[4] * src[pl.ds(base + at - 1, 8), :]
                    out = out + c[5] * zplus
                    return out + c[6] * zminus

                cs = [main[pl.ds(i * 256 + at, 8), :] for i in range(7)]
                outs = []
                for r in range(RHS):
                    v = src[pl.ds(r * 256 + at, 8), :]
                    over = turn[pl.ds(r * 256 + at, 8), :]
                    zplus = rolled(jnp.where(lane == 0, over, v), -1)
                    zminus = rolled(jnp.where(lane == 127, over, v), 1)
                    outs.append(apply(cs, r * 256, v, zplus, zminus))
                    if len(outs) == GROUP:
                        for k, out in enumerate(outs):
                            q = r + 1 - GROUP + k
                            if last:
                                basis[pl.ds((x - 4) * 8 * COLS + s * RHS + q, 8, stride=COLS), :] = out
                            else:
                                dst[pl.ds(q * 256 + at, 8), :] = out
                        outs = []
                if not last:
                    for k, base in enumerate((LOW, HIGH)):
                        cs = [side[pl.ds((k * 7 + i) * 256 + at, 8), :] for i in range(7)]
                        v = src[pl.ds(base + at, 8), :]
                        dst[pl.ds(base + at, 8), :] = apply(cs, base, v, rolled(v, -1), rolled(v, 1))
            return carry

        lax.fori_loop(0, planes // SOME[s], plane, 0)
        if not last:

            def keep(i, carry, s=s, dst=dst):
                where = [(i * KEEPS + u, x) for u in range(KEEPS) for x in range(8)]
                values = [dst[pl.ds(r * 256 + (x + 4) * 16 + 4, 8), :] for r, x in where]
                for (r, x), value in zip(where, values):
                    basis[pl.ds(x * 8 * COLS + s * RHS + r, 8, stride=COLS), :] = value
                return carry

            lax.fori_loop(0, RHS // KEEPS, keep, 0)

    zeros = jnp.zeros((128 - COLS, 256), BF16)

    def product(i, acc):
        for u in range(GRAMS):
            base = pl.multiple_of((i * GRAMS + u) * 2 * COLS, 2 * COLS)
            value = jnp.concatenate([basis[pl.ds(base, COLS), :], basis[pl.ds(base + COLS, COLS), :]], axis=1)
            high = value.astype(BF16)
            low = (value - high.astype(F32)).astype(BF16)
            acc = acc + lax.dot_general(
                wide([high, low]),
                wide([high, zeros, low, zeros]),
                (((1,), (1,)), ((), ())),
                preferred_element_type=F32,
            )
        return acc

    acc = lax.fori_loop(0, 32 // GRAMS, product, jnp.zeros((2 * COLS, 256), F32))
    gram = (acc[:COLS, :128] + acc[COLS:, 128:]) + (acc[:COLS, 128:] + acc[COLS:, :128])
    part = [gram[i * RHS : (i + 1) * RHS] for i in range(STEPS + 1)]
    lane = lax.broadcasted_iota(jnp.int32, (RHS, 128), 1)
    packed[:RHS, :] = jnp.where(
        lane < 80, part[0], jnp.where(lane < 112, rolled(part[3], 32), rolled(part[4], 48))
    )
    packed[RHS:, :] = jnp.where(
        lane < 64, rolled(part[1], -16), jnp.where(lane < 112, rolled(part[2], 32), 0.0)
    )


def solve_combine(parts, basis, solution_field, residual):
    total = parts[0]
    for i in range(1, parts.shape[0]):
        total = total + parts[i]
    first, second = total[:RHS], total[RHS:]
    lane = lax.broadcasted_iota(jnp.int32, (RHS, 128), 1)

    def span(value, start):
        return jnp.where((lane >= start) & (lane < COLS), value, 0.0)

    upper = [
        span(first, 0),
        span(rolled(second, 16), 16),
        span(rolled(second, -32), 32),
        span(rolled(first, -32), 48),
        span(rolled(first, -48), 64),
    ]
    flipped = jnp.transpose(wide(upper + [jnp.zeros((128 - COLS, 128), F32)]))
    gram = wide(
        [
            jnp.where(lane < i * RHS, flipped[i * RHS : (i + 1) * RHS], upper[i])
            for i in range(STEPS + 1)
        ]
    )
    half = 7.0 * gram + 6.0 * rolled(gram, -RHS)
    half = jnp.where(lax.broadcasted_iota(jnp.int32, (COLS, 128), 1) < KEEP, half, 0.0)
    normal = 7.0 * half[:KEEP] + 6.0 * half[RHS:]
    m = [normal[i * 8 : i * 8 + 8] for i in range(8)] + [half[:8], half[8:RHS]]
    lane = lanes()
    for k in range(0, KEEP, BLOCK):
        i0, s = divmod(k, 8)
        inside = (lane >= k) & (lane < k + BLOCK)
        keep = list(range(i0 + 1 if s + BLOCK == 8 else i0, 10))
        columns = {
            i: [jnp.broadcast_to(m[i][:, k + c : k + c + 1], (8, 128)) for c in range(BLOCK)]
            for i in sorted({i0, *keep})
        }

        def spread(value, c, s=s):
            return jnp.broadcast_to(value[s + c : s + c + 1, :], (8, 128))

        pivots = [[spread(columns[i0][c], d) for c in range(BLOCK)] for d in range(BLOCK)]
        rows = [
            jnp.where(lane == k + d, -1.0, jnp.where(inside, 0.0, spread(m[i0], d))) for d in range(BLOCK)
        ]
        for d in range(BLOCK):
            inverse = 1.0 / pivots[d][d]
            for c in range(d + 1, BLOCK):
                pivots[d][c] = pivots[d][c] * inverse
            rows[d] = rows[d] * inverse
            for e in range(BLOCK):
                if e != d:
                    for c in range(d + 1, BLOCK):
                        pivots[e][c] = pivots[e][c] - pivots[e][d] * pivots[d][c]
                    rows[e] = rows[e] - pivots[e][d] * rows[d]
        for i in keep:
            value = jnp.where(inside, 0.0, m[i])
            for c in range(BLOCK):
                value = value - columns[i][c] * rows[c]
            m[i] = value
    coef = wide(m[8:])
    mixed = 7.0 * coef + 6.0 * rolled(coef, RHS)
    both = wide([coef, mixed])
    high = both.astype(BF16).astype(F32)
    mid = (both - high).astype(BF16).astype(F32)
    low = both - high - mid
    lane = lax.broadcasted_iota(jnp.int32, (2 * RHS, 128), 1)

    def tripled(value, parts):
        left = value if parts == 1 else jnp.where(lane < 80, value, rolled(value, 80))
        right = jnp.where(lane < 32, rolled(value, -48), 0.0) if parts > 1 else jnp.zeros_like(value)
        if parts == 3:
            right = jnp.where((lane >= 32) & (lane < 112), rolled(value, 32), right)
        return jnp.concatenate([left, right], axis=1)

    factors = wide([tripled(high, 3), tripled(mid, 2), tripled(low, 1)[RHS:]]).astype(BF16)
    zeros = jnp.zeros((16, 256), BF16)

    def combine(i, carry):
        done = []
        for u in range(PAIRS):
            base = pl.multiple_of((i * PAIRS + u) * 2 * COLS, 2 * COLS)
            value = jnp.concatenate([basis[pl.ds(base, COLS), :], basis[pl.ds(base + COLS, COLS), :]], axis=1)
            high = value.astype(BF16)
            rest = value - high.astype(F32)
            mid = rest.astype(BF16)
            low = (rest - mid.astype(F32)).astype(BF16)
            out = jnp.dot(factors, wide([high, mid, low, zeros]), preferred_element_type=F32)
            mixed = out[RHS : 2 * RHS] + (out[3 * RHS : 4 * RHS] + out[4 * RHS :])
            done.append((out[:RHS] + out[2 * RHS : 3 * RHS], value[:RHS] - mixed))
        for u in range(PAIRS):
            for c in range(2):
                at = pl.ds(2 * (i * PAIRS + u) + c, RHS, stride=64)
                solution_field[at, :] = done[u][0][:, c * 128 : (c + 1) * 128]
                residual[at, :] = done[u][1][:, c * 128 : (c + 1) * 128]
        return carry

    lax.fori_loop(0, 32 // PAIRS, combine, 0)


def call(kernel, ins, outs, scratch=(), smem=False, hbm=False):
    vmem = pl.BlockSpec(memory_space=pltpu.VMEM)
    specs = [pl.BlockSpec(memory_space=pl.ANY) if hbm else vmem] * len(ins)
    if smem:
        specs[0] = pl.BlockSpec(memory_space=pltpu.SMEM)
    return pl.pallas_call(
        kernel,
        out_shape=[jax.ShapeDtypeStruct(s, F32) for s in outs],
        in_specs=specs,
        out_specs=[vmem] * len(outs),
        scratch_shapes=[pltpu.VMEM(s, F32) if isinstance(s, tuple) else s for s in scratch],
        compiler_params=pltpu.CompilerParams(vmem_limit_bytes=LIMIT),
    )(*ins)


def shift(value, axis, by):
    count = lax.axis_size(axis)
    return lax.ppermute(value, axis, [(i, (i + by) % count) for i in range(count)])


def gathered(value, axis):
    count = lax.axis_size(axis)
    return lax.all_to_all(jnp.broadcast_to(value[None], (count,) + value.shape), axis, 0, 0)


def shards(right_side, absorption, velocity):
    axes = ("gx", "gy", ("zx", "core"))
    ends = []
    for axis in axes:
        at = lax.axis_index(axis)
        ends += [at > 0, at < lax.axis_size(axis) - 1]
    flags = jnp.stack(ends).astype(F32)
    ins = [right_side.reshape(1024, 128), absorption.reshape(64, 128), velocity.reshape(192, 128)]
    rs, ab, ve, ends_z = call(
        pack_z, ins, [(1024, 128), (64, 128), (192, 128), (128, 128)], [pltpu.SemaphoreType.DMA((3,))], hbm=True
    )
    zprev = shift(ends_z, axes[2], 1)
    znext = shift(ends_z, axes[2], -1)
    face = (ALL * 32, 128)
    slab, xlow, xhigh, ylow, yhigh = call(
        pack_xy, [flags, rs, ab, ve, zprev, znext], [(128, 128), face, face, face, face], smem=True
    )
    xprev = shift(xhigh, "gx", 1)
    xnext = shift(xlow, "gx", -1)
    yprev = shift(yhigh, "gy", 1)
    ynext = shift(ylow, "gy", -1)
    edge = (ALL * 12, 128)
    elow, ehigh = call(pack_edges, [xprev, xnext], [edge, edge])
    eprev = shift(ehigh, "gy", 1)
    enext = shift(elow, "gy", -1)
    basis, packed = call(
        steps_gram,
        [flags, rs, ab, ve, slab, xprev, xnext, yprev, ynext, eprev, enext],
        [(64 * COLS, 128), (2 * RHS, 128)],
        [(18 * 256, 128), (18 * 256, 128), (256, 128), (5 * 256, 128), (7 * 256, 128), (14 * 256, 128), (RHS * 256, 128)],
        smem=True,
    )
    packed = packed + shift(packed, "core", 1)
    packed = gathered(packed, ("gx", "zx")).sum(0)
    parts = gathered(packed, "gy")
    solution_field, residual = call(solve_combine, [parts, basis], [(1024, 128), (1024, 128)])
    return solution_field.reshape(right_side.shape), residual.reshape(right_side.shape)


def solution(mesh):
    nx, ny, nz = mesh.devices.shape
    split = Mesh(mesh.devices.reshape(nx, ny, nz // 2, 2), ("gx", "gy", "zx", "core"))
    z = ("zx", "core")
    return jax.shard_map(
        shards,
        mesh=split,
        in_specs=(P(None, "gx", "gy", z), P("gx", "gy", z), P(None, "gx", "gy", z)),
        out_specs=(P(None, "gx", "gy", z), P(None, "gx", "gy", z)),
        check_vma=False,
    )
```

```python
import jax
import jax.numpy as jnp
from jax import lax
from jax.experimental import pallas as pl
from jax.experimental.pallas import tpu as pltpu
from jax.sharding import Mesh, PartitionSpec as P

RHS = 16
STEPS = 4
COLS = RHS * (STEPS + 1)
KEEP = RHS * STEPS
ALL = RHS + 8
FILLS = 4
MAKES = 7
OWN = 8
GRAMS = 16
PAIRS = 16
BLOCK = 4
LOW = RHS * 512
HIGH = LOW + 512
LIMIT = 48 * 1024 * 1024
F32 = jnp.float32
BF16 = jnp.bfloat16


def lanes():
    return lax.broadcasted_iota(jnp.int32, (8, 128), 1)


def rolled(x, amount):
    amount = amount % x.shape[-1]
    return x if amount == 0 else pltpu.roll(x, amount, x.ndim - 1)


def wide(pieces):
    return jnp.concatenate(pieces, axis=0)


def face_at(f, side):
    count = 4 if f < RHS else 3
    start = f * 32 if f < RHS else RHS * 32 + (f - RHS) * 24
    return start, count, (0 if side == 0 else 8 - count)


def pack_own(own, ends, xlow, xhigh, ylow, yhigh):
    group = lanes() // 8
    for x in range(8):
        tiles = [own[f * 64 + x * 8 : f * 64 + x * 8 + 8, :] for f in range(RHS + 4)]
        for part, at in ((tiles[:RHS], 0), (tiles[RHS:], 64)):
            acc = rolled(part[0], 4)
            for i in range(1, len(part)):
                acc = jnp.where(group == i, rolled(part[i], 8 * i + 4), acc)
            ends[at + x * 8 : at + x * 8 + 8, :] = acc
        for f, tile in enumerate(tiles):
            for side, (xout, yout) in enumerate(((xlow, ylow), (xhigh, yhigh))):
                start, count, first = face_at(f, side)
                if first <= x < first + count:
                    xout[start + (x - first) * 8 : start + (x - first) * 8 + 8, :] = tile
                yout[start + x * count : start + x * count + count, :] = tile[first : first + count]


def pack_ends(flags, ends, zprev, znext, slabs, xlow, xhigh):
    low = lanes() % 8 < 4
    zm, zp = flags[4], flags[5]
    for j in range(4):
        for x in range(8):
            at = slice((j % 2) * 64 + x * 8, (j % 2) * 64 + x * 8 + 8)
            if j == 0:
                tile = jnp.where(low, zprev[at, :] * zm, znext[at, :] * zp)
            elif j == 1:
                tile = jnp.where(low, zprev[at, :], znext[at, :])
            else:
                tile = ends[at, :]
            slabs[j * 64 + x * 8 : j * 64 + x * 8 + 8, :] = tile
            xout = xlow if x < 4 else xhigh
            xout[j * 32 + x % 4 * 8 : j * 32 + x % 4 * 8 + 8, :] = tile


EDGES = ((-1, 3, 0), (8, 3, 3), (-2, 2, 6), (9, 2, 8), (-3, 1, 10), (10, 1, 11))


def pack_edges(slabs, xprev, xnext, sprev, snext, ylow, yhigh):
    def put(f, prev, nxt, before, after):
        for x, rows, at in EDGES:
            tile = prev[pl.ds(before + x * 8, 8), :] if x < 0 else nxt[pl.ds(after + (x - 8) * 8, 8), :]
            ylow[pl.ds(f * 12 + at, rows), :] = tile[:rows]
            yhigh[pl.ds(f * 12 + at, rows), :] = tile[8 - rows :]

    def body(f, carry):
        put(f, xprev, xnext, f * 32 + 32, f * 32)
        return carry

    lax.fori_loop(0, RHS, body, 0)
    for i in range(4):
        start = face_at(RHS + i, 0)[0]
        put(RHS + i, xprev, xnext, start + 24, start)
        put(RHS + 4 + i, sprev, snext, i * 32 + 32, i * 32)
        for x in range(8):
            tile = slabs[i * 64 + x * 8 : i * 64 + x * 8 + 8, :]
            ylow[ALL * 12 + i * 24 + x * 3 : ALL * 12 + i * 24 + x * 3 + 3, :] = tile[:3]
            yhigh[ALL * 12 + i * 24 + x * 3 : ALL * 12 + i * 24 + x * 3 + 3, :] = tile[5:]


WIDE = 512
NARROW = 256


def steps_gram(
    flags, fields, slabs, xprev, xnext, sprev, snext, yprev, ynext, eprev, enext,
    basis, packed, ea, eb, es, ec, main, side, turn,
):
    lane = lanes()
    lane8 = lane % 8
    row = lax.broadcasted_iota(jnp.int32, (8, 128), 0)
    xm, xp, ym, yp, zm, zp = [flags[i] for i in range(6)]

    def fill(dst, base, wide_field, own, xs, start, count, ys, ystart, ycount, edge_at):
        size = 32 if wide_field else 16
        own_at, halo_at = ((8, 24), (16, 0)) if wide_field else ((0,), (8,))
        todo = []
        for x in range(8):
            todo.append((own_at, x + 4, 0, own[0][pl.ds(own[1] + x * 8, 8), :]))
            todo.append((halo_at, x + 4, 8 - ycount, ys[0][pl.ds(ystart + x * ycount, ycount), :] * ym))
            todo.append((halo_at, x + 4, 0, ys[1][pl.ds(ystart + x * ycount, ycount), :] * yp))
        for i in range(count):
            todo.append((own_at, 4 - count + i, 0, xs[0][pl.ds(start + i * 8, 8), :] * xm))
            todo.append((own_at, 12 + i, 0, xs[1][pl.ds(start + i * 8, 8), :] * xp))
        for x, rows, at in EDGES:
            m = xm if x < 0 else xp
            todo.append((halo_at, x + 4, 8 - rows, eprev[pl.ds(edge_at + at, rows), :] * (m * ym)))
            todo.append((halo_at, x + 4, 0, enext[pl.ds(edge_at + at, rows), :] * (m * yp)))
        for offsets, x, at, value in todo:
            for offset in offsets:
                dst[pl.ds(base + x * size + offset + at, value.shape[0]), :] = value

    def fill_rhs(i, carry):
        for u in range(FILLS):
            r = i * FILLS + u
            fill(ea, r * WIDE, True, (fields, r * 64), (xprev, xnext), r * 32, 4, (yprev, ynext), r * 32, 4, r * 12)
        values = [fields[pl.ds((i * FILLS + u) * 64 + x * 8, 8), :] for u in range(FILLS) for x in range(8)]
        for u in range(FILLS):
            for x in range(8):
                basis[pl.ds(x * 8 * COLS + i * FILLS + u, 8, stride=COLS), :] = values[u * 8 + x]
        return carry

    lax.fori_loop(0, RHS // FILLS, fill_rhs, 0)
    for i in range(4):
        start = face_at(RHS + i, 0)[0]
        own, at = (fields, (RHS + i) * 64), (RHS + i) * 12
        fill(ec, i * NARROW, False, own, (xprev, xnext), start, 3, (yprev, ynext), start, 3, at)
        own, at = (slabs, i * 64), (RHS + 4 + i) * 12
        fill(es, i * NARROW, False, own, (sprev, snext), i * 32, 4, (eprev, enext), ALL * 12 + i * 24, 3, at)

    for x in range(16):
        for tile in range(2):
            at = x * 16 + tile * 8
            outer, inner = es[at : at + 8, :], es[2 * NARROW + at : 2 * NARROW + at + 8, :]
            pair = (jnp.where(lane8 < 4, outer, inner), jnp.where(lane8 < 4, inner, outer))
            for base, value in zip((LOW, HIGH), pair):
                for offset in ((8, 24), (16, 0))[tile]:
                    ea[base + x * 32 + offset : base + x * 32 + offset + 8, :] = value

    def weights(a, vs, ok):
        sixth = ok * F32(1 / 6)
        out = [(a - 1.0) * sixth]
        for v in vs:
            out += [(0.5 * v - 1.0) * sixth, (-0.5 * v - 1.0) * sixth]
        return out

    def make(i, carry):
        done = []
        for u in range(MAKES):
            x = 1 + i * MAKES + u
            okx = jnp.where(x < 4, xm, jnp.where(x >= 12, xp, F32(1)))
            for tile in range(2):
                at = x * 16 + tile * 8
                ok = okx * (jnp.where(row < 4, yp, ym) if tile else jnp.ones((8, 128), F32))
                cs = [ec[pl.ds(i * NARROW + at, 8), :] for i in range(4)]
                done.append((main, at, weights(cs[0], cs[1:], ok)))
                outer, inner = es[pl.ds(NARROW + at, 8), :], es[pl.ds(3 * NARROW + at, 8), :]
                for k, (pick, okz) in enumerate(((lane8 < 4, zm), (lane8 >= 4, zp))):
                    narrow = jnp.where(pick, outer, inner)
                    cs = [jnp.take_along_axis(narrow, lane8 + 8 * i, axis=1) for i in range(4)]
                    values = weights(cs[0], cs[1:], ok * jnp.where(pick, okz, F32(1)))
                    done.append((side, k * 7 * NARROW + at, values))
        for dst, at, values in done:
            for i in range(7):
                dst[pl.ds(i * NARROW + at, 8), :] = values[i]
        return carry

    lax.fori_loop(0, 14 // MAKES, make, 0)

    for s in range(1, STEPS + 1):
        src, dst = (ea, eb) if s % 2 else (eb, ea)
        last = s == STEPS

        tiles = [(x, 0) for x in range(s, 16 - s)]
        if not last:
            tiles += [(x, 1) for x in range(s + 1, 15 - s)]
        for x, tile in tiles:
            at = x * 32 + 8 + tile * 8
            both = jnp.where(lane8 == 4, src[HIGH + at : HIGH + at + 8, :], src[LOW + at : LOW + at + 8, :])
            for r in range(RHS):
                to = r * NARROW + x * 16 + tile * 8
                turn[to : to + 8, :] = rolled(both, -(8 * r + 4))

        def step(x, tile, keep, s=s, src=src, dst=dst, last=last):
            at = x * 32 + 8 + tile * 8
            small = x * 16 + tile * 8

            def apply(c, base, v, zplus, zminus):
                out = c[0] * v
                out = out + c[1] * src[pl.ds(base + at + 32, 8), :]
                out = out + c[2] * src[pl.ds(base + at - 32, 8), :]
                out = out + c[3] * src[pl.ds(base + at + 1, 8), :]
                out = out + c[4] * src[pl.ds(base + at - 1, 8), :]
                out = out + c[5] * zplus
                return out + c[6] * zminus

            def put(base, out):
                for offset in ((8, 24), (16, 0))[tile]:
                    dst[pl.ds(base + x * 32 + offset, 8), :] = out

            cs = [main[pl.ds(i * NARROW + small, 8), :] for i in range(7)]
            for r in range(RHS):
                v = src[pl.ds(r * WIDE + at, 8), :]
                over = turn[pl.ds(r * NARROW + small, 8), :]
                zplus = rolled(jnp.where(lane == 0, over, v), -1)
                zminus = rolled(jnp.where(lane == 127, over, v), 1)
                out = apply(cs, r * WIDE, v, zplus, zminus)
                if keep:
                    basis[pl.ds((x - 4) * 8 * COLS + s * RHS + r, 8, stride=COLS), :] = out
                if not last:
                    put(r * WIDE, out)
            if not last:
                for k, base in enumerate((LOW, HIGH)):
                    cs = [side[pl.ds((k * 7 + i) * NARROW + small, 8), :] for i in range(7)]
                    v = src[pl.ds(base + at, 8), :]
                    put(base, apply(cs, base, v, rolled(v, -1), rolled(v, 1)))

        def inside(i, carry, step=step):
            for u in range(OWN):
                step(4 + i * OWN + u, 0, True)
            return carry

        def outside(i, carry, s=s, step=step):
            for u in range(4 - s):
                step(s + i * (12 - s) + u, 0, False)
            return carry

        def halo(i, carry, s=s, step=step):
            for u in range(7 - s):
                step(s + 1 + i * (7 - s) + u, 1, False)
            return carry

        lax.fori_loop(0, 8 // OWN, inside, 0)
        if not last:
            lax.fori_loop(0, 2, outside, 0)
            lax.fori_loop(0, 2, halo, 0)

    zeros = jnp.zeros((128 - COLS, 256), BF16)

    def product(i, acc):
        for u in range(GRAMS):
            base = pl.multiple_of((i * GRAMS + u) * 2 * COLS, 2 * COLS)
            value = jnp.concatenate([basis[pl.ds(base, COLS), :], basis[pl.ds(base + COLS, COLS), :]], axis=1)
            high = value.astype(BF16)
            low = (value - high.astype(F32)).astype(BF16)
            acc = acc + lax.dot_general(
                wide([high, low]),
                wide([high, zeros, low, zeros]),
                (((1,), (1,)), ((), ())),
                preferred_element_type=F32,
            )
        return acc

    acc = lax.fori_loop(0, 32 // GRAMS, product, jnp.zeros((2 * COLS, 256), F32))
    gram = (acc[:COLS, :128] + acc[COLS:, 128:]) + (acc[:COLS, 128:] + acc[COLS:, :128])
    part = [gram[i * RHS : (i + 1) * RHS] for i in range(STEPS + 1)]
    lane = lax.broadcasted_iota(jnp.int32, (RHS, 128), 1)
    packed[:RHS, :] = jnp.where(
        lane < 80, part[0], jnp.where(lane < 112, rolled(part[3], 32), rolled(part[4], 48))
    )
    packed[RHS:, :] = jnp.where(
        lane < 64, rolled(part[1], -16), jnp.where(lane < 112, rolled(part[2], 32), 0.0)
    )


def solve_combine(parts, basis, solution_field, residual):
    total = parts[0]
    for i in range(1, parts.shape[0]):
        total = total + parts[i]
    first, second = total[:RHS], total[RHS:]
    lane = lax.broadcasted_iota(jnp.int32, (RHS, 128), 1)

    def span(value, start):
        return jnp.where((lane >= start) & (lane < COLS), value, 0.0)

    upper = [
        span(first, 0),
        span(rolled(second, 16), 16),
        span(rolled(second, -32), 32),
        span(rolled(first, -32), 48),
        span(rolled(first, -48), 64),
    ]
    flipped = jnp.transpose(wide(upper + [jnp.zeros((128 - COLS, 128), F32)]))
    gram = wide(
        [
            jnp.where(lane < i * RHS, flipped[i * RHS : (i + 1) * RHS], upper[i])
            for i in range(STEPS + 1)
        ]
    )
    half = 7.0 * gram + 6.0 * rolled(gram, -RHS)
    half = jnp.where(lax.broadcasted_iota(jnp.int32, (COLS, 128), 1) < KEEP, half, 0.0)
    normal = 7.0 * half[:KEEP] + 6.0 * half[RHS:]
    m = [normal[i * 8 : i * 8 + 8] for i in range(8)] + [half[:8], half[8:RHS]]
    lane = lanes()
    for k in range(0, KEEP, BLOCK):
        i0, s = divmod(k, 8)
        inside = (lane >= k) & (lane < k + BLOCK)
        keep = list(range(i0 + 1 if s + BLOCK == 8 else i0, 10))
        columns = {
            i: [jnp.broadcast_to(m[i][:, k + c : k + c + 1], (8, 128)) for c in range(BLOCK)]
            for i in sorted({i0, *keep})
        }

        def spread(value, c, s=s):
            return jnp.broadcast_to(value[s + c : s + c + 1, :], (8, 128))

        pivots = [[spread(columns[i0][c], d) for c in range(BLOCK)] for d in range(BLOCK)]
        rows = [
            jnp.where(lane == k + d, -1.0, jnp.where(inside, 0.0, spread(m[i0], d))) for d in range(BLOCK)
        ]
        for d in range(BLOCK):
            inverse = 1.0 / pivots[d][d]
            for c in range(d + 1, BLOCK):
                pivots[d][c] = pivots[d][c] * inverse
            rows[d] = rows[d] * inverse
            for e in range(BLOCK):
                if e != d:
                    for c in range(d + 1, BLOCK):
                        pivots[e][c] = pivots[e][c] - pivots[e][d] * pivots[d][c]
                    rows[e] = rows[e] - pivots[e][d] * rows[d]
        for i in keep:
            value = jnp.where(inside, 0.0, m[i])
            for c in range(BLOCK):
                value = value - columns[i][c] * rows[c]
            m[i] = value
    coef = wide(m[8:])
    mixed = 7.0 * coef + 6.0 * rolled(coef, RHS)
    both = wide([coef, mixed])
    high = both.astype(BF16).astype(F32)
    mid = (both - high).astype(BF16).astype(F32)
    low = both - high - mid
    lane = lax.broadcasted_iota(jnp.int32, (2 * RHS, 128), 1)

    def tripled(value, parts):
        left = value if parts == 1 else jnp.where(lane < 80, value, rolled(value, 80))
        right = jnp.where(lane < 32, rolled(value, -48), 0.0) if parts > 1 else jnp.zeros_like(value)
        if parts == 3:
            right = jnp.where((lane >= 32) & (lane < 112), rolled(value, 32), right)
        return jnp.concatenate([left, right], axis=1)

    factors = wide([tripled(high, 3), tripled(mid, 2), tripled(low, 1)[RHS:]]).astype(BF16)
    zeros = jnp.zeros((16, 256), BF16)

    def combine(i, carry):
        done = []
        for u in range(PAIRS):
            base = pl.multiple_of((i * PAIRS + u) * 2 * COLS, 2 * COLS)
            value = jnp.concatenate([basis[pl.ds(base, COLS), :], basis[pl.ds(base + COLS, COLS), :]], axis=1)
            high = value.astype(BF16)
            rest = value - high.astype(F32)
            mid = rest.astype(BF16)
            low = (rest - mid.astype(F32)).astype(BF16)
            out = jnp.dot(factors, wide([high, mid, low, zeros]), preferred_element_type=F32)
            mixed = out[RHS : 2 * RHS] + (out[3 * RHS : 4 * RHS] + out[4 * RHS :])
            done.append((out[:RHS] + out[2 * RHS : 3 * RHS], value[:RHS] - mixed))
        for u in range(PAIRS):
            for c in range(2):
                at = pl.ds(2 * (i * PAIRS + u) + c, RHS, stride=64)
                solution_field[at, :] = done[u][0][:, c * 128 : (c + 1) * 128]
                residual[at, :] = done[u][1][:, c * 128 : (c + 1) * 128]
        return carry

    lax.fori_loop(0, 32 // PAIRS, combine, 0)


def call(kernel, ins, outs, scratch=(), smem=False):
    vmem = pl.BlockSpec(memory_space=pltpu.VMEM)
    specs = [vmem] * len(ins)
    if smem:
        specs[0] = pl.BlockSpec(memory_space=pltpu.SMEM)
    return pl.pallas_call(
        kernel,
        out_shape=[jax.ShapeDtypeStruct(s, F32) for s in outs],
        in_specs=specs,
        out_specs=[vmem] * len(outs),
        scratch_shapes=[pltpu.VMEM(s, F32) for s in scratch],
        compiler_params=pltpu.CompilerParams(vmem_limit_bytes=LIMIT),
    )(*ins)


def shift(value, axis, by):
    count = lax.axis_size(axis)
    return lax.ppermute(value, axis, [(i, (i + by) % count) for i in range(count)])


def gathered(value, axis):
    count = lax.axis_size(axis)
    return lax.all_to_all(jnp.broadcast_to(value[None], (count,) + value.shape), axis, 0, 0)


def shards(right_side, absorption, velocity):
    axes = ("gx", "gy", ("zx", "core"))
    ends = []
    for axis in axes:
        at = lax.axis_index(axis)
        ends += [at > 0, at < lax.axis_size(axis) - 1]
    flags = jnp.stack(ends).astype(F32)
    fields = jnp.concatenate([right_side, absorption[None], velocity], axis=0).reshape((RHS + 4) * 64, 128)
    face = (RHS * 32 + 4 * 24, 128)
    ends_z, xlow, xhigh, ylow, yhigh = call(pack_own, [fields], [(128, 128), face, face, face, face])
    xprev = shift(xhigh, "gx", 1)
    xnext = shift(xlow, "gx", -1)
    zprev = shift(ends_z, axes[2], 1)
    znext = shift(ends_z, axes[2], -1)
    yprev = shift(yhigh, "gy", 1)
    ynext = shift(ylow, "gy", -1)
    slabs, slow, shigh = call(
        pack_ends, [flags, ends_z, zprev, znext], [(256, 128), (128, 128), (128, 128)], smem=True
    )
    sprev = shift(shigh, "gx", 1)
    snext = shift(slow, "gx", -1)
    edge = (ALL * 12 + 4 * 24, 128)
    elow, ehigh = call(pack_edges, [slabs, xprev, xnext, sprev, snext], [edge, edge])
    eprev = shift(ehigh, "gy", 1)
    enext = shift(elow, "gy", -1)
    basis, packed = call(
        steps_gram,
        [flags, fields, slabs, xprev, xnext, sprev, snext, yprev, ynext, eprev, enext],
        [(64 * COLS, 128), (2 * RHS, 128)],
        [(18 * WIDE, 128)] * 2 + [(n * NARROW, 128) for n in (4, 4, 7, 14, RHS)],
        smem=True,
    )
    packed = packed + shift(packed, "core", 1)
    packed = gathered(packed, ("gx", "zx")).sum(0)
    parts = gathered(packed, "gy")
    solution_field, residual = call(solve_combine, [parts, basis], [(1024, 128), (1024, 128)])
    return solution_field.reshape(right_side.shape), residual.reshape(right_side.shape)


def solution(mesh):
    nx, ny, nz = mesh.devices.shape
    split = Mesh(mesh.devices.reshape(nx, ny, nz // 2, 2), ("gx", "gy", "zx", "core"))
    z = ("zx", "core")
    return jax.shard_map(
        shards,
        mesh=split,
        in_specs=(P(None, "gx", "gy", z), P("gx", "gy", z), P(None, "gx", "gy", z)),
        out_specs=(P(None, "gx", "gy", z), P(None, "gx", "gy", z)),
        check_vma=False,
    )
```

```python
import jax
import jax.numpy as jnp
from jax import lax
from jax.experimental import pallas as pl
from jax.experimental.pallas import tpu as pltpu
from jax.sharding import Mesh, PartitionSpec as P

RHS = 16
STEPS = 4
COLS = RHS * (STEPS + 1)
KEEP = RHS * STEPS
ALL = RHS + 8
FILLS = 4
MAKES = 7
OWN = 8
GRAMS = 16
PAIRS = 8
BLOCK = 4
LOW = RHS * 512
HIGH = LOW + 512
LIMIT = 28 * 1024 * 1024
F32 = jnp.float32
BF16 = jnp.bfloat16


def lanes():
    return lax.broadcasted_iota(jnp.int32, (8, 128), 1)


def rolled(x, amount):
    amount = amount % x.shape[-1]
    return x if amount == 0 else pltpu.roll(x, amount, x.ndim - 1)


def wide(pieces):
    return jnp.concatenate(pieces, axis=0)


def face_at(f, side):
    count = 4 if f < RHS else 3
    start = f * 32 if f < RHS else RHS * 32 + (f - RHS) * 24
    return start, count, (0 if side == 0 else 8 - count)


def pack_own(own, ends, xlow, xhigh, ylow, yhigh):
    group = lanes() // 8
    for x in range(8):
        tiles = [own[f * 64 + x * 8 : f * 64 + x * 8 + 8, :] for f in range(RHS + 4)]
        for part, at in ((tiles[:RHS], 0), (tiles[RHS:], 64)):
            acc = rolled(part[0], 4)
            for i in range(1, len(part)):
                acc = jnp.where(group == i, rolled(part[i], 8 * i + 4), acc)
            ends[at + x * 8 : at + x * 8 + 8, :] = acc
        for f, tile in enumerate(tiles):
            for side, (xout, yout) in enumerate(((xlow, ylow), (xhigh, yhigh))):
                start, count, first = face_at(f, side)
                if first <= x < first + count:
                    xout[start + (x - first) * 8 : start + (x - first) * 8 + 8, :] = tile
                yout[start + x * count : start + x * count + count, :] = tile[first : first + count]


def pack_ends(flags, ends, zprev, znext, slabs, xlow, xhigh):
    low = lanes() % 8 < 4
    zm, zp = flags[4], flags[5]
    for j in range(4):
        for x in range(8):
            at = slice((j % 2) * 64 + x * 8, (j % 2) * 64 + x * 8 + 8)
            if j == 0:
                tile = jnp.where(low, zprev[at, :] * zm, znext[at, :] * zp)
            elif j == 1:
                tile = jnp.where(low, zprev[at, :], znext[at, :])
            else:
                tile = ends[at, :]
            slabs[j * 64 + x * 8 : j * 64 + x * 8 + 8, :] = tile
            xout = xlow if x < 4 else xhigh
            xout[j * 32 + x % 4 * 8 : j * 32 + x % 4 * 8 + 8, :] = tile


EDGES = ((-1, 3, 0), (8, 3, 3), (-2, 2, 6), (9, 2, 8), (-3, 1, 10), (10, 1, 11))


def pack_edges(slabs, xprev, xnext, sprev, snext, ylow, yhigh):
    def put(f, prev, nxt, before, after):
        for x, rows, at in EDGES:
            tile = prev[pl.ds(before + x * 8, 8), :] if x < 0 else nxt[pl.ds(after + (x - 8) * 8, 8), :]
            ylow[pl.ds(f * 12 + at, rows), :] = tile[:rows]
            yhigh[pl.ds(f * 12 + at, rows), :] = tile[8 - rows :]

    def body(f, carry):
        put(f, xprev, xnext, f * 32 + 32, f * 32)
        return carry

    lax.fori_loop(0, RHS, body, 0)
    for i in range(4):
        start = face_at(RHS + i, 0)[0]
        put(RHS + i, xprev, xnext, start + 24, start)
        put(RHS + 4 + i, sprev, snext, i * 32 + 32, i * 32)
        for x in range(8):
            tile = slabs[i * 64 + x * 8 : i * 64 + x * 8 + 8, :]
            ylow[ALL * 12 + i * 24 + x * 3 : ALL * 12 + i * 24 + x * 3 + 3, :] = tile[:3]
            yhigh[ALL * 12 + i * 24 + x * 3 : ALL * 12 + i * 24 + x * 3 + 3, :] = tile[5:]


WIDE = 512
NARROW = 256


def steps_gram(
    flags, fields, slabs, xprev, xnext, sprev, snext, yprev, ynext, eprev, enext,
    basis, packed, ea, eb, es, ec, main, side, turn,
):
    lane = lanes()
    lane8 = lane % 8
    row = lax.broadcasted_iota(jnp.int32, (8, 128), 0)
    xm, xp, ym, yp, zm, zp = [flags[i] for i in range(6)]

    def fill(dst, base, wide_field, own, xs, start, count, ys, ystart, ycount, edge_at):
        size = 32 if wide_field else 16
        own_at, halo_at = ((8, 24), (16, 0)) if wide_field else ((0,), (8,))
        todo = []
        for x in range(8):
            todo.append((own_at, x + 4, 0, own[0][pl.ds(own[1] + x * 8, 8), :]))
            todo.append((halo_at, x + 4, 8 - ycount, ys[0][pl.ds(ystart + x * ycount, ycount), :] * ym))
            todo.append((halo_at, x + 4, 0, ys[1][pl.ds(ystart + x * ycount, ycount), :] * yp))
        for i in range(count):
            todo.append((own_at, 4 - count + i, 0, xs[0][pl.ds(start + i * 8, 8), :] * xm))
            todo.append((own_at, 12 + i, 0, xs[1][pl.ds(start + i * 8, 8), :] * xp))
        for x, rows, at in EDGES:
            m = xm if x < 0 else xp
            todo.append((halo_at, x + 4, 8 - rows, eprev[pl.ds(edge_at + at, rows), :] * (m * ym)))
            todo.append((halo_at, x + 4, 0, enext[pl.ds(edge_at + at, rows), :] * (m * yp)))
        for offsets, x, at, value in todo:
            for offset in offsets:
                dst[pl.ds(base + x * size + offset + at, value.shape[0]), :] = value

    def fill_rhs(i, carry):
        for u in range(FILLS):
            r = i * FILLS + u
            fill(ea, r * WIDE, True, (fields, r * 64), (xprev, xnext), r * 32, 4, (yprev, ynext), r * 32, 4, r * 12)
        values = [fields[pl.ds((i * FILLS + u) * 64 + x * 8, 8), :] for u in range(FILLS) for x in range(8)]
        for u in range(FILLS):
            for x in range(8):
                basis[pl.ds(x * 8 * COLS + i * FILLS + u, 8, stride=COLS), :] = values[u * 8 + x]
        return carry

    lax.fori_loop(0, RHS // FILLS, fill_rhs, 0)
    for i in range(4):
        start = face_at(RHS + i, 0)[0]
        own, at = (fields, (RHS + i) * 64), (RHS + i) * 12
        fill(ec, i * NARROW, False, own, (xprev, xnext), start, 3, (yprev, ynext), start, 3, at)
        own, at = (slabs, i * 64), (RHS + 4 + i) * 12
        fill(es, i * NARROW, False, own, (sprev, snext), i * 32, 4, (eprev, enext), ALL * 12 + i * 24, 3, at)

    for x in range(16):
        for tile in range(2):
            at = x * 16 + tile * 8
            outer, inner = es[at : at + 8, :], es[2 * NARROW + at : 2 * NARROW + at + 8, :]
            pair = (jnp.where(lane8 < 4, outer, inner), jnp.where(lane8 < 4, inner, outer))
            for base, value in zip((LOW, HIGH), pair):
                for offset in ((8, 24), (16, 0))[tile]:
                    ea[base + x * 32 + offset : base + x * 32 + offset + 8, :] = value

    def weights(a, vs, ok):
        sixth = ok * F32(1 / 6)
        out = [(a - 1.0) * sixth]
        for v in vs:
            out += [(0.5 * v - 1.0) * sixth, (-0.5 * v - 1.0) * sixth]
        return out

    def make(i, carry):
        done = []
        for u in range(MAKES):
            x = 1 + i * MAKES + u
            okx = jnp.where(x < 4, xm, jnp.where(x >= 12, xp, F32(1)))
            for tile in range(2):
                at = x * 16 + tile * 8
                ok = okx * (jnp.where(row < 4, yp, ym) if tile else jnp.ones((8, 128), F32))
                cs = [ec[pl.ds(i * NARROW + at, 8), :] for i in range(4)]
                done.append((main, at, weights(cs[0], cs[1:], ok)))
                outer, inner = es[pl.ds(NARROW + at, 8), :], es[pl.ds(3 * NARROW + at, 8), :]
                for k, (pick, okz) in enumerate(((lane8 < 4, zm), (lane8 >= 4, zp))):
                    narrow = jnp.where(pick, outer, inner)
                    cs = [jnp.take_along_axis(narrow, lane8 + 8 * i, axis=1) for i in range(4)]
                    values = weights(cs[0], cs[1:], ok * jnp.where(pick, okz, F32(1)))
                    done.append((side, k * 7 * NARROW + at, values))
        for dst, at, values in done:
            for i in range(7):
                dst[pl.ds(i * NARROW + at, 8), :] = values[i]
        return carry

    lax.fori_loop(0, 14 // MAKES, make, 0)

    for s in range(1, STEPS + 1):
        src, dst = (ea, eb) if s % 2 else (eb, ea)
        last = s == STEPS

        tiles = [(x, 0) for x in range(s, 16 - s)]
        if not last:
            tiles += [(x, 1) for x in range(s + 1, 15 - s)]
        for x, tile in tiles:
            at = x * 32 + 8 + tile * 8
            both = jnp.where(lane8 == 4, src[HIGH + at : HIGH + at + 8, :], src[LOW + at : LOW + at + 8, :])
            for r in range(RHS):
                to = r * NARROW + x * 16 + tile * 8
                turn[to : to + 8, :] = rolled(both, -(8 * r + 4))

        def step(x, tile, keep, s=s, src=src, dst=dst, last=last):
            at = x * 32 + 8 + tile * 8
            small = x * 16 + tile * 8

            def apply(c, base, v, zplus, zminus):
                out = c[0] * v
                out = out + c[1] * src[pl.ds(base + at + 32, 8), :]
                out = out + c[2] * src[pl.ds(base + at - 32, 8), :]
                out = out + c[3] * src[pl.ds(base + at + 1, 8), :]
                out = out + c[4] * src[pl.ds(base + at - 1, 8), :]
                out = out + c[5] * zplus
                return out + c[6] * zminus

            def put(base, out):
                for offset in ((8, 24), (16, 0))[tile]:
                    dst[pl.ds(base + x * 32 + offset, 8), :] = out

            cs = [main[pl.ds(i * NARROW + small, 8), :] for i in range(7)]
            for r in range(RHS):
                v = src[pl.ds(r * WIDE + at, 8), :]
                over = turn[pl.ds(r * NARROW + small, 8), :]
                zplus = rolled(jnp.where(lane == 0, over, v), -1)
                zminus = rolled(jnp.where(lane == 127, over, v), 1)
                out = apply(cs, r * WIDE, v, zplus, zminus)
                if keep:
                    basis[pl.ds((x - 4) * 8 * COLS + s * RHS + r, 8, stride=COLS), :] = out
                if not last:
                    put(r * WIDE, out)
            if not last:
                for k, base in enumerate((LOW, HIGH)):
                    cs = [side[pl.ds((k * 7 + i) * NARROW + small, 8), :] for i in range(7)]
                    v = src[pl.ds(base + at, 8), :]
                    put(base, apply(cs, base, v, rolled(v, -1), rolled(v, 1)))

        def inside(i, carry, step=step):
            for u in range(OWN):
                step(4 + i * OWN + u, 0, True)
            return carry

        def outside(i, carry, s=s, step=step):
            for u in range(4 - s):
                step(s + i * (12 - s) + u, 0, False)
            return carry

        def halo(i, carry, s=s, step=step):
            for u in range(7 - s):
                step(s + 1 + i * (7 - s) + u, 1, False)
            return carry

        lax.fori_loop(0, 8 // OWN, inside, 0)
        if not last:
            lax.fori_loop(0, 2, outside, 0)
            lax.fori_loop(0, 2, halo, 0)

    zeros = jnp.zeros((128 - COLS, 256), BF16)

    def product(i, acc):
        for u in range(GRAMS):
            base = pl.multiple_of((i * GRAMS + u) * 2 * COLS, 2 * COLS)
            value = jnp.concatenate([basis[pl.ds(base, COLS), :], basis[pl.ds(base + COLS, COLS), :]], axis=1)
            high = value.astype(BF16)
            low = (value - high.astype(F32)).astype(BF16)
            acc = acc + lax.dot_general(
                wide([high, low]),
                wide([high, zeros, low, zeros]),
                (((1,), (1,)), ((), ())),
                preferred_element_type=F32,
            )
        return acc

    acc = lax.fori_loop(0, 32 // GRAMS, product, jnp.zeros((2 * COLS, 256), F32))
    gram = (acc[:COLS, :128] + acc[COLS:, 128:]) + (acc[:COLS, 128:] + acc[COLS:, :128])
    part = [gram[i * RHS : (i + 1) * RHS] for i in range(STEPS + 1)]
    lane = lax.broadcasted_iota(jnp.int32, (RHS, 128), 1)
    packed[:RHS, :] = jnp.where(
        lane < 80, part[0], jnp.where(lane < 112, rolled(part[3], 32), rolled(part[4], 48))
    )
    packed[RHS:, :] = jnp.where(
        lane < 64, rolled(part[1], -16), jnp.where(lane < 112, rolled(part[2], 32), 0.0)
    )


def solved(p, right):
    (a, b), (c, d) = p[0][:2], p[1][:2]
    scale = 1.0 / (a * d - b * c)
    inverse = ((d * scale, -(b * scale)), (-(c * scale), a * scale))
    return [[i[0] * u + i[1] * v for u, v in zip(*right)] for i in inverse]


def solve_combine(parts, basis, solution_field, residual, held, sems):
    total = parts[0]
    for i in range(1, parts.shape[0]):
        total = total + parts[i]
    first, second = total[:RHS], total[RHS:]
    lane = lax.broadcasted_iota(jnp.int32, (RHS, 128), 1)

    def span(value, start):
        return jnp.where((lane >= start) & (lane < COLS), value, 0.0)

    upper = [
        span(first, 0),
        span(rolled(second, 16), 16),
        span(rolled(second, -32), 32),
        span(rolled(first, -32), 48),
        span(rolled(first, -48), 64),
    ]
    flipped = jnp.transpose(wide(upper + [jnp.zeros((128 - COLS, 128), F32)]))
    gram = wide(
        [
            jnp.where(lane < i * RHS, flipped[i * RHS : (i + 1) * RHS], upper[i])
            for i in range(STEPS + 1)
        ]
    )
    half = 7.0 * gram + 6.0 * rolled(gram, -RHS)
    half = jnp.where(lax.broadcasted_iota(jnp.int32, (COLS, 128), 1) < KEEP, half, 0.0)
    normal = 7.0 * half[:KEEP] + 6.0 * half[RHS:]
    m = [normal[i * 8 : i * 8 + 8] for i in range(8)] + [half[:8], half[8:RHS]]
    lane = lanes()

    def column(i, c):
        return jnp.broadcast_to(m[i][:, c : c + 1], (8, 128))

    def row(value, r):
        return jnp.broadcast_to(value[r : r + 1, :], (8, 128))

    def square(r, c):
        columns = [column(r // 8, c + j) for j in range(BLOCK)]
        return [[row(columns[j], r % 8 + i) for j in range(BLOCK)] for i in range(BLOCK)]

    pivots = square(0, 0)
    for k in range(0, KEEP, BLOCK):
        i0, s = divmod(k, 8)
        inside = (lane >= k) & (lane < k + BLOCK)
        keep = list(range(i0 + 1 if s + BLOCK == 8 else i0, 10))
        columns = {i: [column(i, k + c) for c in range(BLOCK)] for i in keep}
        rows = [
            jnp.where(lane == k + d, -1.0, jnp.where(inside, 0.0, row(m[i0], s + d))) for d in range(BLOCK)
        ]
        more = k + BLOCK < KEEP
        if more:
            across, after = square(k, k + BLOCK), square(k + BLOCK, k + BLOCK)
            rights = [across[d] + [rows[d]] for d in range(BLOCK)]
        else:
            rights = [[rows[d]] for d in range(BLOCK)]
        upper = solved(pivots[:2], [pivots[d][2:] + rights[d] for d in (0, 1)])
        rest = [
            [u - (pivots[e][0] * v + pivots[e][1] * w) for u, v, w in zip(pivots[e][2:] + rights[e], *upper)]
            for e in (2, 3)
        ]
        lower = solved(rest, [r[2:] for r in rest])
        upper = [
            [u - (upper[d][0] * v + upper[d][1] * w) for u, v, w in zip(upper[d][2:], *lower)] for d in (0, 1)
        ]
        result = upper + lower
        if more:
            pivots = [
                [
                    after[d][c] - (
                        (across[0][d] * result[0][c] + across[1][d] * result[1][c])
                        + (across[2][d] * result[2][c] + across[3][d] * result[3][c])
                    )
                    for c in range(BLOCK)
                ]
                for d in range(BLOCK)
            ]
        for i in keep:
            value = jnp.where(inside, 0.0, m[i])
            for c in range(BLOCK):
                value = value - columns[i][c] * result[c][-1]
            m[i] = value
    coef = wide(m[8:])
    mixed = 7.0 * coef + 6.0 * rolled(coef, RHS)
    both = wide([coef, mixed])
    high = both.astype(BF16).astype(F32)
    mid = (both - high).astype(BF16).astype(F32)
    low = both - high - mid
    lane = lax.broadcasted_iota(jnp.int32, (2 * RHS, 128), 1)

    def tripled(value, parts):
        left = value if parts == 1 else jnp.where(lane < 80, value, rolled(value, 80))
        right = jnp.where(lane < 32, rolled(value, -48), 0.0) if parts > 1 else jnp.zeros_like(value)
        if parts == 3:
            right = jnp.where((lane >= 32) & (lane < 112), rolled(value, 32), right)
        return jnp.concatenate([left, right], axis=1)

    factors = wide([tripled(high, 3), tripled(mid, 2), tripled(low, 1)[RHS:]]).astype(BF16)
    zeros = jnp.zeros((16, 256), BF16)

    def combine(i, carry):
        done = []
        for u in range(PAIRS):
            base = pl.multiple_of((i * PAIRS + u) * 2 * COLS, 2 * COLS)
            value = jnp.concatenate([basis[pl.ds(base, COLS), :], basis[pl.ds(base + COLS, COLS), :]], axis=1)
            high = value.astype(BF16)
            rest = value - high.astype(F32)
            mid = rest.astype(BF16)
            low = (rest - mid.astype(F32)).astype(BF16)
            out = jnp.dot(factors, wide([high, mid, low, zeros]), preferred_element_type=F32)
            mixed = out[RHS : 2 * RHS] + (out[3 * RHS : 4 * RHS] + out[4 * RHS :])
            done.append((out[:RHS] + out[2 * RHS : 3 * RHS], value[:RHS] - mixed))
        for u in range(PAIRS):
            for c in range(2):
                at = 2 * (i * PAIRS + u) + c
                held[pl.ds(at, RHS, stride=64), :] = done[u][0][:, c * 128 : (c + 1) * 128]
                held[pl.ds(1024 + at, RHS, stride=64), :] = done[u][1][:, c * 128 : (c + 1) * 128]
        return carry

    count = 32 // PAIRS
    copies = []
    for i in range(count):
        combine(i, 0)
        rows = pl.ds(i * 2 * PAIRS, 2 * PAIRS)
        for k, out in enumerate((solution_field, residual)):
            src = held.reshape(2, RHS, 64, 128).at[k, :, rows, :]
            copies.append(pltpu.make_async_copy(src, out.at[:, rows, :], sems.at[i * 2 + k]))
            copies[-1].start()
    for copy in copies:
        copy.wait()


def call(kernel, ins, outs, scratch=(), smem=False, hbm=False):
    vmem = pl.BlockSpec(memory_space=pltpu.VMEM)
    specs = [vmem] * len(ins)
    if smem:
        specs[0] = pl.BlockSpec(memory_space=pltpu.SMEM)
    return pl.pallas_call(
        kernel,
        out_shape=[jax.ShapeDtypeStruct(s, F32) for s in outs],
        in_specs=specs,
        out_specs=[pl.BlockSpec(memory_space=pl.ANY) if hbm else vmem] * len(outs),
        scratch_shapes=[pltpu.VMEM(s, F32) if isinstance(s, tuple) else s for s in scratch],
        compiler_params=pltpu.CompilerParams(vmem_limit_bytes=LIMIT),
    )(*ins)


def shift(value, axis, by):
    count = lax.axis_size(axis)
    return lax.ppermute(value, axis, [(i, (i + by) % count) for i in range(count)])


def gathered(value, axis):
    count = lax.axis_size(axis)
    return lax.all_to_all(jnp.broadcast_to(value[None], (count,) + value.shape), axis, 0, 0)


def shards(right_side, absorption, velocity):
    axes = ("gx", "gy", ("zx", "core"))
    ends = []
    for axis in axes:
        at = lax.axis_index(axis)
        ends += [at > 0, at < lax.axis_size(axis) - 1]
    flags = jnp.stack(ends).astype(F32)
    fields = jnp.concatenate([right_side, absorption[None], velocity], axis=0).reshape((RHS + 4) * 64, 128)
    face = (RHS * 32 + 4 * 24, 128)
    ends_z, xlow, xhigh, ylow, yhigh = call(pack_own, [fields], [(128, 128), face, face, face, face])
    xprev = shift(xhigh, "gx", 1)
    xnext = shift(xlow, "gx", -1)
    zprev = shift(ends_z, axes[2], 1)
    znext = shift(ends_z, axes[2], -1)
    yprev = shift(yhigh, "gy", 1)
    ynext = shift(ylow, "gy", -1)
    slabs, slow, shigh = call(
        pack_ends, [flags, ends_z, zprev, znext], [(256, 128), (128, 128), (128, 128)], smem=True
    )
    sprev = shift(shigh, "gx", 1)
    snext = shift(slow, "gx", -1)
    edge = (ALL * 12 + 4 * 24, 128)
    elow, ehigh = call(pack_edges, [slabs, xprev, xnext, sprev, snext], [edge, edge])
    eprev = shift(ehigh, "gy", 1)
    enext = shift(elow, "gy", -1)
    basis, packed = call(
        steps_gram,
        [flags, fields, slabs, xprev, xnext, sprev, snext, yprev, ynext, eprev, enext],
        [(64 * COLS, 128), (2 * RHS, 128)],
        [(18 * WIDE, 128)] * 2 + [(n * NARROW, 128) for n in (4, 4, 7, 14, RHS)],
        smem=True,
    )
    packed = packed + shift(packed, "core", 1)
    packed = gathered(packed, ("gx", "zx")).sum(0)
    parts = gathered(packed, "gy")
    solution_field, residual = call(
        solve_combine,
        [parts, basis],
        [(RHS, 64, 128), (RHS, 64, 128)],
        [pltpu.VMEM((2048, 128), F32), pltpu.SemaphoreType.DMA((64 // PAIRS,))],
        hbm=True,
    )
    return solution_field.reshape(right_side.shape), residual.reshape(right_side.shape)


def solution(mesh):
    nx, ny, nz = mesh.devices.shape
    split = Mesh(mesh.devices.reshape(nx, ny, nz // 2, 2), ("gx", "gy", "zx", "core"))
    z = ("zx", "core")
    return jax.shard_map(
        shards,
        mesh=split,
        in_specs=(P(None, "gx", "gy", z), P("gx", "gy", z), P(None, "gx", "gy", z)),
        out_specs=(P(None, "gx", "gy", z), P(None, "gx", "gy", z)),
        check_vma=False,
    )
```

```python
import jax
import jax.numpy as jnp
from jax import lax
from jax.experimental import pallas as pl
from jax.experimental.pallas import tpu as pltpu
from jax.sharding import Mesh, PartitionSpec as P

RHS = 16
STEPS = 4
COLS = RHS * (STEPS + 1)
KEEP = RHS * STEPS
FILLS = 4
MAKES = 7
OWN = 8
GRAMS = 16
PAIRS = 8
BLOCK = 4
LOW = RHS * 512
HIGH = LOW + 512
LIMIT = 28 * 1024 * 1024
F32 = jnp.float32
BF16 = jnp.bfloat16


def lanes():
    return lax.broadcasted_iota(jnp.int32, (8, 128), 1)


def rolled(x, amount):
    amount = amount % x.shape[-1]
    return x if amount == 0 else pltpu.roll(x, amount, x.ndim - 1)


def wide(pieces):
    return jnp.concatenate(pieces, axis=0)


FACE_ROWS = RHS * 32 + 4 * 24


def face_at(f, side):
    count = 4 if f < RHS else 3
    start = f * 32 if f < RHS else RHS * 32 + (f - RHS) * 24
    return start, count, (0 if side == 0 else 8 - count)


def pack_own(own, ends, xlow, xhigh, ylow, yhigh):
    group = lanes() // 8
    for x in range(8):
        tiles = [own[f * 64 + x * 8 : f * 64 + x * 8 + 8, :] for f in range(RHS + 4)]
        for part, at in ((tiles[:RHS], 0), (tiles[RHS:], 64)):
            acc = rolled(part[0], 4)
            for i in range(1, len(part)):
                acc = jnp.where(group == i, rolled(part[i], 8 * i + 4), acc)
            ends[at + x * 8 : at + x * 8 + 8, :] = acc
        for f, tile in enumerate(tiles):
            for side, (xout, yout) in enumerate(((xlow, ylow), (xhigh, yhigh))):
                start, count, first = face_at(f, side)
                if first <= x < first + count:
                    xout[start + (x - first) * 8 : start + (x - first) * 8 + 8, :] = tile
                yout[start + x * count : start + x * count + count, :] = tile[first : first + count]


REACH = ((0, 3), (24, 2), (40, 2), (56, 1))


def pack_ends(flags, ends, zprev, znext, slabs, xlow, xhigh):
    low = lanes() % 8 < 4
    zm, zp = flags[4], flags[5]
    for j in range(4):
        for x in range(8):
            at = slice((j % 2) * 64 + x * 8, (j % 2) * 64 + x * 8 + 8)
            if j == 0:
                tile = jnp.where(low, zprev[at, :] * zm, znext[at, :] * zp)
            elif j == 1:
                tile = jnp.where(low, zprev[at, :], znext[at, :])
            else:
                tile = ends[at, :]
            slabs[j * 64 + x * 8 : j * 64 + x * 8 + 8, :] = tile
            start, count = REACH[j]
            for xout, first in ((xlow, 0), (xhigh, 8 - count)):
                if first <= x < first + count:
                    xout[start + (x - first) * 8 : start + (x - first) * 8 + 8, :] = tile


EDGES4 = ((-1, 3, 0), (8, 3, 3), (-2, 2, 6), (9, 2, 8), (-3, 1, 10), (10, 1, 11))
EDGES3 = ((-1, 2, 0), (8, 2, 2), (-2, 1, 4), (9, 1, 5))
EDGES2 = ((-1, 1, 0), (8, 1, 1))
COEF_AT = RHS * 12
ENDS_AT = ((COEF_AT + 24, EDGES3), (COEF_AT + 30, EDGES2), (COEF_AT + 32, EDGES2), (COEF_AT + 34, ()))
FACE_AT = (COEF_AT + 34, COEF_AT + 58, COEF_AT + 74, COEF_AT + 90)
EDGE_ROWS = 384


def pack_edges(slabs, xprev, xnext, sprev, snext, ylow, yhigh, kept):
    def put(table, to, prev, nxt, before, after):
        for x, rows, at in table:
            tile = prev[pl.ds(before + x * 8, 8), :] if x < 0 else nxt[pl.ds(after + (x - 8) * 8, 8), :]
            ylow[pl.ds(to + at, rows), :] = tile[:rows]
            yhigh[pl.ds(to + at, rows), :] = tile[8 - rows :]

    for r in range(RHS):
        put(EDGES4, r * 12, xprev, xnext, r * 32 + 32, r * 32)
    for i in range(4):
        start = face_at(RHS + i, 0)[0]
        put(EDGES3, COEF_AT + i * 6, xprev, xnext, start + 24, start)
        start, count = REACH[i]
        put(ENDS_AT[i][1], ENDS_AT[i][0], sprev, snext, start + count * 8, start)
        for x in range(8):
            tile = slabs[i * 64 + x * 8 : i * 64 + x * 8 + 8, :]
            at = FACE_AT[i] + x * count
            ylow[at : at + count, :] = tile[:count]
            yhigh[at : at + count, :] = tile[8 - count :]
    keep_faces(xprev, xnext, kept)


def keep_faces(prev, nxt, kept):
    kept[:FACE_ROWS, :] = prev[:, :]
    kept[FACE_ROWS:, :] = nxt[:, :]


WIDE = 512
NARROW = 256


def steps_gram(
    flags, fields, slabs, kept, sprev, snext, held, eprev, enext,
    basis, packed, ea, eb, es, ec, main, side, turn,
):
    lane = lanes()
    lane8 = lane % 8
    row = lax.broadcasted_iota(jnp.int32, (8, 128), 0)
    xm, xp, ym, yp, zm, zp = [flags[i] for i in range(6)]

    def fill(dst, base, wide_field, own, xs, count, ys, ycount, table, edge_at):
        size = 32 if wide_field else 16
        own_at, halo_at = ((8, 24), (16, 0)) if wide_field else ((0,), (8,))
        todo = []
        for x in range(8):
            todo.append((own_at, x + 4, 0, own[0][pl.ds(own[1] + x * 8, 8), :]))
            todo.append((halo_at, x + 4, 8 - ycount, ys[0][0][pl.ds(ys[0][1] + x * ycount, ycount), :] * ym))
            todo.append((halo_at, x + 4, 0, ys[1][0][pl.ds(ys[1][1] + x * ycount, ycount), :] * yp))
        for i in range(count):
            (low, low_at), (high, high_at) = xs
            todo.append((own_at, 4 - count + i, 0, low[pl.ds(low_at + i * 8, 8), :] * xm))
            todo.append((own_at, 12 + i, 0, high[pl.ds(high_at + i * 8, 8), :] * xp))
        for x, rows, at in table:
            m = xm if x < 0 else xp
            todo.append((halo_at, x + 4, 8 - rows, eprev[pl.ds(edge_at + at, rows), :] * (m * ym)))
            todo.append((halo_at, x + 4, 0, enext[pl.ds(edge_at + at, rows), :] * (m * yp)))
        for offsets, x, at, value in todo:
            for offset in offsets:
                dst[pl.ds(base + x * size + offset + at, value.shape[0]), :] = value

    def faces(start):
        return (held, start), (held, FACE_ROWS + start)

    def fill_rhs(i, carry):
        for u in range(FILLS):
            r = i * FILLS + u
            xs = (kept, r * 32), (kept, FACE_ROWS + r * 32)
            fill(ea, r * WIDE, True, (fields, r * 64), xs, 4, faces(r * 32), 4, EDGES4, r * 12)
        values = [fields[pl.ds((i * FILLS + u) * 64 + x * 8, 8), :] for u in range(FILLS) for x in range(8)]
        for u in range(FILLS):
            for x in range(8):
                basis[pl.ds(x * 8 * COLS + i * FILLS + u, 8, stride=COLS), :] = values[u * 8 + x]
        return carry

    lax.fori_loop(0, RHS // FILLS, fill_rhs, 0)
    for i in range(4):
        start = face_at(RHS + i, 0)[0]
        own, xs = (fields, (RHS + i) * 64), ((kept, start), (kept, FACE_ROWS + start))
        fill(ec, i * NARROW, False, own, xs, 3, faces(start), 3, EDGES3, COEF_AT + i * 6)
        at, count = REACH[i]
        own, xs = (slabs, i * 64), ((sprev, at), (snext, at))
        ys = (eprev, FACE_AT[i]), (enext, FACE_AT[i])
        fill(es, i * NARROW, False, own, xs, count, ys, count, ENDS_AT[i][1], ENDS_AT[i][0])

    for x in range(16):
        for tile in range(2):
            at = x * 16 + tile * 8
            outer, inner = es[at : at + 8, :], es[2 * NARROW + at : 2 * NARROW + at + 8, :]
            pair = (jnp.where(lane8 < 4, outer, inner), jnp.where(lane8 < 4, inner, outer))
            for base, value in zip((LOW, HIGH), pair):
                for offset in ((8, 24), (16, 0))[tile]:
                    ea[base + x * 32 + offset : base + x * 32 + offset + 8, :] = value

    def weights(a, vs, ok):
        sixth = ok * F32(1 / 6)
        out = [(a - 1.0) * sixth]
        for v in vs:
            out += [(0.5 * v - 1.0) * sixth, (-0.5 * v - 1.0) * sixth]
        return out

    def make(i, carry):
        done = []
        for u in range(MAKES):
            x = 1 + i * MAKES + u
            okx = jnp.where(x < 4, xm, jnp.where(x >= 12, xp, F32(1)))
            for tile in range(2):
                at = x * 16 + tile * 8
                ok = okx * (jnp.where(row < 4, yp, ym) if tile else jnp.ones((8, 128), F32))
                cs = [ec[pl.ds(i * NARROW + at, 8), :] for i in range(4)]
                done.append((main, at, weights(cs[0], cs[1:], ok)))
                outer, inner = es[pl.ds(NARROW + at, 8), :], es[pl.ds(3 * NARROW + at, 8), :]
                for k, (pick, okz) in enumerate(((lane8 < 4, zm), (lane8 >= 4, zp))):
                    narrow = jnp.where(pick, outer, inner)
                    cs = [jnp.take_along_axis(narrow, lane8 + 8 * i, axis=1) for i in range(4)]
                    values = weights(cs[0], cs[1:], ok * jnp.where(pick, okz, F32(1)))
                    done.append((side, k * 7 * NARROW + at, values))
        for dst, at, values in done:
            for i in range(7):
                dst[pl.ds(i * NARROW + at, 8), :] = values[i]
        return carry

    lax.fori_loop(0, 14 // MAKES, make, 0)

    for s in range(1, STEPS + 1):
        src, dst = (ea, eb) if s % 2 else (eb, ea)
        last = s == STEPS

        tiles = [(x, 0) for x in range(s, 16 - s)]
        if not last:
            tiles += [(x, 1) for x in range(s + 1, 15 - s)]
        for x, tile in tiles:
            at = x * 32 + 8 + tile * 8
            both = jnp.where(lane8 == 4, src[HIGH + at : HIGH + at + 8, :], src[LOW + at : LOW + at + 8, :])
            for r in range(RHS):
                to = r * NARROW + x * 16 + tile * 8
                turn[to : to + 8, :] = rolled(both, -(8 * r + 4))

        def step(x, tile, keep, s=s, src=src, dst=dst, last=last):
            at = x * 32 + 8 + tile * 8
            small = x * 16 + tile * 8

            def apply(c, base, v, zplus, zminus):
                out = c[0] * v
                out = out + c[1] * src[pl.ds(base + at + 32, 8), :]
                out = out + c[2] * src[pl.ds(base + at - 32, 8), :]
                out = out + c[3] * src[pl.ds(base + at + 1, 8), :]
                out = out + c[4] * src[pl.ds(base + at - 1, 8), :]
                out = out + c[5] * zplus
                return out + c[6] * zminus

            def put(base, out):
                for offset in ((8, 24), (16, 0))[tile]:
                    dst[pl.ds(base + x * 32 + offset, 8), :] = out

            cs = [main[pl.ds(i * NARROW + small, 8), :] for i in range(7)]
            for r in range(RHS):
                v = src[pl.ds(r * WIDE + at, 8), :]
                over = turn[pl.ds(r * NARROW + small, 8), :]
                zplus = rolled(jnp.where(lane == 0, over, v), -1)
                zminus = rolled(jnp.where(lane == 127, over, v), 1)
                out = apply(cs, r * WIDE, v, zplus, zminus)
                if keep:
                    basis[pl.ds((x - 4) * 8 * COLS + s * RHS + r, 8, stride=COLS), :] = out
                if not last:
                    put(r * WIDE, out)
            if not last:
                for k, base in enumerate((LOW, HIGH)):
                    cs = [side[pl.ds((k * 7 + i) * NARROW + small, 8), :] for i in range(7)]
                    v = src[pl.ds(base + at, 8), :]
                    put(base, apply(cs, base, v, rolled(v, -1), rolled(v, 1)))

        def inside(i, carry, step=step):
            for u in range(OWN):
                step(4 + i * OWN + u, 0, True)
            return carry

        def outside(i, carry, s=s, step=step):
            for u in range(4 - s):
                step(s + i * (12 - s) + u, 0, False)
            return carry

        def halo(i, carry, s=s, step=step):
            for u in range(7 - s):
                step(s + 1 + i * (7 - s) + u, 1, False)
            return carry

        lax.fori_loop(0, 8 // OWN, inside, 0)
        if not last:
            lax.fori_loop(0, 2, outside, 0)
            lax.fori_loop(0, 2, halo, 0)

    zeros = jnp.zeros((128 - COLS, 256), BF16)

    def product(i, acc):
        for u in range(GRAMS):
            base = pl.multiple_of((i * GRAMS + u) * 2 * COLS, 2 * COLS)
            value = jnp.concatenate([basis[pl.ds(base, COLS), :], basis[pl.ds(base + COLS, COLS), :]], axis=1)
            high = value.astype(BF16)
            low = (value - high.astype(F32)).astype(BF16)
            acc = acc + lax.dot_general(
                wide([high, low]),
                wide([high, zeros, low, zeros]),
                (((1,), (1,)), ((), ())),
                preferred_element_type=F32,
            )
        return acc

    acc = lax.fori_loop(0, 32 // GRAMS, product, jnp.zeros((2 * COLS, 256), F32))
    gram = (acc[:COLS, :128] + acc[COLS:, 128:]) + (acc[:COLS, 128:] + acc[COLS:, :128])
    part = [gram[i * RHS : (i + 1) * RHS] for i in range(STEPS + 1)]
    lane = lax.broadcasted_iota(jnp.int32, (RHS, 128), 1)
    packed[:RHS, :] = jnp.where(
        lane < 80, part[0], jnp.where(lane < 112, rolled(part[3], 32), rolled(part[4], 48))
    )
    packed[RHS:, :] = jnp.where(
        lane < 64, rolled(part[1], -16), jnp.where(lane < 112, rolled(part[2], 32), 0.0)
    )


def solved(p, right):
    (a, b), (c, d) = p[0][:2], p[1][:2]
    scale = 1.0 / (a * d - b * c)
    inverse = ((d * scale, -(b * scale)), (-(c * scale), a * scale))
    return [[i[0] * u + i[1] * v for u, v in zip(*right)] for i in inverse]


def solve_combine(parts, basis, solution_field, residual, held, sems):
    total = parts[0]
    for i in range(1, parts.shape[0]):
        total = total + parts[i]
    first, second = total[:RHS], total[RHS:]
    lane = lax.broadcasted_iota(jnp.int32, (RHS, 128), 1)

    def span(value, start):
        return jnp.where((lane >= start) & (lane < COLS), value, 0.0)

    upper = [
        span(first, 0),
        span(rolled(second, 16), 16),
        span(rolled(second, -32), 32),
        span(rolled(first, -32), 48),
        span(rolled(first, -48), 64),
    ]
    flipped = jnp.transpose(wide(upper + [jnp.zeros((128 - COLS, 128), F32)]))
    gram = wide(
        [
            jnp.where(lane < i * RHS, flipped[i * RHS : (i + 1) * RHS], upper[i])
            for i in range(STEPS + 1)
        ]
    )
    half = 7.0 * gram + 6.0 * rolled(gram, -RHS)
    half = jnp.where(lax.broadcasted_iota(jnp.int32, (COLS, 128), 1) < KEEP, half, 0.0)
    normal = 7.0 * half[:KEEP] + 6.0 * half[RHS:]
    m = [normal[i * 8 : i * 8 + 8] for i in range(8)] + [half[:8], half[8:RHS]]
    lane = lanes()

    def column(i, c):
        return jnp.broadcast_to(m[i][:, c : c + 1], (8, 128))

    def row(value, r):
        return jnp.broadcast_to(value[r : r + 1, :], (8, 128))

    def square(r, c):
        columns = [column(r // 8, c + j) for j in range(BLOCK)]
        return [[row(columns[j], r % 8 + i) for j in range(BLOCK)] for i in range(BLOCK)]

    pivots = square(0, 0)
    for k in range(0, KEEP, BLOCK):
        i0, s = divmod(k, 8)
        inside = (lane >= k) & (lane < k + BLOCK)
        keep = list(range(i0 + 1 if s + BLOCK == 8 else i0, 10))
        columns = {i: [column(i, k + c) for c in range(BLOCK)] for i in keep}
        rows = [
            jnp.where(lane == k + d, -1.0, jnp.where(inside, 0.0, row(m[i0], s + d))) for d in range(BLOCK)
        ]
        more = k + BLOCK < KEEP
        if more:
            across, after = square(k, k + BLOCK), square(k + BLOCK, k + BLOCK)
            rights = [across[d] + [rows[d]] for d in range(BLOCK)]
        else:
            rights = [[rows[d]] for d in range(BLOCK)]
        upper = solved(pivots[:2], [pivots[d][2:] + rights[d] for d in (0, 1)])
        rest = [
            [u - (pivots[e][0] * v + pivots[e][1] * w) for u, v, w in zip(pivots[e][2:] + rights[e], *upper)]
            for e in (2, 3)
        ]
        lower = solved(rest, [r[2:] for r in rest])
        upper = [
            [u - (upper[d][0] * v + upper[d][1] * w) for u, v, w in zip(upper[d][2:], *lower)] for d in (0, 1)
        ]
        result = upper + lower
        if more:
            pivots = [
                [
                    after[d][c] - (
                        (across[0][d] * result[0][c] + across[1][d] * result[1][c])
                        + (across[2][d] * result[2][c] + across[3][d] * result[3][c])
                    )
                    for c in range(BLOCK)
                ]
                for d in range(BLOCK)
            ]
        for i in keep:
            value = jnp.where(inside, 0.0, m[i])
            for c in range(BLOCK):
                value = value - columns[i][c] * result[c][-1]
            m[i] = value
    coef = wide(m[8:])
    mixed = 7.0 * coef + 6.0 * rolled(coef, RHS)
    both = wide([coef, mixed])
    high = both.astype(BF16).astype(F32)
    mid = (both - high).astype(BF16).astype(F32)
    low = both - high - mid
    lane = lax.broadcasted_iota(jnp.int32, (2 * RHS, 128), 1)

    def tripled(value, parts):
        left = value if parts == 1 else jnp.where(lane < 80, value, rolled(value, 80))
        right = jnp.where(lane < 32, rolled(value, -48), 0.0) if parts > 1 else jnp.zeros_like(value)
        if parts == 3:
            right = jnp.where((lane >= 32) & (lane < 112), rolled(value, 32), right)
        return jnp.concatenate([left, right], axis=1)

    factors = wide([tripled(high, 3), tripled(mid, 2), tripled(low, 1)[RHS:]]).astype(BF16)
    zeros = jnp.zeros((16, 256), BF16)

    def combine(i, carry):
        done = []
        for u in range(PAIRS):
            base = pl.multiple_of((i * PAIRS + u) * 2 * COLS, 2 * COLS)
            value = jnp.concatenate([basis[pl.ds(base, COLS), :], basis[pl.ds(base + COLS, COLS), :]], axis=1)
            high = value.astype(BF16)
            rest = value - high.astype(F32)
            mid = rest.astype(BF16)
            low = (rest - mid.astype(F32)).astype(BF16)
            out = jnp.dot(factors, wide([high, mid, low, zeros]), preferred_element_type=F32)
            mixed = out[RHS : 2 * RHS] + (out[3 * RHS : 4 * RHS] + out[4 * RHS :])
            done.append((out[:RHS] + out[2 * RHS : 3 * RHS], value[:RHS] - mixed))
        for u in range(PAIRS):
            for c in range(2):
                at = 2 * (i * PAIRS + u) + c
                held[pl.ds(at, RHS, stride=64), :] = done[u][0][:, c * 128 : (c + 1) * 128]
                held[pl.ds(1024 + at, RHS, stride=64), :] = done[u][1][:, c * 128 : (c + 1) * 128]
        return carry

    count = 32 // PAIRS
    copies = []
    for i in range(count):
        combine(i, 0)
        rows = pl.ds(i * 2 * PAIRS, 2 * PAIRS)
        for k, out in enumerate((solution_field, residual)):
            src = held.reshape(2, RHS, 64, 128).at[k, :, rows, :]
            copies.append(pltpu.make_async_copy(src, out.at[:, rows, :], sems.at[i * 2 + k]))
            copies[-1].start()
    for copy in copies:
        copy.wait()


def call(kernel, ins, outs, scratch=(), smem=False, hbm=False):
    vmem = pl.BlockSpec(memory_space=pltpu.VMEM)
    specs = [vmem] * len(ins)
    if smem:
        specs[0] = pl.BlockSpec(memory_space=pltpu.SMEM)
    return pl.pallas_call(
        kernel,
        out_shape=[jax.ShapeDtypeStruct(s, F32) for s in outs],
        in_specs=specs,
        out_specs=[pl.BlockSpec(memory_space=pl.ANY) if hbm else vmem] * len(outs),
        scratch_shapes=[pltpu.VMEM(s, F32) if isinstance(s, tuple) else s for s in scratch],
        compiler_params=pltpu.CompilerParams(vmem_limit_bytes=LIMIT),
    )(*ins)


def shift(value, axis, by):
    count = lax.axis_size(axis)
    return lax.ppermute(value, axis, [(i, (i + by) % count) for i in range(count)])


def gathered(value, axis):
    count = lax.axis_size(axis)
    return lax.all_to_all(jnp.broadcast_to(value[None], (count,) + value.shape), axis, 0, 0)


def shards(right_side, absorption, velocity):
    axes = ("gx", "gy", ("zx", "core"))
    ends = []
    for axis in axes:
        at = lax.axis_index(axis)
        ends += [at > 0, at < lax.axis_size(axis) - 1]
    flags = jnp.stack(ends).astype(F32)
    fields = jnp.concatenate([right_side, absorption[None], velocity], axis=0).reshape((RHS + 4) * 64, 128)
    face = (FACE_ROWS, 128)
    ends_z, xlow, xhigh, ylow, yhigh = call(pack_own, [fields], [(128, 128), face, face, face, face])
    xprev = shift(xhigh, "gx", 1)
    xnext = shift(xlow, "gx", -1)
    zprev = shift(ends_z, axes[2], 1)
    znext = shift(ends_z, axes[2], -1)
    slabs, slow, shigh = call(
        pack_ends, [flags, ends_z, zprev, znext], [(256, 128), (128, 128), (128, 128)], smem=True
    )
    sprev = shift(shigh, "gx", 1)
    snext = shift(slow, "gx", -1)
    yprev = shift(yhigh, "gy", 1)
    ynext = shift(ylow, "gy", -1)
    edge = (EDGE_ROWS, 128)
    elow, ehigh, kept = call(pack_edges, [slabs, xprev, xnext, sprev, snext], [edge, edge, (2 * FACE_ROWS, 128)])
    eprev = shift(ehigh, "gy", 1)
    enext = shift(elow, "gy", -1)
    (held,) = call(keep_faces, [yprev, ynext], [(2 * FACE_ROWS, 128)])
    basis, packed = call(
        steps_gram,
        [flags, fields, slabs, kept, sprev, snext, held, eprev, enext],
        [(64 * COLS, 128), (2 * RHS, 128)],
        [(18 * WIDE, 128)] * 2 + [(n * NARROW, 128) for n in (4, 4, 7, 14, RHS)],
        smem=True,
    )
    packed = packed + shift(packed, "core", 1)
    packed = gathered(packed, ("gx", "zx")).sum(0)
    parts = gathered(packed, "gy")
    solution_field, residual = call(
        solve_combine,
        [parts, basis],
        [(RHS, 64, 128), (RHS, 64, 128)],
        [pltpu.VMEM((2048, 128), F32), pltpu.SemaphoreType.DMA((64 // PAIRS,))],
        hbm=True,
    )
    return solution_field.reshape(right_side.shape), residual.reshape(right_side.shape)


def solution(mesh):
    nx, ny, nz = mesh.devices.shape
    split = Mesh(mesh.devices.reshape(nx, ny, nz // 2, 2), ("gx", "gy", "zx", "core"))
    z = ("zx", "core")
    return jax.shard_map(
        shards,
        mesh=split,
        in_specs=(P(None, "gx", "gy", z), P("gx", "gy", z), P(None, "gx", "gy", z)),
        out_specs=(P(None, "gx", "gy", z), P(None, "gx", "gy", z)),
        check_vma=False,
    )
```

```python
import jax
import jax.numpy as jnp
from jax import lax
from jax.experimental import pallas as pl
from jax.experimental.pallas import tpu as pltpu
from jax.sharding import Mesh, PartitionSpec as P

RHS = 16
STEPS = 4
COLS = RHS * (STEPS + 1)
KEEP = RHS * STEPS
FILLS = 4
MAKES = 7
OWN = 8
GRAMS = 16
PAIRS = 8
BLOCK = 4
LOW = RHS * 512
HIGH = LOW + 512
LIMIT = 28 * 1024 * 1024
F32 = jnp.float32
BF16 = jnp.bfloat16


def lanes():
    return lax.broadcasted_iota(jnp.int32, (8, 128), 1)


def borders():
    places = [(lax.axis_index(axis), lax.axis_size(axis)) for axis in ("gx", "gy")]
    places.append((lax.axis_index("zx") * 2 + lax.axis_index("core"), lax.axis_size("zx") * 2))
    out = []
    for at, size in places:
        out += [jnp.where(at > 0, F32(1), F32(0)), jnp.where(at < size - 1, F32(1), F32(0))]
    return out


def rolled(x, amount):
    amount = amount % x.shape[-1]
    return x if amount == 0 else pltpu.roll(x, amount, x.ndim - 1)


def wide(pieces):
    return jnp.concatenate(pieces, axis=0)


FACE_ROWS = RHS * 32 + 4 * 24


def face_at(f, side):
    count = 4 if f < RHS else 3
    start = f * 32 if f < RHS else RHS * 32 + (f - RHS) * 24
    return start, count, (0 if side == 0 else 8 - count)


def pack_own(own, ends, xlow, xhigh, ylow, yhigh):
    group = lanes() // 8
    for x in range(8):
        tiles = [own[f * 64 + x * 8 : f * 64 + x * 8 + 8, :] for f in range(RHS + 4)]
        for part, at in ((tiles[:RHS], 0), (tiles[RHS:], 64)):
            acc = rolled(part[0], 4)
            for i in range(1, len(part)):
                acc = jnp.where(group == i, rolled(part[i], 8 * i + 4), acc)
            ends[at + x * 8 : at + x * 8 + 8, :] = acc
        for f, tile in enumerate(tiles):
            for side, (xout, yout) in enumerate(((xlow, ylow), (xhigh, yhigh))):
                start, count, first = face_at(f, side)
                if first <= x < first + count:
                    xout[start + (x - first) * 8 : start + (x - first) * 8 + 8, :] = tile
                yout[start + x * count : start + x * count + count, :] = tile[first : first + count]


REACH = ((0, 3), (24, 2), (40, 2), (56, 1))


def pack_ends(ends, mate, other, slabs, xlow, xhigh):
    from_mate = (lanes() % 8 < 4) == (lax.axis_index("core") == 1)
    for j in range(4):
        for x in range(8):
            at = slice((j % 2) * 64 + x * 8, (j % 2) * 64 + x * 8 + 8)
            tile = ends[at, :] if j > 1 else jnp.where(from_mate, mate[at, :], other[at, :])
            slabs[j * 64 + x * 8 : j * 64 + x * 8 + 8, :] = tile
            start, count = REACH[j]
            for xout, first in ((xlow, 0), (xhigh, 8 - count)):
                if first <= x < first + count:
                    xout[start + (x - first) * 8 : start + (x - first) * 8 + 8, :] = tile


EDGES4 = ((-1, 3, 0), (8, 3, 3), (-2, 2, 6), (9, 2, 8), (-3, 1, 10), (10, 1, 11))
EDGES3 = ((-1, 2, 0), (8, 2, 2), (-2, 1, 4), (9, 1, 5))
EDGES2 = ((-1, 1, 0), (8, 1, 1))
COEF_AT = RHS * 12
ENDS_AT = ((COEF_AT + 24, EDGES3), (COEF_AT + 30, EDGES2), (COEF_AT + 32, EDGES2), (COEF_AT + 34, ()))
FACE_AT = (COEF_AT + 34, COEF_AT + 58, COEF_AT + 74, COEF_AT + 90)
EDGE_ROWS = 384


def pack_edges(slabs, xprev, xnext, sprev, snext, ylow, yhigh, kept):
    def put(table, to, prev, nxt, before, after):
        for x, rows, at in table:
            tile = prev[pl.ds(before + x * 8, 8), :] if x < 0 else nxt[pl.ds(after + (x - 8) * 8, 8), :]
            ylow[pl.ds(to + at, rows), :] = tile[:rows]
            yhigh[pl.ds(to + at, rows), :] = tile[8 - rows :]

    for r in range(RHS):
        put(EDGES4, r * 12, xprev, xnext, r * 32 + 32, r * 32)
    for i in range(4):
        start = face_at(RHS + i, 0)[0]
        put(EDGES3, COEF_AT + i * 6, xprev, xnext, start + 24, start)
        start, count = REACH[i]
        put(ENDS_AT[i][1], ENDS_AT[i][0], sprev, snext, start + count * 8, start)
        for x in range(8):
            tile = slabs[i * 64 + x * 8 : i * 64 + x * 8 + 8, :]
            at = FACE_AT[i] + x * count
            ylow[at : at + count, :] = tile[:count]
            yhigh[at : at + count, :] = tile[8 - count :]
    keep_faces(xprev, xnext, kept)


def keep_faces(prev, nxt, kept):
    kept[:FACE_ROWS, :] = prev[:, :]
    kept[FACE_ROWS:, :] = nxt[:, :]


WIDE = 512
NARROW = 256


def steps_gram(
    fields, slabs, kept, sprev, snext, held, eprev, enext,
    basis, packed, ea, eb, es, ec, main, side, turn,
):
    lane = lanes()
    lane8 = lane % 8
    row = lax.broadcasted_iota(jnp.int32, (8, 128), 0)
    xm, xp, ym, yp, zm, zp = borders()
    beyond_ends = jnp.where(lane8 < 4, zm, zp)

    def fill(dst, base, wide_field, own, xs, count, ys, ycount, table, edge_at):
        size = 32 if wide_field else 16
        own_at, halo_at = ((8, 24), (16, 0)) if wide_field else ((0,), (8,))
        todo = []
        for x in range(8):
            todo.append((own_at, x + 4, 0, own[0][pl.ds(own[1] + x * 8, 8), :]))
            todo.append((halo_at, x + 4, 8 - ycount, ys[0][0][pl.ds(ys[0][1] + x * ycount, ycount), :] * ym))
            todo.append((halo_at, x + 4, 0, ys[1][0][pl.ds(ys[1][1] + x * ycount, ycount), :] * yp))
        for i in range(count):
            (low, low_at), (high, high_at) = xs
            todo.append((own_at, 4 - count + i, 0, low[pl.ds(low_at + i * 8, 8), :] * xm))
            todo.append((own_at, 12 + i, 0, high[pl.ds(high_at + i * 8, 8), :] * xp))
        for x, rows, at in table:
            m = xm if x < 0 else xp
            todo.append((halo_at, x + 4, 8 - rows, eprev[pl.ds(edge_at + at, rows), :] * (m * ym)))
            todo.append((halo_at, x + 4, 0, enext[pl.ds(edge_at + at, rows), :] * (m * yp)))
        for offsets, x, at, value in todo:
            for offset in offsets:
                dst[pl.ds(base + x * size + offset + at, value.shape[0]), :] = value

    def faces(start):
        return (held, start), (held, FACE_ROWS + start)

    def fill_rhs(i, carry):
        for u in range(FILLS):
            r = i * FILLS + u
            xs = (kept, r * 32), (kept, FACE_ROWS + r * 32)
            fill(ea, r * WIDE, True, (fields, r * 64), xs, 4, faces(r * 32), 4, EDGES4, r * 12)
        values = [fields[pl.ds((i * FILLS + u) * 64 + x * 8, 8), :] for u in range(FILLS) for x in range(8)]
        for u in range(FILLS):
            for x in range(8):
                basis[pl.ds(x * 8 * COLS + i * FILLS + u, 8, stride=COLS), :] = values[u * 8 + x]
        return carry

    lax.fori_loop(0, RHS // FILLS, fill_rhs, 0)
    for i in range(4):
        start = face_at(RHS + i, 0)[0]
        own, xs = (fields, (RHS + i) * 64), ((kept, start), (kept, FACE_ROWS + start))
        fill(ec, i * NARROW, False, own, xs, 3, faces(start), 3, EDGES3, COEF_AT + i * 6)
        at, count = REACH[i]
        own, xs = (slabs, i * 64), ((sprev, at), (snext, at))
        ys = (eprev, FACE_AT[i]), (enext, FACE_AT[i])
        fill(es, i * NARROW, False, own, xs, count, ys, count, ENDS_AT[i][1], ENDS_AT[i][0])

    for x in range(16):
        for tile in range(2):
            at = x * 16 + tile * 8
            outer, inner = es[at : at + 8, :] * beyond_ends, es[2 * NARROW + at : 2 * NARROW + at + 8, :]
            pair = (jnp.where(lane8 < 4, outer, inner), jnp.where(lane8 < 4, inner, outer))
            for base, value in zip((LOW, HIGH), pair):
                for offset in ((8, 24), (16, 0))[tile]:
                    ea[base + x * 32 + offset : base + x * 32 + offset + 8, :] = value

    def weights(a, vs, ok):
        sixth = ok * F32(1 / 6)
        out = [(a - 1.0) * sixth]
        for v in vs:
            out += [(0.5 * v - 1.0) * sixth, (-0.5 * v - 1.0) * sixth]
        return out

    def make(i, carry):
        done = []
        for u in range(MAKES):
            x = 1 + i * MAKES + u
            okx = jnp.where(x < 4, xm, jnp.where(x >= 12, xp, F32(1)))
            for tile in range(2):
                at = x * 16 + tile * 8
                ok = okx * (jnp.where(row < 4, yp, ym) if tile else jnp.ones((8, 128), F32))
                cs = [ec[pl.ds(i * NARROW + at, 8), :] for i in range(4)]
                done.append((main, at, weights(cs[0], cs[1:], ok)))
                outer, inner = es[pl.ds(NARROW + at, 8), :], es[pl.ds(3 * NARROW + at, 8), :]
                for k, (pick, okz) in enumerate(((lane8 < 4, zm), (lane8 >= 4, zp))):
                    narrow = jnp.where(pick, outer, inner)
                    cs = [jnp.take_along_axis(narrow, lane8 + 8 * i, axis=1) for i in range(4)]
                    values = weights(cs[0], cs[1:], ok * jnp.where(pick, okz, F32(1)))
                    done.append((side, k * 7 * NARROW + at, values))
        for dst, at, values in done:
            for i in range(7):
                dst[pl.ds(i * NARROW + at, 8), :] = values[i]
        return carry

    lax.fori_loop(0, 14 // MAKES, make, 0)

    for s in range(1, STEPS + 1):
        src, dst = (ea, eb) if s % 2 else (eb, ea)
        last = s == STEPS

        tiles = [(x, 0) for x in range(s, 16 - s)]
        if not last:
            tiles += [(x, 1) for x in range(s + 1, 15 - s)]
        for x, tile in tiles:
            at = x * 32 + 8 + tile * 8
            both = jnp.where(lane8 == 4, src[HIGH + at : HIGH + at + 8, :], src[LOW + at : LOW + at + 8, :])
            for r in range(RHS):
                to = r * NARROW + x * 16 + tile * 8
                turn[to : to + 8, :] = rolled(both, -(8 * r + 4))

        def step(x, tile, keep, s=s, src=src, dst=dst, last=last):
            at = x * 32 + 8 + tile * 8
            small = x * 16 + tile * 8

            def apply(c, base, v, zplus, zminus):
                out = c[0] * v
                out = out + c[1] * src[pl.ds(base + at + 32, 8), :]
                out = out + c[2] * src[pl.ds(base + at - 32, 8), :]
                out = out + c[3] * src[pl.ds(base + at + 1, 8), :]
                out = out + c[4] * src[pl.ds(base + at - 1, 8), :]
                out = out + c[5] * zplus
                return out + c[6] * zminus

            def put(base, out):
                for offset in ((8, 24), (16, 0))[tile]:
                    dst[pl.ds(base + x * 32 + offset, 8), :] = out

            cs = [main[pl.ds(i * NARROW + small, 8), :] for i in range(7)]
            for r in range(RHS):
                v = src[pl.ds(r * WIDE + at, 8), :]
                over = turn[pl.ds(r * NARROW + small, 8), :]
                zplus = rolled(jnp.where(lane == 0, over, v), -1)
                zminus = rolled(jnp.where(lane == 127, over, v), 1)
                out = apply(cs, r * WIDE, v, zplus, zminus)
                if keep:
                    basis[pl.ds((x - 4) * 8 * COLS + s * RHS + r, 8, stride=COLS), :] = out
                if not last:
                    put(r * WIDE, out)
            if not last:
                for k, base in enumerate((LOW, HIGH)):
                    cs = [side[pl.ds((k * 7 + i) * NARROW + small, 8), :] for i in range(7)]
                    v = src[pl.ds(base + at, 8), :]
                    put(base, apply(cs, base, v, rolled(v, -1), rolled(v, 1)))

        def inside(i, carry, step=step):
            for u in range(OWN):
                step(4 + i * OWN + u, 0, True)
            return carry

        def outside(i, carry, s=s, step=step):
            for u in range(4 - s):
                step(s + i * (12 - s) + u, 0, False)
            return carry

        def halo(i, carry, s=s, step=step):
            for u in range(7 - s):
                step(s + 1 + i * (7 - s) + u, 1, False)
            return carry

        lax.fori_loop(0, 8 // OWN, inside, 0)
        if not last:
            lax.fori_loop(0, 2, outside, 0)
            lax.fori_loop(0, 2, halo, 0)

    zeros = jnp.zeros((128 - COLS, 256), BF16)

    def product(i, acc):
        for u in range(GRAMS):
            base = pl.multiple_of((i * GRAMS + u) * 2 * COLS, 2 * COLS)
            value = jnp.concatenate([basis[pl.ds(base, COLS), :], basis[pl.ds(base + COLS, COLS), :]], axis=1)
            high = value.astype(BF16)
            low = (value - high.astype(F32)).astype(BF16)
            acc = acc + lax.dot_general(
                wide([high, low]),
                wide([high, zeros, low, zeros]),
                (((1,), (1,)), ((), ())),
                preferred_element_type=F32,
            )
        return acc

    acc = lax.fori_loop(0, 32 // GRAMS, product, jnp.zeros((2 * COLS, 256), F32))
    gram = (acc[:COLS, :128] + acc[COLS:, 128:]) + (acc[:COLS, 128:] + acc[COLS:, :128])
    part = [gram[i * RHS : (i + 1) * RHS] for i in range(STEPS + 1)]
    lane = lax.broadcasted_iota(jnp.int32, (RHS, 128), 1)
    packed[:RHS, :] = jnp.where(
        lane < 80, part[0], jnp.where(lane < 112, rolled(part[3], 32), rolled(part[4], 48))
    )
    packed[RHS:, :] = jnp.where(
        lane < 64, rolled(part[1], -16), jnp.where(lane < 112, rolled(part[2], 32), 0.0)
    )


def solved(p, right):
    (a, b), (c, d) = p[0][:2], p[1][:2]
    scale = 1.0 / (a * d - b * c)
    inverse = ((d * scale, -(b * scale)), (-(c * scale), a * scale))
    return [[i[0] * u + i[1] * v for u, v in zip(*right)] for i in inverse]


def solve_combine(parts, basis, solution_field, residual, held, sems):
    total = parts[0]
    for i in range(1, parts.shape[0]):
        total = total + parts[i]
    first, second = total[:RHS], total[RHS:]
    lane = lax.broadcasted_iota(jnp.int32, (RHS, 128), 1)

    def span(value, start):
        return jnp.where((lane >= start) & (lane < COLS), value, 0.0)

    upper = [
        span(first, 0),
        span(rolled(second, 16), 16),
        span(rolled(second, -32), 32),
        span(rolled(first, -32), 48),
        span(rolled(first, -48), 64),
    ]
    flipped = jnp.transpose(wide(upper + [jnp.zeros((128 - COLS, 128), F32)]))
    gram = wide(
        [
            jnp.where(lane < i * RHS, flipped[i * RHS : (i + 1) * RHS], upper[i])
            for i in range(STEPS + 1)
        ]
    )
    half = 7.0 * gram + 6.0 * rolled(gram, -RHS)
    half = jnp.where(lax.broadcasted_iota(jnp.int32, (COLS, 128), 1) < KEEP, half, 0.0)
    normal = 7.0 * half[:KEEP] + 6.0 * half[RHS:]
    m = [normal[i * 8 : i * 8 + 8] for i in range(8)] + [half[:8], half[8:RHS]]
    lane = lanes()

    def column(i, c):
        return jnp.broadcast_to(m[i][:, c : c + 1], (8, 128))

    def row(value, r):
        return jnp.broadcast_to(value[r : r + 1, :], (8, 128))

    def square(r, c):
        columns = [column(r // 8, c + j) for j in range(BLOCK)]
        return [[row(columns[j], r % 8 + i) for j in range(BLOCK)] for i in range(BLOCK)]

    pivots = square(0, 0)
    for k in range(0, KEEP, BLOCK):
        i0, s = divmod(k, 8)
        inside = (lane >= k) & (lane < k + BLOCK)
        keep = list(range(i0 + 1 if s + BLOCK == 8 else i0, 10))
        columns = {i: [column(i, k + c) for c in range(BLOCK)] for i in keep}
        rows = [
            jnp.where(lane == k + d, -1.0, jnp.where(inside, 0.0, row(m[i0], s + d))) for d in range(BLOCK)
        ]
        more = k + BLOCK < KEEP
        if more:
            across, after = square(k, k + BLOCK), square(k + BLOCK, k + BLOCK)
            rights = [across[d] + [rows[d]] for d in range(BLOCK)]
        else:
            rights = [[rows[d]] for d in range(BLOCK)]
        upper = solved(pivots[:2], [pivots[d][2:] + rights[d] for d in (0, 1)])
        rest = [
            [u - (pivots[e][0] * v + pivots[e][1] * w) for u, v, w in zip(pivots[e][2:] + rights[e], *upper)]
            for e in (2, 3)
        ]
        lower = solved(rest, [r[2:] for r in rest])
        upper = [
            [u - (upper[d][0] * v + upper[d][1] * w) for u, v, w in zip(upper[d][2:], *lower)] for d in (0, 1)
        ]
        result = upper + lower
        if more:
            pivots = [
                [
                    after[d][c] - (
                        (across[0][d] * result[0][c] + across[1][d] * result[1][c])
                        + (across[2][d] * result[2][c] + across[3][d] * result[3][c])
                    )
                    for c in range(BLOCK)
                ]
                for d in range(BLOCK)
            ]
        for i in keep:
            value = jnp.where(inside, 0.0, m[i])
            for c in range(BLOCK):
                value = value - columns[i][c] * result[c][-1]
            m[i] = value
    coef = wide(m[8:])
    mixed = 7.0 * coef + 6.0 * rolled(coef, RHS)
    both = wide([coef, mixed])
    high = both.astype(BF16).astype(F32)
    mid = (both - high).astype(BF16).astype(F32)
    low = both - high - mid
    lane = lax.broadcasted_iota(jnp.int32, (2 * RHS, 128), 1)

    def tripled(value, parts):
        left = value if parts == 1 else jnp.where(lane < 80, value, rolled(value, 80))
        right = jnp.where(lane < 32, rolled(value, -48), 0.0) if parts > 1 else jnp.zeros_like(value)
        if parts == 3:
            right = jnp.where((lane >= 32) & (lane < 112), rolled(value, 32), right)
        return jnp.concatenate([left, right], axis=1)

    factors = wide([tripled(high, 3), tripled(mid, 2), tripled(low, 1)[RHS:]]).astype(BF16)
    zeros = jnp.zeros((16, 256), BF16)

    def combine(i, carry):
        done = []
        for u in range(PAIRS):
            base = pl.multiple_of((i * PAIRS + u) * 2 * COLS, 2 * COLS)
            value = jnp.concatenate([basis[pl.ds(base, COLS), :], basis[pl.ds(base + COLS, COLS), :]], axis=1)
            high = value.astype(BF16)
            rest = value - high.astype(F32)
            mid = rest.astype(BF16)
            low = (rest - mid.astype(F32)).astype(BF16)
            out = jnp.dot(factors, wide([high, mid, low, zeros]), preferred_element_type=F32)
            mixed = out[RHS : 2 * RHS] + (out[3 * RHS : 4 * RHS] + out[4 * RHS :])
            done.append((out[:RHS] + out[2 * RHS : 3 * RHS], value[:RHS] - mixed))
        for u in range(PAIRS):
            for c in range(2):
                at = 2 * (i * PAIRS + u) + c
                held[pl.ds(at, RHS, stride=64), :] = done[u][0][:, c * 128 : (c + 1) * 128]
                held[pl.ds(1024 + at, RHS, stride=64), :] = done[u][1][:, c * 128 : (c + 1) * 128]
        return carry

    count = 32 // PAIRS
    copies = []
    for i in range(count):
        combine(i, 0)
        rows = pl.ds(i * 2 * PAIRS, 2 * PAIRS)
        for k, out in enumerate((solution_field, residual)):
            src = held.reshape(2, RHS, 64, 128).at[k, :, rows, :]
            copies.append(pltpu.make_async_copy(src, out.at[:, rows, :], sems.at[i * 2 + k]))
            copies[-1].start()
    for copy in copies:
        copy.wait()


def call(kernel, ins, outs, scratch=(), hbm=False):
    vmem = pl.BlockSpec(memory_space=pltpu.VMEM)
    specs = [vmem] * len(ins)
    return pl.pallas_call(
        kernel,
        out_shape=[jax.ShapeDtypeStruct(s, F32) for s in outs],
        in_specs=specs,
        out_specs=[pl.BlockSpec(memory_space=pl.ANY) if hbm else vmem] * len(outs),
        scratch_shapes=[pltpu.VMEM(s, F32) if isinstance(s, tuple) else s for s in scratch],
        compiler_params=pltpu.CompilerParams(vmem_limit_bytes=LIMIT),
    )(*ins)


def shift(value, axis, by):
    count = lax.axis_size(axis)
    return lax.ppermute(value, axis, [(i, (i + by) % count) for i in range(count)])


def gathered(value, axis):
    count = lax.axis_size(axis)
    return lax.all_to_all(jnp.broadcast_to(value[None], (count,) + value.shape), axis, 0, 0)


def shards(right_side, absorption, velocity):
    fields = jnp.concatenate([right_side, absorption[None], velocity], axis=0).reshape((RHS + 4) * 64, 128)
    face = (FACE_ROWS, 128)
    ends_z, xlow, xhigh, ylow, yhigh = call(pack_own, [fields], [(128, 128), face, face, face, face])
    xprev = shift(xhigh, "gx", 1)
    xnext = shift(xlow, "gx", -1)
    count = 2 * lax.axis_size("zx")
    mate = lax.ppermute(ends_z, ("zx", "core"), [(i, i ^ 1) for i in range(count)])
    pairs = [((2 * i + 1) % count, (2 * i + 2) % count) for i in range(count // 2)]
    other = lax.ppermute(ends_z, ("zx", "core"), pairs + [(b, a) for a, b in pairs])
    slabs, slow, shigh = call(
        pack_ends, [ends_z, mate, other], [(256, 128), (128, 128), (128, 128)]
    )
    sprev = shift(shigh, "gx", 1)
    snext = shift(slow, "gx", -1)
    yprev = shift(yhigh, "gy", 1)
    ynext = shift(ylow, "gy", -1)
    edge = (EDGE_ROWS, 128)
    elow, ehigh, kept = call(pack_edges, [slabs, xprev, xnext, sprev, snext], [edge, edge, (2 * FACE_ROWS, 128)])
    eprev = shift(ehigh, "gy", 1)
    enext = shift(elow, "gy", -1)
    (held,) = call(keep_faces, [yprev, ynext], [(2 * FACE_ROWS, 128)])
    basis, packed = call(
        steps_gram,
        [fields, slabs, kept, sprev, snext, held, eprev, enext],
        [(64 * COLS, 128), (2 * RHS, 128)],
        [(18 * WIDE, 128)] * 2 + [(n * NARROW, 128) for n in (4, 4, 7, 14, RHS)],
    )
    packed = packed + shift(packed, "core", 1)
    packed = gathered(packed, ("gx", "zx")).sum(0)
    parts = gathered(packed, "gy")
    solution_field, residual = call(
        solve_combine,
        [parts, basis],
        [(RHS, 64, 128), (RHS, 64, 128)],
        [pltpu.VMEM((2048, 128), F32), pltpu.SemaphoreType.DMA((64 // PAIRS,))],
        hbm=True,
    )
    return solution_field.reshape(right_side.shape), residual.reshape(right_side.shape)


def solution(mesh):
    nx, ny, nz = mesh.devices.shape
    split = Mesh(mesh.devices.reshape(nx, ny, nz // 2, 2), ("gx", "gy", "zx", "core"))
    z = ("zx", "core")
    return jax.shard_map(
        shards,
        mesh=split,
        in_specs=(P(None, "gx", "gy", z), P("gx", "gy", z), P(None, "gx", "gy", z)),
        out_specs=(P(None, "gx", "gy", z), P(None, "gx", "gy", z)),
        check_vma=False,
    )
```

```python
import jax
import jax.numpy as jnp
from jax import lax
from jax.experimental import pallas as pl
from jax.experimental.pallas import tpu as pltpu
from jax.sharding import Mesh, PartitionSpec as P

RHS = 16
STEPS = 4
COLS = RHS * (STEPS + 1)
KEEP = RHS * STEPS
FILLS = 4
MAKES = 7
OWN = 8
GRAMS = 16
PAIRS = 8
BLOCK = 4
LOW = RHS * 512
HIGH = LOW + 512
LIMIT = 28 * 1024 * 1024
F32 = jnp.float32
BF16 = jnp.bfloat16


def lanes():
    return lax.broadcasted_iota(jnp.int32, (8, 128), 1)


def borders():
    places = [(lax.axis_index(axis), lax.axis_size(axis)) for axis in ("gx", "gy")]
    places.append((lax.axis_index("zx") * 2 + lax.axis_index("core"), lax.axis_size("zx") * 2))
    out = []
    for at, size in places:
        out += [jnp.where(at > 0, F32(1), F32(0)), jnp.where(at < size - 1, F32(1), F32(0))]
    return out


def rolled(x, amount):
    amount = amount % x.shape[-1]
    return x if amount == 0 else pltpu.roll(x, amount, x.ndim - 1)


def wide(pieces):
    return jnp.concatenate(pieces, axis=0)


FACE_ROWS = RHS * 32 + 4 * 24


def face_at(f, side):
    count = 4 if f < RHS else 3
    start = f * 32 if f < RHS else RHS * 32 + (f - RHS) * 24
    return start, count, (0 if side == 0 else 8 - count)


def pack_own(own, ends, xlow, xhigh, ylow, yhigh):
    group = lanes() // 8
    for x in range(8):
        tiles = [own[f * 64 + x * 8 : f * 64 + x * 8 + 8, :] for f in range(RHS + 4)]
        for part, at in ((tiles[:RHS], 0), (tiles[RHS:], 64)):
            acc = rolled(part[0], 4)
            for i in range(1, len(part)):
                acc = jnp.where(group == i, rolled(part[i], 8 * i + 4), acc)
            ends[at + x * 8 : at + x * 8 + 8, :] = acc
        for f, tile in enumerate(tiles):
            for side, (xout, yout) in enumerate(((xlow, ylow), (xhigh, yhigh))):
                start, count, first = face_at(f, side)
                if first <= x < first + count:
                    xout[start + (x - first) * 8 : start + (x - first) * 8 + 8, :] = tile
                yout[start + x * count : start + x * count + count, :] = tile[first : first + count]


REACH = ((0, 3), (24, 2), (40, 2), (56, 1))


def pack_ends(ends, mate, other, slabs, xlow, xhigh):
    from_mate = (lanes() % 8 < 4) == (lax.axis_index("core") == 1)
    for j in range(4):
        for x in range(8):
            at = slice((j % 2) * 64 + x * 8, (j % 2) * 64 + x * 8 + 8)
            tile = ends[at, :] if j > 1 else jnp.where(from_mate, mate[at, :], other[at, :])
            slabs[j * 64 + x * 8 : j * 64 + x * 8 + 8, :] = tile
            start, count = REACH[j]
            for xout, first in ((xlow, 0), (xhigh, 8 - count)):
                if first <= x < first + count:
                    xout[start + (x - first) * 8 : start + (x - first) * 8 + 8, :] = tile


EDGES4 = ((-1, 3, 0), (8, 3, 3), (-2, 2, 6), (9, 2, 8), (-3, 1, 10), (10, 1, 11))
EDGES3 = ((-1, 2, 0), (8, 2, 2), (-2, 1, 4), (9, 1, 5))
EDGES2 = ((-1, 1, 0), (8, 1, 1))
COEF_AT = RHS * 12
ENDS_AT = ((COEF_AT + 24, EDGES3), (COEF_AT + 30, EDGES2), (COEF_AT + 32, EDGES2), (COEF_AT + 34, ()))
FACE_AT = (COEF_AT + 34, COEF_AT + 58, COEF_AT + 74, COEF_AT + 90)
EDGE_ROWS = 296


def pack_edges(slabs, xprev, xnext, sprev, snext, ylow, yhigh, kept):
    def put(table, to, prev, nxt, before, after):
        for x, rows, at in table:
            tile = prev[pl.ds(before + x * 8, 8), :] if x < 0 else nxt[pl.ds(after + (x - 8) * 8, 8), :]
            ylow[pl.ds(to + at, rows), :] = tile[:rows]
            yhigh[pl.ds(to + at, rows), :] = tile[8 - rows :]

    for r in range(RHS):
        put(EDGES4, r * 12, xprev, xnext, r * 32 + 32, r * 32)
    for i in range(4):
        start = face_at(RHS + i, 0)[0]
        put(EDGES3, COEF_AT + i * 6, xprev, xnext, start + 24, start)
        start, count = REACH[i]
        put(ENDS_AT[i][1], ENDS_AT[i][0], sprev, snext, start + count * 8, start)
        for x in range(8):
            tile = slabs[i * 64 + x * 8 : i * 64 + x * 8 + 8, :]
            at = FACE_AT[i] + x * count
            ylow[at : at + count, :] = tile[:count]
            yhigh[at : at + count, :] = tile[8 - count :]
    keep_faces(xprev, xnext, kept)


def keep_faces(prev, nxt, kept):
    kept[:FACE_ROWS, :] = prev[:, :]
    kept[FACE_ROWS:, :] = nxt[:, :]


WIDE = 512
NARROW = 256


def steps_gram(
    fields, slabs, kept, sprev, snext, held, eprev, enext,
    basis, packed, ea, eb, es, ec, main, side, turn,
):
    lane = lanes()
    lane8 = lane % 8
    row = lax.broadcasted_iota(jnp.int32, (8, 128), 0)
    xm, xp, ym, yp, zm, zp = borders()
    beyond_ends = jnp.where(lane8 < 4, zm, zp)

    def fill(dst, base, wide_field, own, xs, count, ys, ycount, table, edge_at):
        size = 32 if wide_field else 16
        own_at, halo_at = ((8, 24), (16, 0)) if wide_field else ((0,), (8,))
        todo = []
        for x in range(8):
            todo.append((own_at, x + 4, 0, own[0][pl.ds(own[1] + x * 8, 8), :]))
            todo.append((halo_at, x + 4, 8 - ycount, ys[0][0][pl.ds(ys[0][1] + x * ycount, ycount), :] * ym))
            todo.append((halo_at, x + 4, 0, ys[1][0][pl.ds(ys[1][1] + x * ycount, ycount), :] * yp))
        for i in range(count):
            (low, low_at), (high, high_at) = xs
            todo.append((own_at, 4 - count + i, 0, low[pl.ds(low_at + i * 8, 8), :] * xm))
            todo.append((own_at, 12 + i, 0, high[pl.ds(high_at + i * 8, 8), :] * xp))
        for x, rows, at in table:
            m = xm if x < 0 else xp
            todo.append((halo_at, x + 4, 8 - rows, eprev[pl.ds(edge_at + at, rows), :] * (m * ym)))
            todo.append((halo_at, x + 4, 0, enext[pl.ds(edge_at + at, rows), :] * (m * yp)))
        for offsets, x, at, value in todo:
            for offset in offsets:
                dst[pl.ds(base + x * size + offset + at, value.shape[0]), :] = value

    def faces(start):
        return (held, start), (held, FACE_ROWS + start)

    def fill_rhs(i, carry):
        for u in range(FILLS):
            r = i * FILLS + u
            xs = (kept, r * 32), (kept, FACE_ROWS + r * 32)
            fill(ea, r * WIDE, True, (fields, r * 64), xs, 4, faces(r * 32), 4, EDGES4, r * 12)
        values = [fields[pl.ds((i * FILLS + u) * 64 + x * 8, 8), :] for u in range(FILLS) for x in range(8)]
        for u in range(FILLS):
            for x in range(8):
                basis[pl.ds(x * 8 * COLS + i * FILLS + u, 8, stride=COLS), :] = values[u * 8 + x]
        return carry

    lax.fori_loop(0, RHS // FILLS, fill_rhs, 0)
    for i in range(4):
        start = face_at(RHS + i, 0)[0]
        own, xs = (fields, (RHS + i) * 64), ((kept, start), (kept, FACE_ROWS + start))
        fill(ec, i * NARROW, False, own, xs, 3, faces(start), 3, EDGES3, COEF_AT + i * 6)
        at, count = REACH[i]
        own, xs = (slabs, i * 64), ((sprev, at), (snext, at))
        ys = (eprev, FACE_AT[i]), (enext, FACE_AT[i])
        fill(es, i * NARROW, False, own, xs, count, ys, count, ENDS_AT[i][1], ENDS_AT[i][0])

    for x in range(16):
        for tile in range(2):
            at = x * 16 + tile * 8
            outer, inner = es[at : at + 8, :] * beyond_ends, es[2 * NARROW + at : 2 * NARROW + at + 8, :]
            pair = (jnp.where(lane8 < 4, outer, inner), jnp.where(lane8 < 4, inner, outer))
            for base, value in zip((LOW, HIGH), pair):
                for offset in ((8, 24), (16, 0))[tile]:
                    ea[base + x * 32 + offset : base + x * 32 + offset + 8, :] = value

    def weights(a, vs, ok):
        sixth = ok * F32(1 / 6)
        out = [(a - 1.0) * sixth]
        for v in vs:
            out += [(0.5 * v - 1.0) * sixth, (-0.5 * v - 1.0) * sixth]
        return out

    def make(i, carry):
        done = []
        for u in range(MAKES):
            x = 1 + i * MAKES + u
            okx = jnp.where(x < 4, xm, jnp.where(x >= 12, xp, F32(1)))
            for tile in range(2):
                at = x * 16 + tile * 8
                ok = okx * (jnp.where(row < 4, yp, ym) if tile else jnp.ones((8, 128), F32))
                cs = [ec[pl.ds(i * NARROW + at, 8), :] for i in range(4)]
                done.append((main, at, weights(cs[0], cs[1:], ok)))
                outer, inner = es[pl.ds(NARROW + at, 8), :], es[pl.ds(3 * NARROW + at, 8), :]
                for k, (pick, okz) in enumerate(((lane8 < 4, zm), (lane8 >= 4, zp))):
                    narrow = jnp.where(pick, outer, inner)
                    cs = [jnp.take_along_axis(narrow, lane8 + 8 * i, axis=1) for i in range(4)]
                    values = weights(cs[0], cs[1:], ok * jnp.where(pick, okz, F32(1)))
                    done.append((side, k * 7 * NARROW + at, values))
        for dst, at, values in done:
            for i in range(7):
                dst[pl.ds(i * NARROW + at, 8), :] = values[i]
        return carry

    lax.fori_loop(0, 14 // MAKES, make, 0)

    for s in range(1, STEPS + 1):
        src, dst = (ea, eb) if s % 2 else (eb, ea)
        last = s == STEPS

        tiles = [(x, 0) for x in range(s, 16 - s)]
        if not last:
            tiles += [(x, 1) for x in range(s + 1, 15 - s)]
        for x, tile in tiles:
            at = x * 32 + 8 + tile * 8
            both = jnp.where(lane8 == 4, src[HIGH + at : HIGH + at + 8, :], src[LOW + at : LOW + at + 8, :])
            for r in range(RHS):
                to = r * NARROW + x * 16 + tile * 8
                turn[to : to + 8, :] = rolled(both, -(8 * r + 4))

        def step(x, tile, keep, s=s, src=src, dst=dst, last=last):
            at = x * 32 + 8 + tile * 8
            small = x * 16 + tile * 8

            def apply(c, base, v, zplus, zminus):
                out = c[0] * v
                out = out + c[1] * src[pl.ds(base + at + 32, 8), :]
                out = out + c[2] * src[pl.ds(base + at - 32, 8), :]
                out = out + c[3] * src[pl.ds(base + at + 1, 8), :]
                out = out + c[4] * src[pl.ds(base + at - 1, 8), :]
                out = out + c[5] * zplus
                return out + c[6] * zminus

            def put(base, out):
                for offset in ((8, 24), (16, 0))[tile]:
                    dst[pl.ds(base + x * 32 + offset, 8), :] = out

            cs = [main[pl.ds(i * NARROW + small, 8), :] for i in range(7)]
            for r in range(RHS):
                v = src[pl.ds(r * WIDE + at, 8), :]
                over = turn[pl.ds(r * NARROW + small, 8), :]
                zplus = rolled(jnp.where(lane == 0, over, v), -1)
                zminus = rolled(jnp.where(lane == 127, over, v), 1)
                out = apply(cs, r * WIDE, v, zplus, zminus)
                if keep:
                    basis[pl.ds((x - 4) * 8 * COLS + s * RHS + r, 8, stride=COLS), :] = out
                if not last:
                    put(r * WIDE, out)
            if not last:
                for k, base in enumerate((LOW, HIGH)):
                    cs = [side[pl.ds((k * 7 + i) * NARROW + small, 8), :] for i in range(7)]
                    v = src[pl.ds(base + at, 8), :]
                    put(base, apply(cs, base, v, rolled(v, -1), rolled(v, 1)))

        def inside(i, carry, step=step):
            for u in range(OWN):
                step(4 + i * OWN + u, 0, True)
            return carry

        def outside(i, carry, s=s, step=step):
            for u in range(4 - s):
                step(s + i * (12 - s) + u, 0, False)
            return carry

        def halo(i, carry, s=s, step=step):
            for u in range(7 - s):
                step(s + 1 + i * (7 - s) + u, 1, False)
            return carry

        lax.fori_loop(0, 8 // OWN, inside, 0)
        if not last:
            lax.fori_loop(0, 2, outside, 0)
            lax.fori_loop(0, 2, halo, 0)

    zeros = jnp.zeros((128 - COLS, 256), BF16)

    def product(i, acc):
        for u in range(GRAMS):
            base = pl.multiple_of((i * GRAMS + u) * 2 * COLS, 2 * COLS)
            value = jnp.concatenate([basis[pl.ds(base, COLS), :], basis[pl.ds(base + COLS, COLS), :]], axis=1)
            high = value.astype(BF16)
            low = (value - high.astype(F32)).astype(BF16)
            acc = acc + lax.dot_general(
                wide([high, low]),
                wide([high, zeros, low, zeros]),
                (((1,), (1,)), ((), ())),
                preferred_element_type=F32,
            )
        return acc

    acc = lax.fori_loop(0, 32 // GRAMS, product, jnp.zeros((2 * COLS, 256), F32))
    gram = (acc[:COLS, :128] + acc[COLS:, 128:]) + (acc[:COLS, 128:] + acc[COLS:, :128])
    part = [gram[i * RHS : (i + 1) * RHS] for i in range(STEPS + 1)]
    lane = lax.broadcasted_iota(jnp.int32, (RHS, 128), 1)
    packed[:RHS, :] = jnp.where(
        lane < 80, part[0], jnp.where(lane < 112, rolled(part[3], 32), rolled(part[4], 48))
    )
    packed[RHS:, :] = jnp.where(
        lane < 64, rolled(part[1], -16), jnp.where(lane < 112, rolled(part[2], 32), 0.0)
    )


def solved(p, right):
    (a, b), (c, d) = p[0][:2], p[1][:2]
    scale = 1.0 / (a * d - b * c)
    inverse = ((d * scale, -(b * scale)), (-(c * scale), a * scale))
    return [[i[0] * u + i[1] * v for u, v in zip(*right)] for i in inverse]


def solve_combine(parts, basis, solution_field, residual, held, sems):
    total = parts[0]
    for i in range(1, parts.shape[0]):
        total = total + parts[i]
    first, second = total[:RHS], total[RHS:]
    lane = lax.broadcasted_iota(jnp.int32, (RHS, 128), 1)

    def span(value, start):
        return jnp.where((lane >= start) & (lane < COLS), value, 0.0)

    upper = [
        span(first, 0),
        span(rolled(second, 16), 16),
        span(rolled(second, -32), 32),
        span(rolled(first, -32), 48),
        span(rolled(first, -48), 64),
    ]
    flipped = jnp.transpose(wide(upper + [jnp.zeros((128 - COLS, 128), F32)]))
    gram = wide(
        [
            jnp.where(lane < i * RHS, flipped[i * RHS : (i + 1) * RHS], upper[i])
            for i in range(STEPS + 1)
        ]
    )
    half = 7.0 * gram + 6.0 * rolled(gram, -RHS)
    half = jnp.where(lax.broadcasted_iota(jnp.int32, (COLS, 128), 1) < KEEP, half, 0.0)
    normal = 7.0 * half[:KEEP] + 6.0 * half[RHS:]
    m = [normal[i * 8 : i * 8 + 8] for i in range(8)] + [half[:8], half[8:RHS]]
    lane = lanes()

    def column(i, c):
        return jnp.broadcast_to(m[i][:, c : c + 1], (8, 128))

    def row(value, r):
        return jnp.broadcast_to(value[r : r + 1, :], (8, 128))

    def square(r, c):
        columns = [column(r // 8, c + j) for j in range(BLOCK)]
        return [[row(columns[j], r % 8 + i) for j in range(BLOCK)] for i in range(BLOCK)]

    pivots = square(0, 0)
    for k in range(0, KEEP, BLOCK):
        i0, s = divmod(k, 8)
        inside = (lane >= k) & (lane < k + BLOCK)
        keep = list(range(i0 + 1 if s + BLOCK == 8 else i0, 10))
        columns = {i: [column(i, k + c) for c in range(BLOCK)] for i in keep}
        rows = [
            jnp.where(lane == k + d, -1.0, jnp.where(inside, 0.0, row(m[i0], s + d))) for d in range(BLOCK)
        ]
        more = k + BLOCK < KEEP
        if more:
            across, after = square(k, k + BLOCK), square(k + BLOCK, k + BLOCK)
            rights = [across[d] + [rows[d]] for d in range(BLOCK)]
        else:
            rights = [[rows[d]] for d in range(BLOCK)]
        upper = solved(pivots[:2], [pivots[d][2:] + rights[d] for d in (0, 1)])
        rest = [
            [u - (pivots[e][0] * v + pivots[e][1] * w) for u, v, w in zip(pivots[e][2:] + rights[e], *upper)]
            for e in (2, 3)
        ]
        lower = solved(rest, [r[2:] for r in rest])
        upper = [
            [u - (upper[d][0] * v + upper[d][1] * w) for u, v, w in zip(upper[d][2:], *lower)] for d in (0, 1)
        ]
        result = upper + lower
        if more:
            pivots = [
                [
                    after[d][c] - (
                        (across[0][d] * result[0][c] + across[1][d] * result[1][c])
                        + (across[2][d] * result[2][c] + across[3][d] * result[3][c])
                    )
                    for c in range(BLOCK)
                ]
                for d in range(BLOCK)
            ]
        for i in keep:
            value = jnp.where(inside, 0.0, m[i])
            for c in range(BLOCK):
                value = value - columns[i][c] * result[c][-1]
            m[i] = value
    coef = wide(m[8:])
    mixed = 7.0 * coef + 6.0 * rolled(coef, RHS)
    both = wide([coef, mixed])
    high = both.astype(BF16).astype(F32)
    mid = (both - high).astype(BF16).astype(F32)
    low = both - high - mid
    lane = lax.broadcasted_iota(jnp.int32, (2 * RHS, 128), 1)

    def tripled(value, parts):
        left = value if parts == 1 else jnp.where(lane < 80, value, rolled(value, 80))
        right = jnp.where(lane < 32, rolled(value, -48), 0.0) if parts > 1 else jnp.zeros_like(value)
        if parts == 3:
            right = jnp.where((lane >= 32) & (lane < 112), rolled(value, 32), right)
        return jnp.concatenate([left, right], axis=1)

    factors = wide([tripled(high, 3), tripled(mid, 2), tripled(low, 1)[RHS:]]).astype(BF16)
    zeros = jnp.zeros((16, 256), BF16)

    def combine(i, carry):
        done = []
        for u in range(PAIRS):
            base = pl.multiple_of((i * PAIRS + u) * 2 * COLS, 2 * COLS)
            value = jnp.concatenate([basis[pl.ds(base, COLS), :], basis[pl.ds(base + COLS, COLS), :]], axis=1)
            high = value.astype(BF16)
            rest = value - high.astype(F32)
            mid = rest.astype(BF16)
            low = (rest - mid.astype(F32)).astype(BF16)
            out = jnp.dot(factors, wide([high, mid, low, zeros]), preferred_element_type=F32)
            mixed = out[RHS : 2 * RHS] + (out[3 * RHS : 4 * RHS] + out[4 * RHS :])
            done.append((out[:RHS] + out[2 * RHS : 3 * RHS], value[:RHS] - mixed))
        for u in range(PAIRS):
            for c in range(2):
                at = 2 * (i * PAIRS + u) + c
                held[pl.ds(at, RHS, stride=64), :] = done[u][0][:, c * 128 : (c + 1) * 128]
                held[pl.ds(1024 + at, RHS, stride=64), :] = done[u][1][:, c * 128 : (c + 1) * 128]
        return carry

    count = 32 // PAIRS
    copies = []
    for i in range(count):
        combine(i, 0)
        rows = pl.ds(i * 2 * PAIRS, 2 * PAIRS)
        for k, out in enumerate((solution_field, residual)):
            src = held.reshape(2, RHS, 64, 128).at[k, :, rows, :]
            copies.append(pltpu.make_async_copy(src, out.at[:, rows, :], sems.at[i * 2 + k]))
            copies[-1].start()
    for copy in copies:
        copy.wait()


def call(kernel, ins, outs, scratch=(), hbm=False):
    vmem = pl.BlockSpec(memory_space=pltpu.VMEM)
    specs = [vmem] * len(ins)
    return pl.pallas_call(
        kernel,
        out_shape=[jax.ShapeDtypeStruct(s, F32) for s in outs],
        in_specs=specs,
        out_specs=[pl.BlockSpec(memory_space=pl.ANY) if hbm else vmem] * len(outs),
        scratch_shapes=[pltpu.VMEM(s, F32) if isinstance(s, tuple) else s for s in scratch],
        compiler_params=pltpu.CompilerParams(vmem_limit_bytes=LIMIT),
    )(*ins)


def shift(value, axis, by):
    count = lax.axis_size(axis)
    return lax.ppermute(value, axis, [(i, (i + by) % count) for i in range(count)])


def gathered(value, axis):
    count = lax.axis_size(axis)
    return lax.all_to_all(jnp.broadcast_to(value[None], (count,) + value.shape), axis, 0, 0)


def shards(right_side, absorption, velocity):
    fields = jnp.concatenate([right_side, absorption[None], velocity], axis=0).reshape((RHS + 4) * 64, 128)
    face = (FACE_ROWS, 128)
    ends_z, xlow, xhigh, ylow, yhigh = call(pack_own, [fields], [(128, 128), face, face, face, face])
    xprev = shift(xhigh, "gx", 1)
    xnext = shift(xlow, "gx", -1)
    count = 2 * lax.axis_size("zx")
    mate = lax.ppermute(ends_z, ("zx", "core"), [(i, i ^ 1) for i in range(count)])
    pairs = [((2 * i + 1) % count, (2 * i + 2) % count) for i in range(count // 2)]
    other = lax.ppermute(ends_z, ("zx", "core"), pairs + [(b, a) for a, b in pairs])
    slabs, slow, shigh = call(
        pack_ends, [ends_z, mate, other], [(256, 128), (128, 128), (128, 128)]
    )
    sprev = shift(shigh, "gx", 1)
    snext = shift(slow, "gx", -1)
    ylow, sprev, snext = lax.optimization_barrier((ylow, sprev, snext))
    yprev = shift(yhigh, "gy", 1)
    ynext = shift(ylow, "gy", -1)
    edge = (EDGE_ROWS, 128)
    elow, ehigh, kept = call(pack_edges, [slabs, xprev, xnext, sprev, snext], [edge, edge, (2 * FACE_ROWS, 128)])
    eprev = shift(ehigh, "gy", 1)
    enext = shift(elow, "gy", -1)
    (held,) = call(keep_faces, [yprev, ynext], [(2 * FACE_ROWS, 128)])
    basis, packed = call(
        steps_gram,
        [fields, slabs, kept, sprev, snext, held, eprev, enext],
        [(64 * COLS, 128), (2 * RHS, 128)],
        [(18 * WIDE, 128)] * 2 + [(n * NARROW, 128) for n in (4, 4, 7, 14, RHS)],
    )
    packed = packed + shift(packed, "core", 1)
    packed = gathered(packed, ("gx", "zx")).sum(0)
    parts = gathered(packed, "gy")
    solution_field, residual = call(
        solve_combine,
        [parts, basis],
        [(RHS, 64, 128), (RHS, 64, 128)],
        [pltpu.VMEM((2048, 128), F32), pltpu.SemaphoreType.DMA((64 // PAIRS,))],
        hbm=True,
    )
    return solution_field.reshape(right_side.shape), residual.reshape(right_side.shape)


def solution(mesh):
    nx, ny, nz = mesh.devices.shape
    split = Mesh(mesh.devices.reshape(nx, ny, nz // 2, 2), ("gx", "gy", "zx", "core"))
    z = ("zx", "core")
    return jax.shard_map(
        shards,
        mesh=split,
        in_specs=(P(None, "gx", "gy", z), P("gx", "gy", z), P(None, "gx", "gy", z)),
        out_specs=(P(None, "gx", "gy", z), P(None, "gx", "gy", z)),
        check_vma=False,
    )
```

```python
import jax
import jax.numpy as jnp
from jax import lax
from jax.experimental import pallas as pl
from jax.experimental.pallas import tpu as pltpu
from jax.sharding import Mesh, PartitionSpec as P

RHS = 16
STEPS = 4
COLS = RHS * (STEPS + 1)
KEEP = RHS * STEPS
FILLS = 4
MAKES = 7
OWN = 8
GRAMS = 16
PAIRS = 8
BLOCK = 4
LOW = RHS * 512
HIGH = LOW + 512
LIMIT = 28 * 1024 * 1024
F32 = jnp.float32
BF16 = jnp.bfloat16


def lanes():
    return lax.broadcasted_iota(jnp.int32, (8, 128), 1)


def borders():
    places = [(lax.axis_index(axis), lax.axis_size(axis)) for axis in ("gx", "gy")]
    places.append((lax.axis_index("zx") * 2 + lax.axis_index("core"), lax.axis_size("zx") * 2))
    out = []
    for at, size in places:
        out += [jnp.where(at > 0, F32(1), F32(0)), jnp.where(at < size - 1, F32(1), F32(0))]
    return out


def rolled(x, amount):
    amount = amount % x.shape[-1]
    return x if amount == 0 else pltpu.roll(x, amount, x.ndim - 1)


def wide(pieces):
    return jnp.concatenate(pieces, axis=0)


FACE_ROWS = RHS * 32 + 4 * 24


def face_at(f, side):
    count = 4 if f < RHS else 3
    start = f * 32 if f < RHS else RHS * 32 + (f - RHS) * 24
    return start, count, (0 if side == 0 else 8 - count)


def pack_own(own, ends, xlow, xhigh, ylow, yhigh):
    group = lanes() // 8
    for x in range(8):
        tiles = [own[f * 64 + x * 8 : f * 64 + x * 8 + 8, :] for f in range(RHS + 4)]
        for part, at in ((tiles[:RHS], 0), (tiles[RHS:], 64)):
            acc = rolled(part[0], 4)
            for i in range(1, len(part)):
                acc = jnp.where(group == i, rolled(part[i], 8 * i + 4), acc)
            ends[at + x * 8 : at + x * 8 + 8, :] = acc
        for f, tile in enumerate(tiles):
            for side, (xout, yout) in enumerate(((xlow, ylow), (xhigh, yhigh))):
                start, count, first = face_at(f, side)
                if first <= x < first + count:
                    xout[start + (x - first) * 8 : start + (x - first) * 8 + 8, :] = tile
                yout[start + x * count : start + x * count + count, :] = tile[first : first + count]


REACH = ((0, 3), (24, 2), (40, 2), (56, 1))


def pack_ends(ends, mate, other, slabs, xlow, xhigh):
    from_mate = (lanes() % 8 < 4) == (lax.axis_index("core") == 1)
    for j in range(4):
        for x in range(8):
            at = slice((j % 2) * 64 + x * 8, (j % 2) * 64 + x * 8 + 8)
            tile = ends[at, :] if j > 1 else jnp.where(from_mate, mate[at, :], other[at, :])
            slabs[j * 64 + x * 8 : j * 64 + x * 8 + 8, :] = tile
            start, count = REACH[j]
            for xout, first in ((xlow, 0), (xhigh, 8 - count)):
                if first <= x < first + count:
                    xout[start + (x - first) * 8 : start + (x - first) * 8 + 8, :] = tile


EDGES4 = ((-1, 3, 0), (8, 3, 3), (-2, 2, 6), (9, 2, 8), (-3, 1, 10), (10, 1, 11))
EDGES3 = ((-1, 2, 0), (8, 2, 2), (-2, 1, 4), (9, 1, 5))
EDGES2 = ((-1, 1, 0), (8, 1, 1))
COEF_AT = RHS * 12
ENDS_AT = ((COEF_AT + 24, EDGES3), (COEF_AT + 30, EDGES2), (COEF_AT + 32, EDGES2), (COEF_AT + 34, ()))
FACE_AT = (COEF_AT + 34, COEF_AT + 58, COEF_AT + 74, COEF_AT + 90)
EDGE_ROWS = 296


def pack_edges(slabs, xprev, xnext, sprev, snext, ylow, yhigh, kept):
    def put(table, to, prev, nxt, before, after):
        for x, rows, at in table:
            tile = prev[pl.ds(before + x * 8, 8), :] if x < 0 else nxt[pl.ds(after + (x - 8) * 8, 8), :]
            ylow[pl.ds(to + at, rows), :] = tile[:rows]
            yhigh[pl.ds(to + at, rows), :] = tile[8 - rows :]

    for r in range(RHS):
        put(EDGES4, r * 12, xprev, xnext, r * 32 + 32, r * 32)
    for i in range(4):
        start = face_at(RHS + i, 0)[0]
        put(EDGES3, COEF_AT + i * 6, xprev, xnext, start + 24, start)
        start, count = REACH[i]
        put(ENDS_AT[i][1], ENDS_AT[i][0], sprev, snext, start + count * 8, start)
        for x in range(8):
            tile = slabs[i * 64 + x * 8 : i * 64 + x * 8 + 8, :]
            at = FACE_AT[i] + x * count
            ylow[at : at + count, :] = tile[:count]
            yhigh[at : at + count, :] = tile[8 - count :]
    keep_faces(xprev, xnext, kept)


def keep_faces(prev, nxt, kept):
    kept[:FACE_ROWS, :] = prev[:, :]
    kept[FACE_ROWS:, :] = nxt[:, :]


WIDE = 512
NARROW = 256


def steps_gram(
    fields, slabs, kept, sprev, snext, held, eprev, enext,
    basis, packed, ea, eb, es, ec, main, side, turn,
):
    lane = lanes()
    lane8 = lane % 8
    row = lax.broadcasted_iota(jnp.int32, (8, 128), 0)
    xm, xp, ym, yp, zm, zp = borders()
    beyond_ends = jnp.where(lane8 < 4, zm, zp)

    def fill(dst, base, wide_field, own, xs, count, ys, ycount, table, edge_at):
        size = 32 if wide_field else 16
        own_at, halo_at = ((8, 24), (16, 0)) if wide_field else ((0,), (8,))
        todo = []
        for x in range(8):
            todo.append((own_at, x + 4, 0, own[0][pl.ds(own[1] + x * 8, 8), :]))
            todo.append((halo_at, x + 4, 8 - ycount, ys[0][0][pl.ds(ys[0][1] + x * ycount, ycount), :] * ym))
            todo.append((halo_at, x + 4, 0, ys[1][0][pl.ds(ys[1][1] + x * ycount, ycount), :] * yp))
        for i in range(count):
            (low, low_at), (high, high_at) = xs
            todo.append((own_at, 4 - count + i, 0, low[pl.ds(low_at + i * 8, 8), :] * xm))
            todo.append((own_at, 12 + i, 0, high[pl.ds(high_at + i * 8, 8), :] * xp))
        for x, rows, at in table:
            m = xm if x < 0 else xp
            todo.append((halo_at, x + 4, 8 - rows, eprev[pl.ds(edge_at + at, rows), :] * (m * ym)))
            todo.append((halo_at, x + 4, 0, enext[pl.ds(edge_at + at, rows), :] * (m * yp)))
        for offsets, x, at, value in todo:
            for offset in offsets:
                dst[pl.ds(base + x * size + offset + at, value.shape[0]), :] = value

    def faces(start):
        return (held, start), (held, FACE_ROWS + start)

    def fill_rhs(i, carry):
        for u in range(FILLS):
            r = i * FILLS + u
            xs = (kept, r * 32), (kept, FACE_ROWS + r * 32)
            fill(ea, r * WIDE, True, (fields, r * 64), xs, 4, faces(r * 32), 4, EDGES4, r * 12)
        values = [fields[pl.ds((i * FILLS + u) * 64 + x * 8, 8), :] for u in range(FILLS) for x in range(8)]
        for u in range(FILLS):
            for x in range(8):
                basis[pl.ds(x * 8 * COLS + i * FILLS + u, 8, stride=COLS), :] = values[u * 8 + x]
        return carry

    lax.fori_loop(0, RHS // FILLS, fill_rhs, 0)
    for i in range(4):
        start = face_at(RHS + i, 0)[0]
        own, xs = (fields, (RHS + i) * 64), ((kept, start), (kept, FACE_ROWS + start))
        fill(ec, i * NARROW, False, own, xs, 3, faces(start), 3, EDGES3, COEF_AT + i * 6)
        at, count = REACH[i]
        own, xs = (slabs, i * 64), ((sprev, at), (snext, at))
        ys = (eprev, FACE_AT[i]), (enext, FACE_AT[i])
        fill(es, i * NARROW, False, own, xs, count, ys, count, ENDS_AT[i][1], ENDS_AT[i][0])

    for x in range(16):
        for tile in range(2):
            at = x * 16 + tile * 8
            outer, inner = es[at : at + 8, :] * beyond_ends, es[2 * NARROW + at : 2 * NARROW + at + 8, :]
            pair = (jnp.where(lane8 < 4, outer, inner), jnp.where(lane8 < 4, inner, outer))
            for base, value in zip((LOW, HIGH), pair):
                for offset in ((8, 24), (16, 0))[tile]:
                    ea[base + x * 32 + offset : base + x * 32 + offset + 8, :] = value

    def weights(a, vs, ok):
        sixth = ok * F32(1 / 6)
        out = [(a - 1.0) * sixth]
        for v in vs:
            out += [(0.5 * v - 1.0) * sixth, (-0.5 * v - 1.0) * sixth]
        return out

    def make(i, carry):
        done = []
        for u in range(MAKES):
            x = 1 + i * MAKES + u
            okx = jnp.where(x < 4, xm, jnp.where(x >= 12, xp, F32(1)))
            for tile in range(2):
                at = x * 16 + tile * 8
                ok = okx * (jnp.where(row < 4, yp, ym) if tile else jnp.ones((8, 128), F32))
                cs = [ec[pl.ds(i * NARROW + at, 8), :] for i in range(4)]
                done.append((main, at, weights(cs[0], cs[1:], ok)))
                outer, inner = es[pl.ds(NARROW + at, 8), :], es[pl.ds(3 * NARROW + at, 8), :]
                for k, (pick, okz) in enumerate(((lane8 < 4, zm), (lane8 >= 4, zp))):
                    narrow = jnp.where(pick, outer, inner)
                    cs = [jnp.take_along_axis(narrow, lane8 + 8 * i, axis=1) for i in range(4)]
                    values = weights(cs[0], cs[1:], ok * jnp.where(pick, okz, F32(1)))
                    done.append((side, k * 7 * NARROW + at, values))
        for dst, at, values in done:
            for i in range(7):
                dst[pl.ds(i * NARROW + at, 8), :] = values[i]
        return carry

    lax.fori_loop(0, 14 // MAKES, make, 0)

    for s in range(1, STEPS + 1):
        src, dst = (ea, eb) if s % 2 else (eb, ea)
        last = s == STEPS

        tiles = [(x, 0) for x in range(s, 16 - s)]
        if not last:
            tiles += [(x, 1) for x in range(s + 1, 15 - s)]
        for x, tile in tiles:
            at = x * 32 + 8 + tile * 8
            both = jnp.where(lane8 == 4, src[HIGH + at : HIGH + at + 8, :], src[LOW + at : LOW + at + 8, :])
            for r in range(RHS):
                to = r * NARROW + x * 16 + tile * 8
                turn[to : to + 8, :] = rolled(both, -(8 * r + 4))

        def step(x, tile, keep, s=s, src=src, dst=dst, last=last):
            at = x * 32 + 8 + tile * 8
            small = x * 16 + tile * 8

            def apply(c, base, v, zplus, zminus):
                out = c[0] * v
                out = out + c[1] * src[pl.ds(base + at + 32, 8), :]
                out = out + c[2] * src[pl.ds(base + at - 32, 8), :]
                out = out + c[3] * src[pl.ds(base + at + 1, 8), :]
                out = out + c[4] * src[pl.ds(base + at - 1, 8), :]
                out = out + c[5] * zplus
                return out + c[6] * zminus

            def put(base, out):
                for offset in ((8, 24), (16, 0))[tile]:
                    dst[pl.ds(base + x * 32 + offset, 8), :] = out

            cs = [main[pl.ds(i * NARROW + small, 8), :] for i in range(7)]
            for r in range(RHS):
                v = src[pl.ds(r * WIDE + at, 8), :]
                over = turn[pl.ds(r * NARROW + small, 8), :]
                zplus = rolled(jnp.where(lane == 0, over, v), -1)
                zminus = rolled(jnp.where(lane == 127, over, v), 1)
                out = apply(cs, r * WIDE, v, zplus, zminus)
                if keep:
                    basis[pl.ds((x - 4) * 8 * COLS + s * RHS + r, 8, stride=COLS), :] = out
                if not last:
                    put(r * WIDE, out)
            if not last:
                for k, base in enumerate((LOW, HIGH)):
                    cs = [side[pl.ds((k * 7 + i) * NARROW + small, 8), :] for i in range(7)]
                    v = src[pl.ds(base + at, 8), :]
                    put(base, apply(cs, base, v, rolled(v, -1), rolled(v, 1)))

        def inside(i, carry, step=step):
            for u in range(OWN):
                step(4 + i * OWN + u, 0, True)
            return carry

        def outside(i, carry, s=s, step=step):
            for u in range(4 - s):
                step(s + i * (12 - s) + u, 0, False)
            return carry

        def halo(i, carry, s=s, step=step):
            for u in range(7 - s):
                step(s + 1 + i * (7 - s) + u, 1, False)
            return carry

        lax.fori_loop(0, 8 // OWN, inside, 0)
        if not last:
            lax.fori_loop(0, 2, outside, 0)
            lax.fori_loop(0, 2, halo, 0)

    zeros = jnp.zeros((128 - COLS, 256), BF16)

    def product(i, acc):
        for u in range(GRAMS):
            base = pl.multiple_of((i * GRAMS + u) * 2 * COLS, 2 * COLS)
            value = jnp.concatenate([basis[pl.ds(base, COLS), :], basis[pl.ds(base + COLS, COLS), :]], axis=1)
            high = value.astype(BF16)
            low = (value - high.astype(F32)).astype(BF16)
            acc = acc + lax.dot_general(
                wide([high, low]),
                wide([high, zeros, low, zeros]),
                (((1,), (1,)), ((), ())),
                preferred_element_type=F32,
            )
        return acc

    acc = lax.fori_loop(0, 32 // GRAMS, product, jnp.zeros((2 * COLS, 256), F32))
    gram = (acc[:COLS, :128] + acc[COLS:, 128:]) + (acc[:COLS, 128:] + acc[COLS:, :128])
    part = [gram[i * RHS : (i + 1) * RHS] for i in range(STEPS + 1)]
    lane = lax.broadcasted_iota(jnp.int32, (RHS, 128), 1)
    packed[:RHS, :] = jnp.where(
        lane < 80, part[0], jnp.where(lane < 112, rolled(part[3], 32), rolled(part[4], 48))
    )
    packed[RHS:, :] = jnp.where(
        lane < 64, rolled(part[1], -16), jnp.where(lane < 112, rolled(part[2], 32), 0.0)
    )


def solved(p, right):
    (a, b), (c, d) = p[0][:2], p[1][:2]
    scale = 1.0 / (a * d - b * c)
    inverse = ((d * scale, -(b * scale)), (-(c * scale), a * scale))
    return [[i[0] * u + i[1] * v for u, v in zip(*right)] for i in inverse]


def solve_combine(parts, basis, solution_field, residual, held, sems):
    total = parts[0]
    for i in range(1, parts.shape[0]):
        total = total + parts[i]
    first, second = total[:RHS], total[RHS:]
    lane = lax.broadcasted_iota(jnp.int32, (RHS, 128), 1)

    def span(value, start):
        return jnp.where((lane >= start) & (lane < COLS), value, 0.0)

    upper = [
        span(first, 0),
        span(rolled(second, 16), 16),
        span(rolled(second, -32), 32),
        span(rolled(first, -32), 48),
        span(rolled(first, -48), 64),
    ]
    flipped = jnp.transpose(wide(upper + [jnp.zeros((128 - COLS, 128), F32)]))
    gram = wide(
        [
            jnp.where(lane < i * RHS, flipped[i * RHS : (i + 1) * RHS], upper[i])
            for i in range(STEPS + 1)
        ]
    )
    half = 7.0 * gram + 6.0 * rolled(gram, -RHS)
    half = jnp.where(lax.broadcasted_iota(jnp.int32, (COLS, 128), 1) < KEEP, half, 0.0)
    normal = 7.0 * half[:KEEP] + 6.0 * half[RHS:]
    m = [normal[i * 8 : i * 8 + 8] for i in range(8)] + [half[:8], half[8:RHS]]
    lane = lanes()

    def column(i, c):
        return jnp.broadcast_to(m[i][:, c : c + 1], (8, 128))

    def row(value, r):
        return jnp.broadcast_to(value[r : r + 1, :], (8, 128))

    def square(r, c):
        columns = [column(r // 8, c + j) for j in range(BLOCK)]
        return [[row(columns[j], r % 8 + i) for j in range(BLOCK)] for i in range(BLOCK)]

    pivots = square(0, 0)
    for k in range(0, KEEP, BLOCK):
        i0, s = divmod(k, 8)
        inside = (lane >= k) & (lane < k + BLOCK)
        keep = list(range(i0 + 1 if s + BLOCK == 8 else i0, 10))
        columns = {i: [column(i, k + c) for c in range(BLOCK)] for i in keep}
        rows = [
            jnp.where(lane == k + d, -1.0, jnp.where(inside, 0.0, row(m[i0], s + d))) for d in range(BLOCK)
        ]
        more = k + BLOCK < KEEP
        if more:
            across, after = square(k, k + BLOCK), square(k + BLOCK, k + BLOCK)
            rights = [across[d] + [rows[d]] for d in range(BLOCK)]
        else:
            rights = [[rows[d]] for d in range(BLOCK)]
        upper = solved(pivots[:2], [pivots[d][2:] + rights[d] for d in (0, 1)])
        rest = [
            [u - (pivots[e][0] * v + pivots[e][1] * w) for u, v, w in zip(pivots[e][2:] + rights[e], *upper)]
            for e in (2, 3)
        ]
        lower = solved(rest, [r[2:] for r in rest])
        upper = [
            [u - (upper[d][0] * v + upper[d][1] * w) for u, v, w in zip(upper[d][2:], *lower)] for d in (0, 1)
        ]
        result = upper + lower
        if more:
            pivots = [
                [
                    after[d][c] - (
                        (across[0][d] * result[0][c] + across[1][d] * result[1][c])
                        + (across[2][d] * result[2][c] + across[3][d] * result[3][c])
                    )
                    for c in range(BLOCK)
                ]
                for d in range(BLOCK)
            ]
        for i in keep:
            value = jnp.where(inside, 0.0, m[i])
            for c in range(BLOCK):
                value = value - columns[i][c] * result[c][-1]
            m[i] = value
    coef = wide(m[8:])
    mixed = 7.0 * coef + 6.0 * rolled(coef, RHS)
    both = wide([coef, mixed])
    high = both.astype(BF16).astype(F32)
    mid = (both - high).astype(BF16).astype(F32)
    low = both - high - mid
    lane = lax.broadcasted_iota(jnp.int32, (2 * RHS, 128), 1)

    def tripled(value, parts):
        left = value if parts == 1 else jnp.where(lane < 80, value, rolled(value, 80))
        right = jnp.where(lane < 32, rolled(value, -48), 0.0) if parts > 1 else jnp.zeros_like(value)
        if parts == 3:
            right = jnp.where((lane >= 32) & (lane < 112), rolled(value, 32), right)
        return jnp.concatenate([left, right], axis=1)

    factors = wide([tripled(high, 3), tripled(mid, 2), tripled(low, 1)[RHS:]]).astype(BF16)
    zeros = jnp.zeros((16, 256), BF16)

    def combine(i, carry):
        done = []
        for u in range(PAIRS):
            base = pl.multiple_of((i * PAIRS + u) * 2 * COLS, 2 * COLS)
            value = jnp.concatenate([basis[pl.ds(base, COLS), :], basis[pl.ds(base + COLS, COLS), :]], axis=1)
            high = value.astype(BF16)
            rest = value - high.astype(F32)
            mid = rest.astype(BF16)
            low = (rest - mid.astype(F32)).astype(BF16)
            out = jnp.dot(factors, wide([high, mid, low, zeros]), preferred_element_type=F32)
            mixed = out[RHS : 2 * RHS] + (out[3 * RHS : 4 * RHS] + out[4 * RHS :])
            done.append((out[:RHS] + out[2 * RHS : 3 * RHS], value[:RHS] - mixed))
        for u in range(PAIRS):
            for c in range(2):
                at = 2 * (i * PAIRS + u) + c
                held[pl.ds(at, RHS, stride=64), :] = done[u][0][:, c * 128 : (c + 1) * 128]
                held[pl.ds(1024 + at, RHS, stride=64), :] = done[u][1][:, c * 128 : (c + 1) * 128]
        return carry

    count = 32 // PAIRS
    copies = []
    for i in range(count):
        combine(i, 0)
        rows = pl.ds(i * 2 * PAIRS, 2 * PAIRS)
        for k, out in enumerate((solution_field, residual)):
            src = held.reshape(2, RHS, 64, 128).at[k, :, rows, :]
            copies.append(pltpu.make_async_copy(src, out.at[:, rows, :], sems.at[i * 2 + k]))
            copies[-1].start()
    for copy in copies:
        copy.wait()


def call(kernel, ins, outs, scratch=(), hbm=False):
    vmem = pl.BlockSpec(memory_space=pltpu.VMEM)
    specs = [vmem] * len(ins)
    return pl.pallas_call(
        kernel,
        out_shape=[jax.ShapeDtypeStruct(s, F32) for s in outs],
        in_specs=specs,
        out_specs=[pl.BlockSpec(memory_space=pl.ANY) if hbm else vmem] * len(outs),
        scratch_shapes=[pltpu.VMEM(s, F32) if isinstance(s, tuple) else s for s in scratch],
        compiler_params=pltpu.CompilerParams(vmem_limit_bytes=LIMIT),
    )(*ins)


def shift(value, axis, by):
    count = lax.axis_size(axis)
    return lax.ppermute(value, axis, [(i, (i + by) % count) for i in range(count)])


def gathered(value, axis):
    count = lax.axis_size(axis)
    return lax.all_to_all(jnp.broadcast_to(value[None], (count,) + value.shape), axis, 0, 0)


def shards(right_side, absorption, velocity):
    fields = jnp.concatenate([right_side, absorption[None], velocity], axis=0).reshape((RHS + 4) * 64, 128)
    face = (FACE_ROWS, 128)
    ends_z, xlow, xhigh, ylow, yhigh = call(pack_own, [fields], [(128, 128), face, face, face, face])
    xprev = shift(xhigh, "gx", 1)
    xnext = shift(xlow, "gx", -1)
    count = 2 * lax.axis_size("zx")
    mate = lax.ppermute(ends_z, ("zx", "core"), [(i, i ^ 1) for i in range(count)])
    pairs = [((2 * i + 1) % count, (2 * i + 2) % count) for i in range(count // 2)]
    other = lax.ppermute(ends_z, ("zx", "core"), pairs + [(b, a) for a, b in pairs])
    slabs, slow, shigh = call(
        pack_ends, [ends_z, mate, other], [(256, 128), (128, 128), (128, 128)]
    )
    sprev = shift(shigh, "gx", 1)
    snext = shift(slow, "gx", -1)
    yprev = shift(yhigh, "gy", 1)
    ynext = shift(ylow, "gy", -1)
    edge = (EDGE_ROWS, 128)
    elow, ehigh, kept = call(pack_edges, [slabs, xprev, xnext, sprev, snext], [edge, edge, (2 * FACE_ROWS, 128)])
    eprev = shift(ehigh, "gy", 1)
    enext = shift(elow, "gy", -1)
    (held,) = call(keep_faces, [yprev, ynext], [(2 * FACE_ROWS, 128)])
    basis, packed = call(
        steps_gram,
        [fields, slabs, kept, sprev, snext, held, eprev, enext],
        [(64 * COLS, 128), (2 * RHS, 128)],
        [(18 * WIDE, 128)] * 2 + [(n * NARROW, 128) for n in (4, 4, 7, 14, RHS)],
    )
    packed = packed + shift(packed, "core", 1)
    packed = gathered(packed, ("gx", "zx")).sum(0)
    parts = gathered(packed, "gy")
    solution_field, residual = call(
        solve_combine,
        [parts, basis],
        [(RHS, 64, 128), (RHS, 64, 128)],
        [pltpu.VMEM((2048, 128), F32), pltpu.SemaphoreType.DMA((64 // PAIRS,))],
        hbm=True,
    )
    return solution_field.reshape(right_side.shape), residual.reshape(right_side.shape)


def solution(mesh):
    nx, ny, nz = mesh.devices.shape
    split = Mesh(mesh.devices.reshape(nx, ny, nz // 2, 2), ("gx", "gy", "zx", "core"))
    z = ("zx", "core")
    return jax.shard_map(
        shards,
        mesh=split,
        in_specs=(P(None, "gx", "gy", z), P("gx", "gy", z), P(None, "gx", "gy", z)),
        out_specs=(P(None, "gx", "gy", z), P(None, "gx", "gy", z)),
        check_vma=False,
    )
```

```python
import jax
import jax.numpy as jnp
from jax import lax
from jax.experimental import pallas as pl
from jax.experimental.pallas import tpu as pltpu
from jax.sharding import Mesh, PartitionSpec as P

RHS = 16
STEPS = 4
COLS = RHS * (STEPS + 1)
KEEP = RHS * STEPS
FILLS = 4
MAKES = 7
OWN = 8
GRAMS = 32
PAIRS = 8
BLOCK = 4
LOW = RHS * 512
HIGH = LOW + 512
LIMIT = 28 * 1024 * 1024
F32 = jnp.float32
BF16 = jnp.bfloat16


def lanes():
    return lax.broadcasted_iota(jnp.int32, (8, 128), 1)


def borders():
    places = [(lax.axis_index(axis), lax.axis_size(axis)) for axis in ("gx", "gy")]
    places.append((lax.axis_index("zx") * 2 + lax.axis_index("core"), lax.axis_size("zx") * 2))
    out = []
    for at, size in places:
        out += [jnp.where(at > 0, F32(1), F32(0)), jnp.where(at < size - 1, F32(1), F32(0))]
    return out


def rolled(x, amount):
    amount = amount % x.shape[-1]
    return x if amount == 0 else pltpu.roll(x, amount, x.ndim - 1)


def wide(pieces):
    return jnp.concatenate(pieces, axis=0)


FACE_ROWS = RHS * 32 + 4 * 24


def face_at(f, side):
    count = 4 if f < RHS else 3
    start = f * 32 if f < RHS else RHS * 32 + (f - RHS) * 24
    return start, count, (0 if side == 0 else 8 - count)


def pack_own(own, ends, xlow, xhigh, ylow, yhigh):
    group = lanes() // 8
    for x in range(8):
        tiles = [own[f * 64 + x * 8 : f * 64 + x * 8 + 8, :] for f in range(RHS + 4)]
        for part, at in ((tiles[:RHS], 0), (tiles[RHS:], 64)):
            acc = rolled(part[0], 4)
            for i in range(1, len(part)):
                acc = jnp.where(group == i, rolled(part[i], 8 * i + 4), acc)
            ends[at + x * 8 : at + x * 8 + 8, :] = acc
        for f, tile in enumerate(tiles):
            for side, (xout, yout) in enumerate(((xlow, ylow), (xhigh, yhigh))):
                start, count, first = face_at(f, side)
                if first <= x < first + count:
                    xout[start + (x - first) * 8 : start + (x - first) * 8 + 8, :] = tile
                yout[start + x * count : start + x * count + count, :] = tile[first : first + count]


REACH = ((0, 3), (24, 2), (40, 2), (56, 1))


def pack_ends(ends, mate, other, slabs, xlow, xhigh):
    from_mate = (lanes() % 8 < 4) == (lax.axis_index("core") == 1)
    for j in range(4):
        for x in range(8):
            at = slice((j % 2) * 64 + x * 8, (j % 2) * 64 + x * 8 + 8)
            tile = ends[at, :] if j > 1 else jnp.where(from_mate, mate[at, :], other[at, :])
            slabs[j * 64 + x * 8 : j * 64 + x * 8 + 8, :] = tile
            start, count = REACH[j]
            for xout, first in ((xlow, 0), (xhigh, 8 - count)):
                if first <= x < first + count:
                    xout[start + (x - first) * 8 : start + (x - first) * 8 + 8, :] = tile


EDGES4 = ((-1, 3, 0), (8, 3, 3), (-2, 2, 6), (9, 2, 8), (-3, 1, 10), (10, 1, 11))
EDGES3 = ((-1, 2, 0), (8, 2, 2), (-2, 1, 4), (9, 1, 5))
EDGES2 = ((-1, 1, 0), (8, 1, 1))
COEF_AT = RHS * 12
ENDS_AT = ((COEF_AT + 24, EDGES3), (COEF_AT + 30, EDGES2), (COEF_AT + 32, EDGES2), (COEF_AT + 34, ()))
FACE_AT = (COEF_AT + 34, COEF_AT + 58, COEF_AT + 74, COEF_AT + 90)
EDGE_ROWS = 384


def pack_edges(slabs, xprev, xnext, sprev, snext, ylow, yhigh, kept):
    def put(table, to, prev, nxt, before, after):
        for x, rows, at in table:
            tile = prev[pl.ds(before + x * 8, 8), :] if x < 0 else nxt[pl.ds(after + (x - 8) * 8, 8), :]
            ylow[pl.ds(to + at, rows), :] = tile[:rows]
            yhigh[pl.ds(to + at, rows), :] = tile[8 - rows :]

    for r in range(RHS):
        put(EDGES4, r * 12, xprev, xnext, r * 32 + 32, r * 32)
    for i in range(4):
        start = face_at(RHS + i, 0)[0]
        put(EDGES3, COEF_AT + i * 6, xprev, xnext, start + 24, start)
        start, count = REACH[i]
        put(ENDS_AT[i][1], ENDS_AT[i][0], sprev, snext, start + count * 8, start)
        for x in range(8):
            tile = slabs[i * 64 + x * 8 : i * 64 + x * 8 + 8, :]
            at = FACE_AT[i] + x * count
            ylow[at : at + count, :] = tile[:count]
            yhigh[at : at + count, :] = tile[8 - count :]
    keep_faces(xprev, xnext, kept)


def keep_faces(prev, nxt, kept):
    kept[:FACE_ROWS, :] = prev[:, :]
    kept[FACE_ROWS:, :] = nxt[:, :]


WIDE = 512
NARROW = 256


def steps_gram(
    fields, slabs, kept, sprev, snext, held, eprev, enext,
    basis, packed, ea, eb, es, ec, main, side, turn,
):
    lane = lanes()
    lane8 = lane % 8
    row = lax.broadcasted_iota(jnp.int32, (8, 128), 0)
    xm, xp, ym, yp, zm, zp = borders()
    beyond_ends = jnp.where(lane8 < 4, zm, zp)

    def fill(dst, base, wide_field, own, xs, count, ys, ycount, table, edge_at):
        size = 32 if wide_field else 16
        own_at, halo_at = ((8, 24), (16, 0)) if wide_field else ((0,), (8,))
        todo = []
        for x in range(8):
            todo.append((own_at, x + 4, 0, own[0][pl.ds(own[1] + x * 8, 8), :]))
            todo.append((halo_at, x + 4, 8 - ycount, ys[0][0][pl.ds(ys[0][1] + x * ycount, ycount), :] * ym))
            todo.append((halo_at, x + 4, 0, ys[1][0][pl.ds(ys[1][1] + x * ycount, ycount), :] * yp))
        for i in range(count):
            (low, low_at), (high, high_at) = xs
            todo.append((own_at, 4 - count + i, 0, low[pl.ds(low_at + i * 8, 8), :] * xm))
            todo.append((own_at, 12 + i, 0, high[pl.ds(high_at + i * 8, 8), :] * xp))
        for x, rows, at in table:
            m = xm if x < 0 else xp
            todo.append((halo_at, x + 4, 8 - rows, eprev[pl.ds(edge_at + at, rows), :] * (m * ym)))
            todo.append((halo_at, x + 4, 0, enext[pl.ds(edge_at + at, rows), :] * (m * yp)))
        for offsets, x, at, value in todo:
            for offset in offsets:
                dst[pl.ds(base + x * size + offset + at, value.shape[0]), :] = value

    def faces(start):
        return (held, start), (held, FACE_ROWS + start)

    def fill_rhs(i, carry):
        for u in range(FILLS):
            r = i * FILLS + u
            xs = (kept, r * 32), (kept, FACE_ROWS + r * 32)
            fill(ea, r * WIDE, True, (fields, r * 64), xs, 4, faces(r * 32), 4, EDGES4, r * 12)
        values = [fields[pl.ds((i * FILLS + u) * 64 + x * 8, 8), :] for u in range(FILLS) for x in range(8)]
        for u in range(FILLS):
            for x in range(8):
                basis[pl.ds(x * 8 * COLS + i * FILLS + u, 8, stride=COLS), :] = values[u * 8 + x]
        return carry

    lax.fori_loop(0, RHS // FILLS, fill_rhs, 0)
    for i in range(4):
        start = face_at(RHS + i, 0)[0]
        own, xs = (fields, (RHS + i) * 64), ((kept, start), (kept, FACE_ROWS + start))
        fill(ec, i * NARROW, False, own, xs, 3, faces(start), 3, EDGES3, COEF_AT + i * 6)
        at, count = REACH[i]
        own, xs = (slabs, i * 64), ((sprev, at), (snext, at))
        ys = (eprev, FACE_AT[i]), (enext, FACE_AT[i])
        fill(es, i * NARROW, False, own, xs, count, ys, count, ENDS_AT[i][1], ENDS_AT[i][0])

    for x in range(16):
        for tile in range(2):
            at = x * 16 + tile * 8
            outer, inner = es[at : at + 8, :] * beyond_ends, es[2 * NARROW + at : 2 * NARROW + at + 8, :]
            pair = (jnp.where(lane8 < 4, outer, inner), jnp.where(lane8 < 4, inner, outer))
            for base, value in zip((LOW, HIGH), pair):
                for offset in ((8, 24), (16, 0))[tile]:
                    ea[base + x * 32 + offset : base + x * 32 + offset + 8, :] = value

    def weights(a, vs, ok):
        sixth = ok * F32(1 / 6)
        out = [(a - 1.0) * sixth]
        for v in vs:
            out += [(0.5 * v - 1.0) * sixth, (-0.5 * v - 1.0) * sixth]
        return out

    def make(i, carry):
        done = []
        for u in range(MAKES):
            x = 1 + i * MAKES + u
            okx = jnp.where(x < 4, xm, jnp.where(x >= 12, xp, F32(1)))
            for tile in range(2):
                at = x * 16 + tile * 8
                ok = okx * (jnp.where(row < 4, yp, ym) if tile else jnp.ones((8, 128), F32))
                cs = [ec[pl.ds(i * NARROW + at, 8), :] for i in range(4)]
                done.append((main, at, weights(cs[0], cs[1:], ok)))
                outer, inner = es[pl.ds(NARROW + at, 8), :], es[pl.ds(3 * NARROW + at, 8), :]
                for k, (pick, okz) in enumerate(((lane8 < 4, zm), (lane8 >= 4, zp))):
                    narrow = jnp.where(pick, outer, inner)
                    cs = [jnp.take_along_axis(narrow, lane8 + 8 * i, axis=1) for i in range(4)]
                    values = weights(cs[0], cs[1:], ok * jnp.where(pick, okz, F32(1)))
                    done.append((side, k * 7 * NARROW + at, values))
        for dst, at, values in done:
            for i in range(7):
                dst[pl.ds(i * NARROW + at, 8), :] = values[i]
        return carry

    lax.fori_loop(0, 14 // MAKES, make, 0)

    for s in range(1, STEPS + 1):
        src, dst = (ea, eb) if s % 2 else (eb, ea)
        last = s == STEPS

        tiles = [(x, 0) for x in range(s, 16 - s)]
        if not last:
            tiles += [(x, 1) for x in range(s + 1, 15 - s)]
        for x, tile in tiles:
            at = x * 32 + 8 + tile * 8
            both = jnp.where(lane8 == 4, src[HIGH + at : HIGH + at + 8, :], src[LOW + at : LOW + at + 8, :])
            for r in range(RHS):
                to = r * NARROW + x * 16 + tile * 8
                turn[to : to + 8, :] = rolled(both, -(8 * r + 4))

        def step(x, tile, keep, s=s, src=src, dst=dst, last=last):
            at = x * 32 + 8 + tile * 8
            small = x * 16 + tile * 8

            def apply(c, base, v, zplus, zminus):
                out = c[0] * v
                out = out + c[1] * src[pl.ds(base + at + 32, 8), :]
                out = out + c[2] * src[pl.ds(base + at - 32, 8), :]
                out = out + c[3] * src[pl.ds(base + at + 1, 8), :]
                out = out + c[4] * src[pl.ds(base + at - 1, 8), :]
                out = out + c[5] * zplus
                return out + c[6] * zminus

            def put(base, out):
                for offset in ((8, 24), (16, 0))[tile]:
                    dst[pl.ds(base + x * 32 + offset, 8), :] = out

            cs = [main[pl.ds(i * NARROW + small, 8), :] for i in range(7)]
            for r in range(RHS):
                v = src[pl.ds(r * WIDE + at, 8), :]
                over = turn[pl.ds(r * NARROW + small, 8), :]
                zplus = rolled(jnp.where(lane == 0, over, v), -1)
                zminus = rolled(jnp.where(lane == 127, over, v), 1)
                out = apply(cs, r * WIDE, v, zplus, zminus)
                if keep:
                    basis[pl.ds((x - 4) * 8 * COLS + s * RHS + r, 8, stride=COLS), :] = out
                if not last:
                    put(r * WIDE, out)
            if not last:
                for k, base in enumerate((LOW, HIGH)):
                    cs = [side[pl.ds((k * 7 + i) * NARROW + small, 8), :] for i in range(7)]
                    v = src[pl.ds(base + at, 8), :]
                    put(base, apply(cs, base, v, rolled(v, -1), rolled(v, 1)))

        def inside(i, carry, step=step):
            for u in range(OWN):
                step(4 + i * OWN + u, 0, True)
            return carry

        def outside(i, carry, s=s, step=step):
            for u in range(4 - s):
                step(s + i * (12 - s) + u, 0, False)
            return carry

        def halo(i, carry, s=s, step=step):
            for u in range(7 - s):
                step(s + 1 + i * (7 - s) + u, 1, False)
            return carry

        lax.fori_loop(0, 8 // OWN, inside, 0)
        if not last:
            for half in range(2):
                outside(half, 0)
                halo(half, 0)

    zeros = jnp.zeros((128 - COLS, 256), BF16)

    def product(i, acc):
        for u in range(GRAMS):
            base = pl.multiple_of((i * GRAMS + u) * 2 * COLS, 2 * COLS)
            value = jnp.concatenate([basis[pl.ds(base, COLS), :], basis[pl.ds(base + COLS, COLS), :]], axis=1)
            high = value.astype(BF16)
            low = (value - high.astype(F32)).astype(BF16)
            acc = acc + lax.dot_general(
                wide([high, low]),
                wide([high, zeros, low, zeros]),
                (((1,), (1,)), ((), ())),
                preferred_element_type=F32,
            )
        return acc

    acc = lax.fori_loop(0, 32 // GRAMS, product, jnp.zeros((2 * COLS, 256), F32))
    gram = (acc[:COLS, :128] + acc[COLS:, 128:]) + (acc[:COLS, 128:] + acc[COLS:, :128])
    part = [gram[i * RHS : (i + 1) * RHS] for i in range(STEPS + 1)]
    lane = lax.broadcasted_iota(jnp.int32, (RHS, 128), 1)
    packed[:RHS, :] = jnp.where(
        lane < 80, part[0], jnp.where(lane < 112, rolled(part[3], 32), rolled(part[4], 48))
    )
    packed[RHS:, :] = jnp.where(
        lane < 64, rolled(part[1], -16), jnp.where(lane < 112, rolled(part[2], 32), 0.0)
    )


def solved(p, right):
    (a, b), (c, d) = p[0][:2], p[1][:2]
    scale = 1.0 / (a * d - b * c)
    inverse = ((d * scale, -(b * scale)), (-(c * scale), a * scale))
    return [[i[0] * u + i[1] * v for u, v in zip(*right)] for i in inverse]


def solve_combine(parts, basis, solution_field, residual, held, sems):
    total = parts[0]
    for i in range(1, parts.shape[0]):
        total = total + parts[i]
    first, second = total[:RHS], total[RHS:]
    lane = lax.broadcasted_iota(jnp.int32, (RHS, 128), 1)

    def span(value, start):
        return jnp.where((lane >= start) & (lane < COLS), value, 0.0)

    upper = [
        span(first, 0),
        span(rolled(second, 16), 16),
        span(rolled(second, -32), 32),
        span(rolled(first, -32), 48),
        span(rolled(first, -48), 64),
    ]
    flipped = jnp.transpose(wide(upper + [jnp.zeros((128 - COLS, 128), F32)]))
    gram = wide(
        [
            jnp.where(lane < i * RHS, flipped[i * RHS : (i + 1) * RHS], upper[i])
            for i in range(STEPS + 1)
        ]
    )
    half = 7.0 * gram + 6.0 * rolled(gram, -RHS)
    half = jnp.where(lax.broadcasted_iota(jnp.int32, (COLS, 128), 1) < KEEP, half, 0.0)
    normal = 7.0 * half[:KEEP] + 6.0 * half[RHS:]
    m = [normal[i * 8 : i * 8 + 8] for i in range(8)] + [half[:8], half[8:RHS]]
    lane = lanes()

    def column(i, c):
        return jnp.broadcast_to(m[i][:, c : c + 1], (8, 128))

    def row(value, r):
        return jnp.broadcast_to(value[r : r + 1, :], (8, 128))

    def square(r, c):
        columns = [column(r // 8, c + j) for j in range(BLOCK)]
        return [[row(columns[j], r % 8 + i) for j in range(BLOCK)] for i in range(BLOCK)]

    pivots = square(0, 0)
    for k in range(0, KEEP, BLOCK):
        i0, s = divmod(k, 8)
        inside = (lane >= k) & (lane < k + BLOCK)
        keep = list(range(i0 + 1 if s + BLOCK == 8 else i0, 10))
        columns = {i: [column(i, k + c) for c in range(BLOCK)] for i in keep}
        rows = [
            jnp.where(lane == k + d, -1.0, jnp.where(inside, 0.0, row(m[i0], s + d))) for d in range(BLOCK)
        ]
        more = k + BLOCK < KEEP
        if more:
            across, after = square(k, k + BLOCK), square(k + BLOCK, k + BLOCK)
            rights = [across[d] + [rows[d]] for d in range(BLOCK)]
        else:
            rights = [[rows[d]] for d in range(BLOCK)]
        upper = solved(pivots[:2], [pivots[d][2:] + rights[d] for d in (0, 1)])
        rest = [
            [u - (pivots[e][0] * v + pivots[e][1] * w) for u, v, w in zip(pivots[e][2:] + rights[e], *upper)]
            for e in (2, 3)
        ]
        lower = solved(rest, [r[2:] for r in rest])
        upper = [
            [u - (upper[d][0] * v + upper[d][1] * w) for u, v, w in zip(upper[d][2:], *lower)] for d in (0, 1)
        ]
        result = upper + lower
        if more:
            pivots = [
                [
                    after[d][c] - (
                        (across[0][d] * result[0][c] + across[1][d] * result[1][c])
                        + (across[2][d] * result[2][c] + across[3][d] * result[3][c])
                    )
                    for c in range(BLOCK)
                ]
                for d in range(BLOCK)
            ]
        for i in keep:
            value = jnp.where(inside, 0.0, m[i])
            for c in range(BLOCK):
                value = value - columns[i][c] * result[c][-1]
            m[i] = value
    coef = wide(m[8:])
    mixed = 7.0 * coef + 6.0 * rolled(coef, RHS)
    both = wide([coef, mixed])
    high = both.astype(BF16).astype(F32)
    mid = (both - high).astype(BF16).astype(F32)
    low = both - high - mid
    lane = lax.broadcasted_iota(jnp.int32, (2 * RHS, 128), 1)

    def tripled(value, parts):
        left = value if parts == 1 else jnp.where(lane < 80, value, rolled(value, 80))
        right = jnp.where(lane < 32, rolled(value, -48), 0.0) if parts > 1 else jnp.zeros_like(value)
        if parts == 3:
            right = jnp.where((lane >= 32) & (lane < 112), rolled(value, 32), right)
        return jnp.concatenate([left, right], axis=1)

    factors = wide([tripled(high, 3), tripled(mid, 2), tripled(low, 1)[RHS:]]).astype(BF16)
    zeros = jnp.zeros((16, 256), BF16)

    def combine(i, carry):
        done = []
        for u in range(PAIRS):
            base = pl.multiple_of((i * PAIRS + u) * 2 * COLS, 2 * COLS)
            value = jnp.concatenate([basis[pl.ds(base, COLS), :], basis[pl.ds(base + COLS, COLS), :]], axis=1)
            high = value.astype(BF16)
            rest = value - high.astype(F32)
            mid = rest.astype(BF16)
            low = (rest - mid.astype(F32)).astype(BF16)
            out = jnp.dot(factors, wide([high, mid, low, zeros]), preferred_element_type=F32)
            mixed = out[RHS : 2 * RHS] + (out[3 * RHS : 4 * RHS] + out[4 * RHS :])
            done.append((out[:RHS] + out[2 * RHS : 3 * RHS], value[:RHS] - mixed))
        for u in range(PAIRS):
            for c in range(2):
                at = 2 * (i * PAIRS + u) + c
                held[pl.ds(at, RHS, stride=64), :] = done[u][0][:, c * 128 : (c + 1) * 128]
                held[pl.ds(1024 + at, RHS, stride=64), :] = done[u][1][:, c * 128 : (c + 1) * 128]
        return carry

    count = 32 // PAIRS
    copies = []
    for i in range(count):
        combine(i, 0)
        rows = pl.ds(i * 2 * PAIRS, 2 * PAIRS)
        for k, out in enumerate((solution_field, residual)):
            src = held.reshape(2, RHS, 64, 128).at[k, :, rows, :]
            copies.append(pltpu.make_async_copy(src, out.at[:, rows, :], sems.at[i * 2 + k]))
            copies[-1].start()
    for copy in copies:
        copy.wait()


def call(kernel, ins, outs, scratch=(), hbm=False):
    vmem = pl.BlockSpec(memory_space=pltpu.VMEM)
    specs = [vmem] * len(ins)
    return pl.pallas_call(
        kernel,
        out_shape=[jax.ShapeDtypeStruct(s, F32) for s in outs],
        in_specs=specs,
        out_specs=[pl.BlockSpec(memory_space=pl.ANY) if hbm else vmem] * len(outs),
        scratch_shapes=[pltpu.VMEM(s, F32) if isinstance(s, tuple) else s for s in scratch],
        compiler_params=pltpu.CompilerParams(vmem_limit_bytes=LIMIT),
    )(*ins)


def shift(value, axis, by):
    count = lax.axis_size(axis)
    return lax.ppermute(value, axis, [(i, (i + by) % count) for i in range(count)])


def gathered(value, axis):
    count = lax.axis_size(axis)
    return lax.all_to_all(jnp.broadcast_to(value[None], (count,) + value.shape), axis, 0, 0)


def shards(right_side, absorption, velocity):
    fields = jnp.concatenate([right_side, absorption[None], velocity], axis=0).reshape((RHS + 4) * 64, 128)
    face = (FACE_ROWS, 128)
    ends_z, xlow, xhigh, ylow, yhigh = call(pack_own, [fields], [(128, 128), face, face, face, face])
    xprev = shift(xhigh, "gx", 1)
    xnext = shift(xlow, "gx", -1)
    count = 2 * lax.axis_size("zx")
    mate = lax.ppermute(ends_z, ("zx", "core"), [(i, i ^ 1) for i in range(count)])
    pairs = [((2 * i + 1) % count, (2 * i + 2) % count) for i in range(count // 2)]
    other = lax.ppermute(ends_z, ("zx", "core"), pairs + [(b, a) for a, b in pairs])
    slabs, slow, shigh = call(
        pack_ends, [ends_z, mate, other], [(256, 128), (128, 128), (128, 128)]
    )
    sprev = shift(shigh, "gx", 1)
    snext = shift(slow, "gx", -1)
    yprev = shift(yhigh, "gy", 1)
    ynext = shift(ylow, "gy", -1)
    edge = (EDGE_ROWS, 128)
    elow, ehigh, kept = call(pack_edges, [slabs, xprev, xnext, sprev, snext], [edge, edge, (2 * FACE_ROWS, 128)])
    eprev = shift(ehigh, "gy", 1)
    enext = shift(elow, "gy", -1)
    (held,) = call(keep_faces, [yprev, ynext], [(2 * FACE_ROWS, 128)])
    basis, packed = call(
        steps_gram,
        [fields, slabs, kept, sprev, snext, held, eprev, enext],
        [(64 * COLS, 128), (2 * RHS, 128)],
        [(18 * WIDE, 128)] * 2 + [(n * NARROW, 128) for n in (4, 4, 7, 14, RHS)],
    )
    packed = packed + shift(packed, "core", 1)
    packed = gathered(packed, ("gx", "zx")).sum(0)
    parts = gathered(packed, "gy")
    solution_field, residual = call(
        solve_combine,
        [parts, basis],
        [(RHS, 64, 128), (RHS, 64, 128)],
        [pltpu.VMEM((2048, 128), F32), pltpu.SemaphoreType.DMA((64 // PAIRS,))],
        hbm=True,
    )
    return solution_field.reshape(right_side.shape), residual.reshape(right_side.shape)


def solution(mesh):
    nx, ny, nz = mesh.devices.shape
    split = Mesh(mesh.devices.reshape(nx, ny, nz // 2, 2), ("gx", "gy", "zx", "core"))
    z = ("zx", "core")
    return jax.shard_map(
        shards,
        mesh=split,
        in_specs=(P(None, "gx", "gy", z), P("gx", "gy", z), P(None, "gx", "gy", z)),
        out_specs=(P(None, "gx", "gy", z), P(None, "gx", "gy", z)),
        check_vma=False,
    )
```
